128 devices in a mesh: rep: 8 (over z_lo, x), shard: 16 (over z_hi, y, core).
Axes of the slice: x: 4, y: 4, z: 4 (z_hi: 2, z_lo: 2; z = z_hi * 2 + z_lo), core: 2. Of those that a mesh axis runs over, the one named last changes fastest.
Arguments:
- inputs: bfloat16 [16, 1024, 512], P('rep', 'shard'), may hold values from -6 to 6
- qkv_weight: bfloat16 [2, 512, 1536], P(None, 'shard'), as said below
- proj_weight: bfloat16 [2, 512, 512], P(None, 'shard'), as said below
- up_weight: bfloat16 [2, 512, 2048], P(None, 'shard'), may hold values from -0.25 to 0.25
- down_weight: bfloat16 [2, 2048, 512], P(None, 'shard'), may hold values from -0.125 to 0.125
- bias_rows: bfloat16 [2, 3, 512], P(None, None, 'shard'), may hold values from -2 to 2
- norm_gain: bfloat16 [2, 2, 512], P(None, None, 'shard'), may hold values from 0.5 to 1.5
- norm_shift: bfloat16 [2, 2, 512], P(None, None, 'shard'), may hold values from -2 to 2
- up_bias: bfloat16 [2, 2048], P(None, 'shard'), may hold values from -2 to 2
- cotangent: bfloat16 [16, 1024, 512], P('rep', 'shard'), may hold values from -6 to 6
Outputs:
- outputs: bfloat16 [16, 1024, 512], P('rep', 'shard')
- input_grad: float32 [16, 1024, 512], P('rep', 'shard')
- qkv_grad: float32 [2, 512, 1536], P(None, 'shard')
- proj_grad: float32 [2, 512, 512], P(None, 'shard')
- up_grad: float32 [2, 512, 2048], P(None, 'shard')
- down_grad: float32 [2, 2048, 512], P(None, 'shard')
- bias_grad: float32 [2, 3, 512], P(None, None, 'shard')
- gain_grad: float32 [2, 2, 512], P(None, None, 'shard')
- shift_grad: float32 [2, 2, 512], P(None, None, 'shard')
- up_bias_grad: float32 [2, 2048], P(None, 'shard')
The draws below stay inside these ranges and needn't reach their ends.
Inputs may be any that keep to these rules, and one draw needn't show every extreme that they name: `qkv_weight`: entries of a normal law of deviation 512^-0.5, clipped at four deviations. `proj_weight`: entries of a normal law of deviation max(2, 1)^-0.5, clipped at four deviations.
All inputs are finite; a program needn't handle non-finite values.
Results may differ from the reference program's by a relative error of at most 0.022.
Values may be sent and summed in bfloat16 or wider, within the bound.
A program may use at most 128 MiB of HBM per device.

```python
import jax
import jax.numpy as jnp
from jax import lax

D = 512
H = 8
HD = 64
FF = 2048
LAYERS = 2
LENGTH = 1024
NSEQ = 16


def clipped_normal(key, shape, deviation, limit):
    values = jax.random.normal(key, shape, jnp.float32)
    return jnp.clip(values, -limit, limit) * deviation


def draw_inputs(key, part):
    key = jax.random.fold_in(key, 11)
    return clipped_normal(key, (NSEQ, LENGTH, D), 1.0, 6.0).astype(jnp.bfloat16)


def draw_qkv_weight(key, part):
    key = jax.random.fold_in(key, 23)
    return clipped_normal(key, (LAYERS, D, 3 * D), D ** (-0.5), 4.0).astype(jnp.bfloat16)


def draw_proj_weight(key, part):
    key = jax.random.fold_in(key, 37)
    return clipped_normal(key, (LAYERS, D, D), max(D // 256, 1) ** (-0.5), 4.0).astype(jnp.bfloat16)


def draw_bias_rows(key, part):
    key = jax.random.fold_in(key, 41)
    row_scale = jnp.array([0.03, 0.3, 0.3], jnp.float32)
    values = clipped_normal(key, (LAYERS, 3, D), 1.0, 6.0)
    return (values * row_scale[None, :, None]).astype(jnp.bfloat16)


def levels(own_key, dims, cuts, smallest, largest):
    level = 1.0
    for dim, parts in cuts:
        draws = jax.random.uniform(jax.random.fold_in(jax.random.fold_in(own_key, 6), dim), (parts,), jnp.float32, smallest / len(cuts), largest / len(cuts))
        level = level * jnp.repeat(jnp.exp(draws), dims[dim] // parts).reshape((-1,) + (1,) * (len(dims) - 1 - dim))
    return level


def normal_values(own_key, extent, scale, most, shards=(), held_as=jnp.bfloat16):
    drawn = jax.random.normal(own_key, extent, jnp.float32) * scale
    if len(shards) > 0:
        drawn = levels(own_key, extent, shards, -0.22, 0.18) * drawn
    return jnp.clip(drawn, min=-most, max=most).astype(held_as)


def setup_inputs(seed: int = 0) -> dict:
    keys = jax.random.split(jax.random.key(seed), 11)
    return {
        "inputs": draw_inputs(jax.random.fold_in(keys[10], 71), 0),
        "qkv_weight": draw_qkv_weight(jax.random.fold_in(keys[10], 71), 0),
        "proj_weight": draw_proj_weight(jax.random.fold_in(keys[10], 71), 0),
        "up_weight": normal_values(keys[3], (LAYERS, D, FF), D ** -0.5, 0.25, ((1, 16),)),
        "down_weight": normal_values(keys[4], (LAYERS, FF, D), FF ** -0.5, 0.125, ((1, 16),)),
        "bias_rows": draw_bias_rows(jax.random.fold_in(keys[10], 71), 0),
        "norm_gain": jnp.clip(1.0 + 0.1 * jax.random.normal(keys[6], (LAYERS, 2, D), jnp.float32), 0.5, 1.5).astype(jnp.bfloat16),
        "norm_shift": normal_values(keys[7], (LAYERS, 2, D), 0.3, 2.0, ((2, 16),)),
        "up_bias": normal_values(keys[8], (LAYERS, FF), 0.3, 2.0, ((1, 16),)),
        "cotangent": normal_values(keys[9], (NSEQ, LENGTH, D), 1.0, 6.0, ((0, 8), (1, 16))),
    }


@jax.custom_vjp
def low(v):
    return lax.optimization_barrier(v.astype(jnp.bfloat16)).astype(jnp.float32)

@jax.custom_vjp
def low_back(v):
    return v

def low_keep(v):
    return (low(v), None)

def low_pass(kept, grad):
    return (grad,)

def back_keep(v):
    return (v, None)

def back_low(kept, grad):
    return (low(grad),)
low.defvjp(low_keep, low_pass)
low_back.defvjp(back_keep, back_low)
highest = lax.Precision.HIGHEST

def layer_norm(values, gain, shift):
    center = values - lax.optimization_barrier(jnp.mean(values, axis=-1, keepdims=True))
    spread = lax.optimization_barrier(jnp.mean(center * center, axis=-1, keepdims=True))
    return center * lax.rsqrt(spread + 1e-06) * gain + shift

def seq_layer(hidden, weights):
    qkv_w, proj_w, up_w, down_w, biases, gains, shifts, up_b = weights
    length = hidden.shape[0]
    source = low(hidden)
    bias_all = jnp.concatenate([jnp.zeros_like(biases[0]), jnp.zeros_like(biases[0]), biases[0]])
    joined = low(low_back(jnp.dot(source, qkv_w, precision=highest) + bias_all))
    queries = joined[:, :D].reshape(length, H, HD)
    keys_all = joined[:, D:2 * D].reshape(length, H, HD)
    values_all = joined[:, 2 * D:].reshape(length, H, HD)
    scores = low_back(jnp.einsum('qhd,khd->hqk', queries, keys_all, precision=highest) * HD ** (-0.5))
    probs = low(jax.nn.softmax(scores, axis=-1))
    context = jnp.einsum('hqk,khd->qhd', probs, values_all, precision=highest).reshape(length, D)
    context = low(low_back(context))
    branch = low_back(jnp.dot(context, proj_w, precision=highest) + biases[1])
    middle = layer_norm(hidden + branch, gains[0], shifts[0])
    upper = low_back(jnp.dot(low(middle), up_w, precision=highest) + up_b)
    active = low(jax.nn.gelu(upper, approximate=False))
    branch_two = low_back(jnp.dot(active, down_w, precision=highest) + biases[2])
    return layer_norm(middle + branch_two, gains[1], shifts[1])

def reference(inputs, qkv_weight, proj_weight, up_weight, down_weight, bias_rows, norm_gain, norm_shift, up_bias, cotangent):
    params = tuple((member.astype(jnp.float32) for member in (qkv_weight, proj_weight, up_weight, down_weight, bias_rows, norm_gain, norm_shift, up_bias)))

    def forward(hidden_all, weights):

        def one_seq(hidden):
            for layer_at in range(LAYERS):
                hidden = seq_layer(hidden, tuple((member[layer_at] for member in weights)))
            return hidden
        return lax.map(jax.checkpoint(one_seq), hidden_all)
    outputs, pullback = jax.vjp(forward, inputs.astype(jnp.float32), params)
    input_grad, grads = pullback(cotangent.astype(jnp.float32))
    return (outputs.astype(jnp.bfloat16), input_grad, grads[0], grads[1], grads[2], grads[3], grads[4], grads[5], grads[6], grads[7])
```

```python
import functools

import jax
import jax.numpy as jnp
from jax import lax
from jax.experimental import pallas as pl
from jax.experimental.pallas import tpu as pltpu
from jax.sharding import PartitionSpec as P

MESH = pl.DeviceIdType.MESH
F32 = jnp.float32
BF16 = jnp.bfloat16
H, HD, D, FF, LAYERS = 8, 64, 512, 2048, 2
ZH, Y, CORES = 2, 4, 2
GROUP = ZH * Y * CORES
ROWS = 64
TOK = 2 * ROWS
LENGTH = GROUP * ROWS
QB = 256
NQ = LENGTH // QB
QKV, PROJ, UP, DOWN = range(4)
SHARD = ((32, 3 * D), (32, D), (32, FF), (128, D))


def nn(a, b):
    return jnp.dot(a, b, preferred_element_type=F32)


def nt(a, b):
    return lax.dot_general(a, b, (((1,), (1,)), ((), ())), preferred_element_type=F32)


def tn(a, b):
    return lax.dot_general(a, b, (((0,), (0,)), ((), ())), preferred_element_type=F32)


def norm_forward(values, gain, shift):
    center = values - jnp.mean(values, axis=-1, keepdims=True)
    spread = jnp.mean(center * center, axis=-1, keepdims=True)
    scale = lax.rsqrt(spread + 1e-06)
    unit = center * scale
    return unit * gain + shift, unit, scale


def norm_backward(grad, unit, scale, gain):
    d_unit = grad * gain
    first = jnp.mean(d_unit, axis=-1, keepdims=True)
    second = jnp.mean(d_unit * unit, axis=-1, keepdims=True)
    d_gain = jnp.sum(grad * unit, axis=0, keepdims=True)
    d_shift = jnp.sum(grad, axis=0, keepdims=True)
    return scale * (d_unit - first - unit * second), d_gain, d_shift


def column_sum(values):
    return jnp.sum(values, axis=0, keepdims=True)


def wait_bytes(ref, sem):
    pltpu.make_async_copy(ref, ref, sem).wait()


class Place:
    def __init__(self, nx, nzl):
        self.nx, self.nzl, self.nz = nx, nzl, ZH * nzl
        rep, shard = lax.axis_index("rep"), lax.axis_index("shard")
        self.rep, self.shard = rep, shard
        self.zl, self.x = lax.div(rep, nx), lax.rem(rep, nx)
        self.zh, self.y = lax.div(shard, Y * CORES), lax.rem(lax.div(shard, CORES), Y)
        self.core = lax.rem(shard, CORES)
        self.z = self.zh * nzl + self.zl

    def at(self, x=None, y=None, z=None, core=None):
        x = self.x if x is None else x
        y = self.y if y is None else y
        z = self.z if z is None else z
        core = self.core if core is None else core
        zh, zl = lax.div(z, self.nzl), lax.rem(z, self.nzl)
        return (zl * self.nx + x, zh * (Y * CORES) + y * CORES + core)

    def xs(self, d):
        return lax.rem(self.x + d, self.nx)

    def ys(self, d):
        return lax.rem(self.y + d, Y)

    def zs(self, d):
        return lax.rem(self.z + d, self.nz)

    def peers(self):
        found = []
        for dy in range(Y):
            for dz in range(self.nz):
                if dy or dz:
                    found.append(self.at(y=self.ys(dy), z=self.zs(dz)))
        for dx in range(1, self.nx):
            for dz in range(self.nz):
                found.append(self.at(x=self.xs(dx), z=self.zs(dz)))
        for dy in range(Y):
            for zh in range(ZH):
                z = lax.rem(self.z + zh * self.nzl, self.nz)
                found.append(self.at(y=self.ys(dy), z=z, core=1 - self.core))
        return found


def remote(src, dst, send_sem, recv_sem, device):
    pltpu.make_async_remote_copy(
        src_ref=src, dst_ref=dst, send_sem=send_sem, recv_sem=recv_sem, device_id=device, device_id_type=MESH
    ).start()


class Exchange:
    def __init__(self, place, out, into, sems):
        self.place, self.out, self.into, self.sems = place, out, into, sems

    def start(self):
        me = self.place.shard
        for d in range(1, GROUP):
            to = lax.rem(me + d, GROUP)
            remote(self.out.at[to], self.into.at[me], self.sems.at[0], self.sems.at[1], (self.place.rep, to))
        self.into[me] = self.out[me]

    def wait(self):
        wait_bytes(self.into.at[pl.ds(0, GROUP - 1)], self.sems.at[1])

    def finish(self):
        wait_bytes(self.out.at[pl.ds(0, GROUP - 1)], self.sems.at[0])


class Weight:
    def __init__(self, place, own, full, sems, sums, axis, result):
        self.place, self.own, self.full, self.sems = place, own, full, sems
        self.pair, self.chip, self.recv1, self.sum1, self.recv2, self.recv3 = sums
        self.axis, self.result = axis, result
        self.rows, self.cols = own.shape

    def sem(self, i):
        return self.sems.at[i]

    def g0(self):
        p, full = self.place, self.full
        slot = full.at[p.zh, p.y, p.core]
        slot[...] = self.own[...]
        for d in (1, 3, 2):
            remote(self.own, slot, self.sem(0), self.sem(4), p.at(y=p.ys(d)))
        remote(self.own, slot, self.sem(0), self.sem(3), p.at(z=p.nz - 1 - p.z))

    def g1(self):
        p, full = self.place, self.full
        slot = full.at[1 - p.zh, p.y, p.core]
        wait_bytes(full.at[0, 0, 0], self.sem(3))
        for d in (1, 3, 2):
            remote(slot, slot, self.sem(1), self.sem(5), p.at(y=p.ys(d)))

    def g2(self):
        p, full = self.place, self.full
        wait_bytes(full.at[0, pl.ds(0, 3), 0], self.sem(4))
        half = full.at[p.zh, :, p.core]
        remote(half, half, self.sem(2), self.sem(6), p.at(core=1 - p.core))

    def g3(self):
        p, full = self.place, self.full
        wait_bytes(full.at[0, pl.ds(0, 3), 0], self.sem(5))
        half = full.at[1 - p.zh, :, p.core]
        remote(half, half, self.sem(2), self.sem(6), p.at(core=1 - p.core))

    def g4(self):
        wait_bytes(self.full.at[:, :, 0], self.sem(6))

    def sent(self):
        full = self.full
        wait_bytes(full.at[0, :, 0], self.sem(0))
        wait_bytes(full.at[0, pl.ds(0, 3), 0], self.sem(1))
        wait_bytes(full.at[:, :, 0], self.sem(2))

    def value(self):
        return self.full[...].reshape(GROUP * self.rows, self.cols)

    def store(self, start, block):
        count = block.shape[0]
        per_y = CORES * self.rows
        block = block.astype(BF16)
        if count == Y * per_y:
            self.full[start // count] = block.reshape(Y, CORES, self.rows, self.cols)
        else:
            n = count // per_y
            zh, y = divmod(start // per_y, Y)
            self.full[zh, y : y + n] = block.reshape(n, CORES, self.rows, self.cols)

    def e0(self):
        p, full = self.place, self.full
        remote(full.at[:, :, 1 - p.core], self.pair, self.sem(7), self.sem(8), p.at(core=1 - p.core))

    def e1(self):
        p = self.place
        nx, nzl = p.nx, p.nzl
        half, part = self.rows // nzl, self.cols // nx
        wait_bytes(self.pair, self.sem(8))
        for zh in range(ZH):
            for y in range(Y):
                total = self.full[zh, y, p.core].astype(F32) + self.pair[zh, y].astype(F32)
                total = total.astype(BF16)
                for x in range(nx):
                    for zl in range(nzl):
                        a, b = (y, x) if self.axis == "y" else (x, y)
                        self.chip[a, b, zh * nzl + zl] = total[
                            zl * half : (zl + 1) * half, x * part : (x + 1) * part
                        ]
        na = Y if self.axis == "y" else nx
        for d in (1, 3, 2)[: na - 1] if na == 4 else range(1, na):
            if self.axis == "y":
                to, device = p.ys(d), p.at(y=p.ys(d))
            else:
                to, device = p.xs(d), p.at(x=p.xs(d))
            remote(self.chip.at[to], self.recv1.at[d - 1], self.sem(9), self.sem(10), device)

    def e2(self):
        p = self.place
        na, nb = (Y, p.nx) if self.axis == "y" else (p.nx, Y)
        a, b = (p.y, p.x) if self.axis == "y" else (p.x, p.y)
        if na > 1:
            wait_bytes(self.recv1, self.sem(10))
        for at in range(nb):
            for z in range(p.nz):
                total = self.chip[a, at, z].astype(F32)
                for d in range(na - 1):
                    total = total + self.recv1[d, at, z].astype(F32)
                self.sum1[at, z] = total.astype(BF16)
        for db in range(nb):
            for dz in range(p.nz):
                if db == 0 and dz == 0:
                    continue
                to_b, to_z = lax.rem(b + db, nb), p.zs(dz)
                device = p.at(x=to_b, z=to_z) if self.axis == "y" else p.at(y=to_b, z=to_z)
                remote(
                    self.sum1.at[to_b, to_z],
                    self.recv2.at[db * p.nz + dz - 1],
                    self.sem(11),
                    self.sem(12),
                    device,
                )

    def e3(self):
        p = self.place
        b = p.x if self.axis == "y" else p.y
        wait_bytes(self.recv2, self.sem(12))
        total = self.sum1[b, p.z].astype(F32)
        for i in range(self.recv2.shape[0]):
            total = total + self.recv2[i].astype(F32)
        slot = self.recv3.at[p.rep]
        slot[...] = total.astype(BF16)
        nrep = p.nx * p.nzl
        for d in range(1, nrep):
            remote(slot, slot, self.sem(13), self.sem(14), (lax.rem(p.rep + d, nrep), p.shard))

    def e4(self):
        p = self.place
        nx, nzl = p.nx, p.nzl
        half, part = self.rows // nzl, self.cols // nx
        if nx * nzl > 1:
            wait_bytes(self.recv3.at[pl.ds(0, nx * nzl - 1)], self.sem(14))
        for zl in range(nzl):
            for x in range(nx):
                self.result[zl * half : (zl + 1) * half, x * part : (x + 1) * part] = self.recv3[
                    zl * nx + x
                ].astype(F32)

    def reduced(self):
        p = self.place
        wait_bytes(self.pair, self.sem(7))
        if self.recv1.shape[0] and (Y if self.axis == "y" else p.nx) > 1:
            wait_bytes(self.recv1, self.sem(9))
        wait_bytes(self.recv2, self.sem(11))
        if p.nx * p.nzl > 1:
            wait_bytes(self.recv3.at[pl.ds(0, p.nx * p.nzl - 1)], self.sem(13))


def side_by_side(block):
    n = block.shape[-2] // 2
    return jnp.concatenate([block[..., :n, :], block[..., n:, :]], axis=-1)


def one_above_other(block):
    return jnp.concatenate([block[..., :HD], block[..., HD:]], axis=-2)


def split_heads(joined, slots):
    for s in range(2):
        rows = joined[s * ROWS : (s + 1) * ROWS]
        for h in range(H):
            at = h * HD
            query, key = rows[:, at : at + HD], rows[:, D + at : D + at + HD]
            slots[s * H + h, 0:ROWS] = jnp.concatenate([query, key], axis=1)
            slots[s * H + h, ROWS:96] = side_by_side(rows[:, 2 * D + at : 2 * D + at + HD])


def split_context(context, slots):
    for s in range(2):
        rows = context[s * ROWS : (s + 1) * ROWS]
        for h in range(H):
            slots[s * H + h] = side_by_side(rows[:, h * HD : (h + 1) * HD])


def join_context(slots):
    parts = []
    for s in range(2):
        heads = [one_above_other(slots[s * H + h]) for h in range(H)]
        parts.append(jnp.concatenate(heads, axis=1))
    return jnp.concatenate(parts, axis=0)


def join_heads(slots):
    parts = []
    for s in range(2):
        both = [slots[s * H + h] for h in range(H)]
        queries = [block[0:ROWS, :HD] for block in both]
        keys = [block[0:ROWS, HD:] for block in both]
        values = [one_above_other(block[ROWS:96]) for block in both]
        parts.append(jnp.concatenate(queries + keys + values, axis=1))
    return jnp.concatenate(parts, axis=0)


def head_parts(slots):
    both = slots[:, 0:ROWS, :].reshape(LENGTH, 2 * HD)
    values = one_above_other(slots[:, ROWS:96, :]).reshape(LENGTH, HD)
    queries = (both[:, :HD].astype(F32) * 0.125).astype(BF16)
    return queries, both[:, HD:], values


def kernel(nx, nzl, *refs):
    refs = list(refs)

    def take(n):
        got = refs[:n]
        del refs[:n]
        return got

    x_ref, cot_ref = take(2)
    own = take(4)
    bias_ref, gain_ref, shift_ref, upb_ref = take(4)
    out_ref, dx_ref = take(2)
    results = take(4)
    bias_out, gain_out, shift_out, upb_out = take(4)
    full = [take(4) for _ in range(LAYERS)]
    sums = [[take(6) for _ in range(4)] for _ in range(LAYERS)]
    swaps = [take(8) for _ in range(LAYERS)]
    small_own, small_all, small_grad, small_in, small_rep = take(5)
    small, small_up, d_small, d_small_up = take(4)
    saved = [take(8) for _ in range(LAYERS)]
    probs = take(LAYERS)
    query_ref, dc_ref, ctx_ref, dq_ref, dk_ref, dv_ref = take(6)
    weight_sems, swap_sems, small_sems = take(3)

    p = Place(nx, nzl)
    weights = [
        [
            Weight(
                p,
                own[w].at[l],
                full[l][w],
                weight_sems.at[l * 4 + w],
                sums[l][w],
                "y",
                results[w].at[l],
            )
            for w in range(4)
        ]
        for l in range(LAYERS)
    ]
    swap = [
        [Exchange(p, swaps[l][2 * i], swaps[l][2 * i + 1], swap_sems.at[l * 4 + i]) for i in range(4)]
        for l in range(LAYERS)
    ]

    barrier = pltpu.get_barrier_semaphore()
    peers = p.peers()
    for peer in peers:
        pl.semaphore_signal(barrier, inc=1, device_id=peer, device_id_type=MESH)
    small_own[...] = jnp.zeros_like(small_own)
    for l in range(LAYERS):
        at = l * 8
        small_own[at : at + 1, :] = upb_ref[l : l + 1, :].astype(F32)
        small_own[at + 1 : at + 4, 0:32] = bias_ref[l].astype(F32)
        small_own[at + 4 : at + 6, 0:32] = gain_ref[l].astype(F32)
        small_own[at + 6 : at + 8, 0:32] = shift_ref[l].astype(F32)
    pl.semaphore_wait(barrier, len(peers))

    me = p.shard
    order = [weights[l][w] for l in range(LAYERS) for w in range(4)]
    order[0].g0()
    for d in range(1, GROUP):
        to = lax.rem(me + d, GROUP)
        remote(small_own, small_all.at[me], small_sems.at[0], small_sems.at[1], (p.rep, to))
    small_all[me] = small_own[...]
    for weight in order[1:]:
        weight.g0()
    order[0].g1()
    order[0].g2()
    order[1].g1()
    order[2].g1()
    order[3].g1()

    wait_bytes(small_all.at[pl.ds(0, GROUP - 1)], small_sems.at[1])
    for l in range(LAYERS):
        for q in range(4):
            part = [small_all[4 * q + i, l * 8 : l * 8 + 8, 0:32] for i in range(4)]
            small[l, :, q * 128 : (q + 1) * 128] = jnp.concatenate(part, axis=1)
        for t in range(GROUP):
            small_up[l, :, t * 128 : (t + 1) * 128] = small_all[t, l * 8 : l * 8 + 1, :]

    order[0].g3()

    hidden = x_ref[...].astype(F32)
    for l in range(LAYERS):
        qkv, proj, up, down = weights[l]
        to_heads, to_tokens, _, _ = swap[l]
        source_ref, unit1, scale1, unit2, scale2, mid_ref, act_ref, slope_ref = saved[l]
        source = hidden.astype(BF16)
        source_ref[...] = source
        qkv.g4()
        joined = nn(source, qkv.value())
        value_bias = small[l, 1:2, :]
        joined = jnp.concatenate([joined[:, : 2 * D], joined[:, 2 * D :] + value_bias], axis=1)
        split_heads(joined.astype(BF16), to_heads.out)
        to_heads.start()
        proj.g2()
        proj.g3()
        if l + 1 < LAYERS:
            for weight in weights[l + 1]:
                weight.g1()
        to_heads.wait()
        queries, keys, values = head_parts(to_heads.into[...])
        query_ref[...] = queries.reshape(NQ, QB, HD)
        values_t = values.T

        def attend(i, carry):
            scores = nt(keys, query_ref[i])
            expo = jnp.exp(scores - jnp.max(scores, axis=0, keepdims=True))
            prob = expo * (1.0 / jnp.sum(expo, axis=0, keepdims=True))
            probs[l][i] = prob
            ctx_ref[i] = nn(values_t, prob.astype(BF16)).T.astype(BF16)
            return carry

        lax.fori_loop(0, NQ, attend, 0)
        context = ctx_ref[...].reshape(GROUP, ROWS, HD)
        to_tokens.out[...] = side_by_side(context)
        to_tokens.start()
        up.g2()
        up.g3()
        proj.g4()
        to_tokens.wait()
        context = join_context(to_tokens.into)
        first = hidden + nn(context, proj.value()) + small[l, 2:3, :]
        middle, unit, scale = norm_forward(first, small[l, 4:5, :], small[l, 6:7, :])
        unit1[...], scale1[...] = unit, scale
        mid_low = middle.astype(BF16)
        mid_ref[...] = mid_low
        up.g4()
        for j in range(4):
            at = j * 512
            upper = nn(mid_low, up.full[:, :, :, :, at : at + 512].reshape(D, 512))
            upper = upper + small_up[l, :, at : at + 512]
            phi = 0.5 + 0.5 * lax.erf(upper * (0.5**0.5))
            act_ref[:, at : at + 512] = (upper * phi).astype(BF16)
            density = jnp.exp(-0.5 * upper * upper) * 0.3989422804014327
            slope_ref[:, at : at + 512] = phi + upper * density
        down.g2()
        down.g3()
        down.g4()
        if l + 1 < LAYERS:
            weights[l + 1][0].g2()
            weights[l + 1][0].g3()
        second = middle + nn(act_ref[...], down.value()) + small[l, 3:4, :]
        hidden, unit, scale = norm_forward(second, small[l, 5:6, :], small[l, 7:8, :])
        unit2[...], scale2[...] = unit, scale
    out_ref[...] = hidden.astype(BF16)

    grad = cot_ref[...].astype(F32)
    pending = []
    for l in reversed(range(LAYERS)):
        qkv, proj, up, down = weights[l]
        to_heads, to_tokens, d_to_heads, d_to_tokens = swap[l]
        source_ref, unit1, scale1, unit2, scale2, mid_ref, act_ref, slope_ref = saved[l]
        grad_two, d_small[l, 5:6, :], d_small[l, 7:8, :] = norm_backward(
            grad, unit2[...], scale2[...], small[l, 5:6, :]
        )
        low_two = grad_two.astype(BF16)
        d_small[l, 3:4, :] = column_sum(low_two.astype(F32))
        down.sent()
        d_uppers = []
        for j in range(4):
            at = j * 512
            d_act = nt(low_two, down.full[j // 2, (j % 2) * 2 : (j % 2) * 2 + 2].reshape(512, D))
            d_upper = (d_act * slope_ref[:, at : at + 512]).astype(BF16)
            d_small_up[l, :, at : at + 512] = column_sum(d_upper.astype(F32))
            d_uppers.append(d_upper)
        d_upper = jnp.concatenate(d_uppers, axis=1)
        for j in range(8):
            down.store(j * 256, tn(act_ref[:, j * 256 : (j + 1) * 256], low_two))
        down.e0()
        grad_mid = grad_two + nt(d_upper, up.value())
        up.sent()
        for j in range(2):
            up.store(j * 256, tn(mid_ref[:, j * 256 : (j + 1) * 256], d_upper))
        up.e0()
        grad_one, d_small[l, 4:5, :], d_small[l, 6:7, :] = norm_backward(
            grad_mid, unit1[...], scale1[...], small[l, 4:5, :]
        )
        low_one = grad_one.astype(BF16)
        d_small[l, 2:3, :] = column_sum(low_one.astype(F32))
        d_context = nt(low_one, proj.value()).astype(BF16)
        split_context(d_context, d_to_heads.out)
        d_to_heads.start()
        context = join_context(to_tokens.into)
        proj.sent()
        for j in range(2):
            proj.store(j * 256, tn(context[:, j * 256 : (j + 1) * 256], low_one))
        proj.e0()
        down.e1()
        for step in pending:
            step()
        pending = []
        d_to_heads.wait()
        queries, keys, values = head_parts(to_heads.into[...])
        query_ref[...] = queries.reshape(NQ, QB, HD)
        dc_ref[...] = one_above_other(d_to_heads.into[...]).reshape(NQ, QB, HD)
        keys_t = keys.T
        dk_ref[...] = jnp.zeros_like(dk_ref)
        dv_ref[...] = jnp.zeros_like(dv_ref)

        def attend_back(i, carry):
            d_ctx = dc_ref[i]
            d_prob = nt(values, d_ctx)
            prob = probs[l][i]
            row = jnp.sum(prob * d_prob, axis=0, keepdims=True)
            d_score = (prob * (d_prob - row)).astype(BF16)
            dv_ref[...] += nn(prob.astype(BF16), d_ctx)
            dk_ref[...] += nn(d_score, query_ref[i])
            dq_ref[i] = (nn(keys_t, d_score) * 0.125).T.astype(BF16)
            return carry

        lax.fori_loop(0, NQ, attend_back, 0)
        both = jnp.concatenate([dq_ref[...].reshape(LENGTH, HD), dk_ref[...].astype(BF16)], axis=1)
        d_to_tokens.out[:, 0:ROWS, :] = both.reshape(GROUP, ROWS, 2 * HD)
        d_to_tokens.out[:, ROWS:96, :] = side_by_side(dv_ref[...].astype(BF16).reshape(GROUP, ROWS, HD))
        d_to_tokens.start()
        up.e1()
        down.e2()
        d_to_tokens.wait()
        d_joined = join_heads(d_to_tokens.into)
        d_small[l, 1:2, :] = column_sum(d_joined[:, 2 * D :].astype(F32))
        grad = grad_one + nt(d_joined, qkv.value())
        qkv.sent()
        for j in range(2):
            qkv.store(j * 256, tn(source_ref[:, j * 256 : (j + 1) * 256], d_joined))
        qkv.e0()
        proj.e1()
        up.e2()
        down.e3()
        if l > 0:
            pending = [qkv.e1, proj.e2, up.e3, down.e4]
            rest = [qkv.e2, proj.e3, up.e4, qkv.e3, proj.e4, qkv.e4]
    dx_ref[...] = grad

    small_grad[...] = jnp.zeros_like(small_grad)
    for l in range(LAYERS):
        for t in range(GROUP):
            small_grad[t, l * 8 + 1 : l * 8 + 8, 0:32] = d_small[l, 1:8, t * 32 : (t + 1) * 32]
            small_grad[t, l * 8 : l * 8 + 1, :] = d_small_up[l, :, t * 128 : (t + 1) * 128]
    for d in range(1, GROUP):
        to = lax.rem(me + d, GROUP)
        remote(small_grad.at[to], small_in.at[me], small_sems.at[2], small_sems.at[3], (p.rep, to))
    small_in[me] = small_grad[me]

    qkv, proj, up, down = weights[0]
    for step in rest[:3]:
        step()
    qkv.e1()
    proj.e2()
    up.e3()
    wait_bytes(small_in.at[pl.ds(0, GROUP - 1)], small_sems.at[3])
    total = small_in[0]
    for t in range(1, GROUP):
        total = total + small_in[t]
    slot = small_rep.at[p.rep]
    slot[...] = total
    nrep = nx * nzl
    for d in range(1, nrep):
        remote(slot, slot, small_sems.at[4], small_sems.at[5], (lax.rem(p.rep + d, nrep), me))
    for step in rest[3:]:
        step()
    down.e4()
    qkv.e2()
    proj.e3()
    up.e4()
    qkv.e3()
    proj.e4()
    if nrep > 1:
        wait_bytes(small_rep.at[pl.ds(0, nrep - 1)], small_sems.at[5])
    total = small_rep[0]
    for t in range(1, nrep):
        total = total + small_rep[t]
    for l in range(LAYERS):
        at = l * 8
        upb_out[l : l + 1, :] = total[at : at + 1, :]
        bias_out[l] = total[at + 1 : at + 4, 0:32]
        gain_out[l] = total[at + 4 : at + 6, 0:32]
        shift_out[l] = total[at + 6 : at + 8, 0:32]
    qkv.e4()

    for weight in order:
        weight.reduced()
    for l in range(LAYERS):
        for one in swap[l]:
            one.finish()
    wait_bytes(small_all.at[pl.ds(0, GROUP - 1)], small_sems.at[0])
    wait_bytes(small_grad.at[pl.ds(0, GROUP - 1)], small_sems.at[2])
    if nrep > 1:
        wait_bytes(small_rep.at[pl.ds(0, nrep - 1)], small_sems.at[4])


def scratch(nx, nzl):
    nz, nrep = ZH * nzl, nx * nzl
    shapes = []
    for _ in range(LAYERS):
        for r, c in SHARD:
            shapes.append(pltpu.VMEM((ZH, Y, CORES, r, c), BF16))
    for _ in range(LAYERS):
        for r, c in SHARD:
            piece = (r // nzl, c // nx)
            shapes.append(pltpu.VMEM((ZH, Y, r, c), BF16))
            shapes.append(pltpu.VMEM((Y, nx, nz) + piece, BF16))
            shapes.append(pltpu.VMEM((Y - 1, nx, nz) + piece, BF16))
            shapes.append(pltpu.VMEM((nx, nz) + piece, BF16))
            shapes.append(pltpu.VMEM((nx * nz - 1,) + piece, BF16))
            shapes.append(pltpu.VMEM((nrep,) + piece, BF16))
    for _ in range(LAYERS):
        for rows in (96, 32, 32, 96):
            shapes += [pltpu.VMEM((GROUP, rows, 128), BF16)] * 2
    shapes += [pltpu.VMEM((16, 128), F32)]
    shapes += [pltpu.VMEM((GROUP, 16, 128), F32)] * 3
    shapes += [pltpu.VMEM((nrep, 16, 128), F32)]
    shapes += [pltpu.VMEM((LAYERS, 8, D), F32), pltpu.VMEM((LAYERS, 1, FF), F32)] * 2
    for _ in range(LAYERS):
        shapes += [
            pltpu.VMEM((TOK, D), BF16),
            pltpu.VMEM((TOK, D), F32),
            pltpu.VMEM((TOK, 1), F32),
            pltpu.VMEM((TOK, D), F32),
            pltpu.VMEM((TOK, 1), F32),
            pltpu.VMEM((TOK, D), BF16),
            pltpu.VMEM((TOK, FF), BF16),
            pltpu.VMEM((TOK, FF), F32),
        ]
    shapes += [pltpu.VMEM((NQ, LENGTH, QB), F32)] * LAYERS
    shapes += [pltpu.VMEM((NQ, QB, HD), BF16)] * 4
    shapes += [pltpu.VMEM((LENGTH, HD), F32)] * 2
    shapes += [
        pltpu.SemaphoreType.DMA((LAYERS * 4, 15)),
        pltpu.SemaphoreType.DMA((LAYERS * 4, 2)),
        pltpu.SemaphoreType.DMA((6,)),
    ]
    return shapes


def solution(mesh):
    nrep = mesh.shape["rep"]
    nzl = 2 if nrep >= 2 else 1
    nx = nrep // nzl

    def shards(inputs, *arguments):
        cotangent, members = arguments[-1], arguments[:-1]
        shapes = [jax.ShapeDtypeStruct((TOK, D), BF16), jax.ShapeDtypeStruct((TOK, D), F32)]
        shapes += [jax.ShapeDtypeStruct(member.shape, F32) for member in members]
        got = pl.pallas_call(
            functools.partial(kernel, nx, nzl),
            out_shape=shapes,
            in_specs=[pl.BlockSpec(memory_space=pltpu.VMEM)] * 10,
            out_specs=[pl.BlockSpec(memory_space=pltpu.VMEM)] * 10,
            scratch_shapes=scratch(nx, nzl),
            compiler_params=pltpu.CompilerParams(
                collective_id=0, has_side_effects=True, vmem_limit_bytes=63 * 1024 * 1024
            ),
            cost_estimate=pl.CostEstimate(flops=7 * 10**9, bytes_accessed=8 * 10**6, transcendentals=5 * 10**6),
        )(inputs.reshape(TOK, D), cotangent.reshape(TOK, D), *members)
        return (got[0].reshape(inputs.shape), got[1].reshape(inputs.shape), *got[2:])

    rows, columns = P(None, "shard", None), P(None, None, "shard")
    both = P("rep", "shard", None)
    weights = (rows, rows, rows, rows, columns, columns, columns, P(None, "shard"))
    return jax.shard_map(
        shards,
        mesh=mesh,
        in_specs=(both, *weights, both),
        out_specs=(both, both, *weights),
        check_vma=False,
    )
```

```python
import functools

import jax
import jax.numpy as jnp
from jax import lax
from jax.experimental import pallas as pl
from jax.experimental.pallas import tpu as pltpu
from jax.sharding import PartitionSpec as P

MESH = pl.DeviceIdType.MESH
F32 = jnp.float32
BF16 = jnp.bfloat16
H, HD, D, FF, LAYERS = 8, 64, 512, 2048, 2
ZH, Y, CORES = 2, 4, 2
GROUP = ZH * Y * CORES
ROWS = 64
TOK = 2 * ROWS
LENGTH = GROUP * ROWS
QB = 256
NQ = LENGTH // QB
QKV, PROJ, UP, DOWN = range(4)
PARTS = (
    (QKV, 0, 32, 512, "x", "x"),
    (QKV, 512, 32, 512, "z", "y"),
    (QKV, 1024, 32, 512, "y", "x"),
    (PROJ, 0, 32, 512, "x", "y"),
    (UP, 0, 32, 1024, "x", "x"),
    (UP, 1024, 32, 1024, "z", "y"),
    (DOWN, 0, 128, 256, "x", "x"),
    (DOWN, 256, 128, 256, "y", "y"),
)
SEMS = 17


def nn(a, b):
    return jnp.dot(a, b, preferred_element_type=F32)


def nt(a, b):
    return lax.dot_general(a, b, (((1,), (1,)), ((), ())), preferred_element_type=F32)


def tn(a, b):
    return lax.dot_general(a, b, (((0,), (0,)), ((), ())), preferred_element_type=F32)


def norm_forward(values, gain, shift):
    center = values - jnp.mean(values, axis=-1, keepdims=True)
    spread = jnp.mean(center * center, axis=-1, keepdims=True)
    scale = lax.rsqrt(spread + 1e-06)
    unit = center * scale
    return unit * gain + shift, unit, scale


def norm_backward(grad, unit, scale, gain):
    d_unit = grad * gain
    first = jnp.mean(d_unit, axis=-1, keepdims=True)
    second = jnp.mean(d_unit * unit, axis=-1, keepdims=True)
    d_gain = jnp.sum(grad * unit, axis=0, keepdims=True)
    d_shift = jnp.sum(grad, axis=0, keepdims=True)
    return scale * (d_unit - first - unit * second), d_gain, d_shift


def column_sum(values):
    return jnp.sum(values, axis=0, keepdims=True)


def wait_bytes(ref, sem):
    pltpu.make_async_copy(ref, ref, sem).wait()


class Place:
    def __init__(self, nx, nzl):
        self.nx, self.nzl, self.nz = nx, nzl, ZH * nzl
        rep, shard = lax.axis_index("rep"), lax.axis_index("shard")
        self.rep, self.shard = rep, shard
        self.zl, self.x = lax.div(rep, nx), lax.rem(rep, nx)
        self.zh, self.y = lax.div(shard, Y * CORES), lax.rem(lax.div(shard, CORES), Y)
        self.core = lax.rem(shard, CORES)
        self.z = self.zh * nzl + self.zl

    def at(self, x=None, y=None, z=None, core=None):
        x = self.x if x is None else x
        y = self.y if y is None else y
        z = self.z if z is None else z
        core = self.core if core is None else core
        zh, zl = lax.div(z, self.nzl), lax.rem(z, self.nzl)
        return (zl * self.nx + x, zh * (Y * CORES) + y * CORES + core)

    def xs(self, d):
        return lax.rem(self.x + d, self.nx)

    def ys(self, d):
        return lax.rem(self.y + d, Y)

    def zs(self, d):
        return lax.rem(self.z + d, self.nz)

    def group(self):
        steps = [(dy, dz, dc) for dy in (2, 1, 3, 0) for dz in (1, 0) for dc in range(CORES) if dy or dz or dc]
        steps.sort(key=lambda step: -(2 * min(step[0], 1) + 2 * step[1] + step[2]))
        found = []
        for dy, dz, dc in steps:
            z = lax.rem(self.z + dz * self.nzl, self.nz)
            found.append(self.at(y=self.ys(dy), z=z, core=lax.rem(self.core + dc, CORES))[1])
        return found

    def peers(self):
        found = []
        for dy in range(Y):
            for dz in range(self.nz):
                if dy or dz:
                    found.append(self.at(y=self.ys(dy), z=self.zs(dz)))
        for dx in range(1, self.nx):
            for dz in range(self.nz):
                found.append(self.at(x=self.xs(dx), z=self.zs(dz)))
        for dy in range(Y):
            for zh in range(ZH):
                z = lax.rem(self.z + zh * self.nzl, self.nz)
                found.append(self.at(y=self.ys(dy), z=z, core=1 - self.core))
        return found


def remote(src, dst, send_sem, recv_sem, device):
    pltpu.make_async_remote_copy(
        src_ref=src, dst_ref=dst, send_sem=send_sem, recv_sem=recv_sem, device_id=device, device_id_type=MESH
    ).start()


class Exchange:
    def __init__(self, place, out, into, sems):
        self.place, self.out, self.into, self.sems = place, out, into, sems

    def start(self):
        me = self.place.shard
        for to in self.place.group():
            remote(self.out.at[to], self.into.at[me], self.sems.at[0], self.sems.at[1], (self.place.rep, to))
        self.into[me] = self.out[me]

    def wait(self):
        wait_bytes(self.into.at[pl.ds(0, GROUP - 1)], self.sems.at[1])

    def finish(self):
        wait_bytes(self.out.at[pl.ds(0, GROUP - 1)], self.sems.at[0])


class Part:
    def __init__(self, place, own, full, sems, sums, far, near, result, out):
        self.place, self.own, self.full, self.sems = place, own, full, sems
        self.pair, self.chip, self.recv1, self.sum1, self.recv2, self.recv3 = sums
        self.far, self.near, self.result, self.out = far, near, result, out
        self.rows, self.cols = own.shape
        p = place
        self.n = {"x": p.nx, "y": Y, "z": p.nz}
        self.me = {"x": p.x, "y": p.y, "z": p.z}
        self.axes = {"x": "xyz", "y": "yxz", "z": "zxy"}[near]

    def sem(self, i):
        return self.sems.at[i]

    def sibling(self):
        return self.place.at(core=1 - self.place.core)

    def across(self):
        return self.place.nz - 1 - self.place.z

    def keep(self):
        p = self.place
        self.full[p.zh, p.y, p.core] = self.own[...]

    def quarter(self, ref, x):
        nx = self.place.nx
        if self.rows == 128:
            n = self.rows // nx
            return ref.at[..., pl.ds(pl.multiple_of(x * n, n), n), :]
        n = self.cols // nx
        return ref.at[..., pl.ds(pl.multiple_of(x * n, n), n)]

    def g0(self):
        p = self.place
        slot = self.full.at[p.zh, p.y, p.core]
        if self.far == "x":
            src, dst = self.quarter(self.own, p.x), self.quarter(slot, p.x)
            for d in (2, 1, 3, 0):
                remote(src, dst, self.sem(4), self.sem(1), p.at(y=p.ys(d), z=self.across()))
            for d in (2, 1, 3):
                remote(src, dst, self.sem(3), self.sem(0), p.at(y=p.ys(d)))
        else:
            if self.far == "y":
                remote(self.own, slot, self.sem(3), self.sem(0), p.at(z=self.across()))
            for d in (2, 1, 3):
                remote(self.own, slot, self.sem(4), self.sem(1), p.at(y=p.ys(d)))

    def g1(self):
        p, full = self.place, self.full
        if self.far == "x":
            wait_bytes(self.quarter(full.at[0, pl.ds(0, 3), 0], 0), self.sem(0))
            wait_bytes(self.quarter(full.at[0, :, 0], 0), self.sem(1))
            mine = self.quarter(full.at[:, :, p.core], p.x)
            for d in order_of(p.nx):
                remote(mine, mine, self.sem(5), self.sem(2), p.at(x=p.xs(d)))
        elif self.far == "y":
            wait_bytes(full.at[0, 0, 0], self.sem(0))
            slot = full.at[1 - p.zh, p.y, p.core]
            for d in (2, 1, 3):
                remote(slot, slot, self.sem(5), self.sem(2), p.at(y=p.ys(d)))
        else:
            wait_bytes(full.at[0, pl.ds(0, 3), 0], self.sem(1))
            half = full.at[p.zh, :, p.core]
            remote(half, half, self.sem(5), self.sem(2), p.at(z=self.across()))

    def g2(self):
        p, full = self.place, self.full
        if self.far == "x":
            if p.nx > 1:
                wait_bytes(full.at[:, pl.ds(0, p.nx - 1), 0], self.sem(2))
        elif self.far == "y":
            wait_bytes(full.at[0, pl.ds(0, 3), 0], self.sem(1))
            wait_bytes(full.at[0, pl.ds(0, 3), 0], self.sem(2))
        else:
            wait_bytes(full.at[0, :, 0], self.sem(2))
        both = full.at[:, :, p.core]
        remote(both, both, self.sem(6), self.sem(7), self.sibling())

    def g3(self):
        wait_bytes(self.full.at[:, :, 0], self.sem(7))

    def sent(self):
        full, nx = self.full, self.place.nx
        if self.far == "x":
            wait_bytes(self.quarter(full.at[0, pl.ds(0, 3), 0], 0), self.sem(3))
            wait_bytes(self.quarter(full.at[0, :, 0], 0), self.sem(4))
            if nx > 1:
                wait_bytes(full.at[:, pl.ds(0, nx - 1), 0], self.sem(5))
        elif self.far == "y":
            wait_bytes(full.at[0, 0, 0], self.sem(3))
            wait_bytes(full.at[0, pl.ds(0, 3), 0], self.sem(4))
            wait_bytes(full.at[0, pl.ds(0, 3), 0], self.sem(5))
        else:
            wait_bytes(full.at[0, pl.ds(0, 3), 0], self.sem(4))
            wait_bytes(full.at[0, :, 0], self.sem(5))
        wait_bytes(full.at[:, :, 0], self.sem(6))

    def value(self):
        return self.full[...].reshape(GROUP * self.rows, self.cols)

    def store(self, start, block):
        count = block.shape[0]
        per_y = CORES * self.rows
        block = block.astype(BF16)
        if count == ZH * Y * per_y:
            self.full[...] = block.reshape(ZH, Y, CORES, self.rows, self.cols)
        elif count == Y * per_y:
            self.full[start // count] = block.reshape(Y, CORES, self.rows, self.cols)
        else:
            n = count // per_y
            zh, y = divmod(start // per_y, Y)
            self.full[zh, y : y + n] = block.reshape(n, CORES, self.rows, self.cols)

    def piece(self, zl, x):
        p = self.place
        if self.rows == 128:
            n = self.rows // (p.nx * p.nzl)
            at = (zl * p.nx + x) * n
            return slice(at, at + n), slice(None)
        half, part = self.rows // p.nzl, self.cols // p.nx
        return slice(zl * half, (zl + 1) * half), slice(x * part, (x + 1) * part)

    def e0(self):
        p, full = self.place, self.full
        remote(full.at[:, :, 1 - p.core], self.pair, self.sem(8), self.sem(9), self.sibling())

    def e1(self):
        p = self.place
        wait_bytes(self.pair, self.sem(9))
        for zh in range(ZH):
            for y in range(Y):
                total = self.full[zh, y, p.core].astype(F32) + self.pair[zh, y].astype(F32)
                total = total.astype(BF16)
                for x in range(p.nx):
                    for zl in range(p.nzl):
                        at = {"x": x, "y": y, "z": zh * p.nzl + zl}
                        rows, cols = self.piece(zl, x)
                        self.chip[tuple(at[axis] for axis in self.axes)] = total[rows, cols]
        a = self.axes[0]
        for d in order_of(self.n[a]):
            to = lax.rem(self.me[a] + d, self.n[a])
            remote(self.chip.at[to], self.recv1.at[d - 1], self.sem(10), self.sem(11), p.at(**{a: to}))

    def e2(self):
        p = self.place
        a, b, c = self.axes
        nb, nc = self.n[b], self.n[c]
        if self.n[a] > 1:
            wait_bytes(self.recv1, self.sem(11))
        for ib in range(nb):
            total = self.chip[self.me[a], ib].astype(F32)
            for d in range(self.n[a] - 1):
                total = total + self.recv1[d, ib].astype(F32)
            self.sum1[ib] = total.astype(BF16)
        pairs = [(db, dc) for db in range(nb) for dc in range(nc) if db or dc]
        for db, dc in sorted(pairs, key=lambda at: -(min(at[0], 1) + min(at[1], 1))):
            to_b, to_c = lax.rem(self.me[b] + db, nb), lax.rem(self.me[c] + dc, nc)
            remote(
                self.sum1.at[to_b, to_c],
                self.recv2.at[db * nc + dc - 1],
                self.sem(12),
                self.sem(13),
                p.at(**{b: to_b, c: to_c}),
            )

    def e3(self):
        p = self.place
        _, b, c = self.axes
        wait_bytes(self.recv2, self.sem(13))
        total = self.sum1[self.me[b], self.me[c]].astype(F32)
        for i in range(self.recv2.shape[0]):
            total = total + self.recv2[i].astype(F32)
        slot = self.recv3.at[p.rep]
        slot[...] = total.astype(BF16)
        nrep = p.nx * p.nzl
        for d in range(1, nrep):
            remote(slot, slot, self.sem(14), self.sem(15), (lax.rem(p.rep + d, nrep), p.shard))

    def e4(self):
        p = self.place
        nrep = p.nx * p.nzl
        if nrep > 1:
            wait_bytes(self.recv3.at[pl.ds(0, nrep - 1)], self.sem(15))
        for zl in range(p.nzl):
            for x in range(p.nx):
                rows, cols = self.piece(zl, x)
                self.result[rows, cols] = self.recv3[zl * p.nx + x].astype(F32)
        pltpu.make_async_copy(self.result, self.out, self.sem(16)).start()

    def reduced(self):
        p = self.place
        wait_bytes(self.pair, self.sem(8))
        if self.n[self.axes[0]] > 1:
            wait_bytes(self.recv1, self.sem(10))
        wait_bytes(self.recv2, self.sem(12))
        if p.nx * p.nzl > 1:
            wait_bytes(self.recv3.at[pl.ds(0, p.nx * p.nzl - 1)], self.sem(14))
        pltpu.make_async_copy(self.result, self.out, self.sem(16)).wait()


def order_of(n):
    return (2, 1, 3) if n == 4 else tuple(range(1, n))


def side_by_side(block):
    n = block.shape[-2] // 2
    return jnp.concatenate([block[..., :n, :], block[..., n:, :]], axis=-1)


def one_above_other(block):
    return jnp.concatenate([block[..., :HD], block[..., HD:]], axis=-2)


def split_heads(joined, slots):
    for s in range(2):
        rows = joined[s * ROWS : (s + 1) * ROWS]
        for h in range(H):
            at = h * HD
            query, key = rows[:, at : at + HD], rows[:, D + at : D + at + HD]
            slots[s * H + h, 0:ROWS] = jnp.concatenate([query, key], axis=1)
            slots[s * H + h, ROWS:96] = side_by_side(rows[:, 2 * D + at : 2 * D + at + HD])


def split_context(context, slots):
    for s in range(2):
        rows = context[s * ROWS : (s + 1) * ROWS]
        for h in range(H):
            slots[s * H + h] = side_by_side(rows[:, h * HD : (h + 1) * HD])


def join_context(slots):
    parts = []
    for s in range(2):
        heads = [one_above_other(slots[s * H + h]) for h in range(H)]
        parts.append(jnp.concatenate(heads, axis=1))
    return jnp.concatenate(parts, axis=0)


def join_heads(slots):
    parts = []
    for s in range(2):
        both = [slots[s * H + h] for h in range(H)]
        queries = [block[0:ROWS, :HD] for block in both]
        keys = [block[0:ROWS, HD:] for block in both]
        values = [one_above_other(block[ROWS:96]) for block in both]
        parts.append(jnp.concatenate(queries + keys + values, axis=1))
    return jnp.concatenate(parts, axis=0)


def head_parts(slots):
    both = slots[:, 0:ROWS, :].reshape(LENGTH, 2 * HD)
    values = one_above_other(slots[:, ROWS:96, :]).reshape(LENGTH, HD)
    queries = (both[:, :HD].astype(F32) * 0.125).astype(BF16)
    return queries, both[:, HD:], values


def kernel(nx, nzl, *refs):
    refs = list(refs)

    def take(n):
        got = refs[:n]
        del refs[:n]
        return got

    x_ref, cot_ref = take(2)
    own = take(4)
    bias_ref, gain_ref, shift_ref, upb_ref = take(4)
    out_hbm, dx_hbm = take(2)
    result_hbm = take(4)
    bias_out, gain_out, shift_out, upb_out = take(4)
    out_ref, dx_ref = take(2)
    results = take(4)
    full = [take(len(PARTS)) for _ in range(LAYERS)]
    sums = [[take(6) for _ in PARTS] for _ in range(LAYERS)]
    swaps = [take(8) for _ in range(LAYERS)]
    small_own, small_all, small_grad, small_in, small_rep = take(5)
    small, small_up, d_small, d_small_up = take(4)
    saved = [take(8) for _ in range(LAYERS)]
    probs = take(LAYERS)
    query_ref, dc_ref, ctx_ref, dq_ref, dk_ref, dv_ref = take(6)
    part_sems, swap_sems, small_sems, out_sems = take(4)

    p = Place(nx, nzl)
    parts = []
    for l in range(LAYERS):
        row = []
        for i, (w, at, _, cols, far, near) in enumerate(PARTS):
            here = pl.ds(at, cols)
            row.append(
                Part(
                    p,
                    own[w].at[l, :, here],
                    full[l][i],
                    part_sems.at[l * len(PARTS) + i],
                    sums[l][i],
                    far,
                    near,
                    results[w].at[l, :, here],
                    result_hbm[w].at[l, :, here],
                )
            )
        parts.append(row)
    swap = [
        [Exchange(p, swaps[l][2 * i], swaps[l][2 * i + 1], swap_sems.at[l * 4 + i]) for i in range(4)]
        for l in range(LAYERS)
    ]
    everything = [part for row in parts for part in row]

    for part in everything:
        part.keep()
    small_own[...] = jnp.zeros_like(small_own)
    for l in range(LAYERS):
        at = l * 8
        small_own[at : at + 1, :] = upb_ref[l : l + 1, :].astype(F32)
        small_own[at + 1 : at + 4, 0:32] = bias_ref[l].astype(F32)
        small_own[at + 4 : at + 6, 0:32] = gain_ref[l].astype(F32)
        small_own[at + 6 : at + 8, 0:32] = shift_ref[l].astype(F32)
    small_all[p.shard] = small_own[...]
    barrier = pltpu.get_barrier_semaphore()
    peers = p.peers()
    for peer in peers:
        pl.semaphore_signal(barrier, inc=1, device_id=peer, device_id_type=MESH)
    pl.semaphore_wait(barrier, len(peers))

    me = p.shard

    def run(which, *steps):
        for step in steps:
            for part in which:
                getattr(part, step)()

    early, late = parts[0][:3], parts[0][3:]
    run(early, "g0")
    for to in p.group():
        remote(small_own, small_all.at[me], small_sems.at[0], small_sems.at[1], (p.rep, to))
    run(late, "g0")
    run(early, "g1")
    run(late, "g1")
    wait_bytes(small_all.at[pl.ds(0, GROUP - 1)], small_sems.at[1])
    for l in range(LAYERS):
        for q in range(4):
            part = [small_all[4 * q + i, l * 8 : l * 8 + 8, 0:32] for i in range(4)]
            small[l, :, q * 128 : (q + 1) * 128] = jnp.concatenate(part, axis=1)
        for t in range(GROUP):
            small_up[l, :, t * 128 : (t + 1) * 128] = small_all[t, l * 8 : l * 8 + 1, :]
    run(early, "g2", "g3")

    hidden = x_ref[...].astype(F32)
    for l in range(LAYERS):
        proj, up, down = parts[l][3], parts[l][4:6], parts[l][6:8]
        to_heads, to_tokens, _, _ = swap[l]
        source_ref, unit1, scale1, unit2, scale2, mid_ref, act_ref, slope_ref = saved[l]
        source = hidden.astype(BF16)
        source_ref[...] = source
        joined = [nn(source, part.value()) for part in parts[l][:3]]
        joined[2] = joined[2] + small[l, 1:2, :]
        split_heads(jnp.concatenate(joined, axis=1).astype(BF16), to_heads.out)
        to_heads.start()
        if l + 1 < LAYERS:
            run(parts[l + 1], "g0")
        run([proj], "g2")
        to_heads.wait()
        queries, keys, values = head_parts(to_heads.into[...])
        query_ref[...] = queries.reshape(NQ, QB, HD)
        values_t = values.T

        def attend(i, carry):
            scores = nt(keys, query_ref[i])
            expo = jnp.exp(scores - jnp.max(scores, axis=0, keepdims=True))
            prob = expo * (1.0 / jnp.sum(expo, axis=0, keepdims=True))
            probs[l][i] = prob
            ctx_ref[i] = nn(values_t, prob.astype(BF16)).T.astype(BF16)
            return carry

        lax.fori_loop(0, NQ, attend, 0)
        context = ctx_ref[...].reshape(GROUP, ROWS, HD)
        to_tokens.out[...] = side_by_side(context)
        to_tokens.start()
        run(up, "g2")
        if l + 1 < LAYERS:
            run(parts[l + 1], "g1")
        run([proj], "g3")
        to_tokens.wait()
        context = join_context(to_tokens.into)
        first = hidden + nn(context, proj.value()) + small[l, 2:3, :]
        middle, unit, scale = norm_forward(first, small[l, 4:5, :], small[l, 6:7, :])
        unit1[...], scale1[...] = unit, scale
        mid_low = middle.astype(BF16)
        mid_ref[...] = mid_low
        run(up, "g3")
        run(down, "g2")
        for j in range(4):
            at = j * 512
            weight = up[j // 2].full[:, :, :, :, (j % 2) * 512 : (j % 2) * 512 + 512].reshape(D, 512)
            upper = nn(mid_low, weight) + small_up[l, :, at : at + 512]
            phi = 0.5 + 0.5 * lax.erf(upper * (0.5**0.5))
            act_ref[:, at : at + 512] = (upper * phi).astype(BF16)
            density = jnp.exp(-0.5 * upper * upper) * 0.3989422804014327
            slope_ref[:, at : at + 512] = phi + upper * density
        if l + 1 < LAYERS:
            run(parts[l + 1][:3], "g2")
        run(down, "g3")
        second = jnp.concatenate([nn(act_ref[...], part.value()) for part in down], axis=1)
        second = middle + second + small[l, 3:4, :]
        hidden, unit, scale = norm_forward(second, small[l, 5:6, :], small[l, 7:8, :])
        unit2[...], scale2[...] = unit, scale
        if l + 1 < LAYERS:
            run(parts[l + 1][:3], "g3")
    out_ref[...] = hidden.astype(BF16)
    out_copy = pltpu.make_async_copy(out_ref, out_hbm, out_sems.at[0])
    out_copy.start()

    grad = cot_ref[...].astype(F32)
    for l in reversed(range(LAYERS)):
        qkv, proj, up, down = parts[l][:3], parts[l][3], parts[l][4:6], parts[l][6:8]
        above = parts[l + 1] if l + 1 < LAYERS else []
        to_heads, to_tokens, d_to_heads, d_to_tokens = swap[l]
        source_ref, unit1, scale1, unit2, scale2, mid_ref, act_ref, slope_ref = saved[l]
        grad_two, d_small[l, 5:6, :], d_small[l, 7:8, :] = norm_backward(
            grad, unit2[...], scale2[...], small[l, 5:6, :]
        )
        low_two = grad_two.astype(BF16)
        d_small[l, 3:4, :] = column_sum(low_two.astype(F32))
        d_uppers = []
        for j in range(4):
            at = j * 512
            d_act = 0.0
            for i in range(2):
                weight = down[i].full[j // 2, (j % 2) * 2 : (j % 2) * 2 + 2].reshape(512, 256)
                d_act = d_act + nt(low_two[:, i * 256 : (i + 1) * 256], weight)
            d_upper = (d_act * slope_ref[:, at : at + 512]).astype(BF16)
            d_small_up[l, :, at : at + 512] = column_sum(d_upper.astype(F32))
            d_uppers.append(d_upper)
        d_upper = jnp.concatenate(d_uppers, axis=1)
        run(above[:3], "e1")
        grad_mid = grad_two
        for i in range(2):
            grad_mid = grad_mid + nt(d_upper[:, i * 1024 : (i + 1) * 1024], up[i].value())
        grad_one, d_small[l, 4:5, :], d_small[l, 6:7, :] = norm_backward(
            grad_mid, unit1[...], scale1[...], small[l, 4:5, :]
        )
        low_one = grad_one.astype(BF16)
        d_small[l, 2:3, :] = column_sum(low_one.astype(F32))
        d_context = nt(low_one, proj.value()).astype(BF16)
        split_context(d_context, d_to_heads.out)
        d_to_heads.start()
        run(down + up + [proj], "sent")
        for i in range(2):
            for j in range(8):
                block = tn(act_ref[:, j * 256 : (j + 1) * 256], low_two[:, i * 256 : (i + 1) * 256])
                down[i].store(j * 256, block)
            down[i].e0()
        for i in range(2):
            for j in range(2):
                block = tn(mid_ref[:, j * 256 : (j + 1) * 256], d_upper[:, i * 1024 : (i + 1) * 1024])
                up[i].store(j * 256, block)
            up[i].e0()
        context = join_context(to_tokens.into)
        for j in range(2):
            proj.store(j * 256, tn(context[:, j * 256 : (j + 1) * 256], low_one))
        proj.e0()
        d_to_heads.wait()
        run(down, "e1")
        queries, keys, values = head_parts(to_heads.into[...])
        query_ref[...] = queries.reshape(NQ, QB, HD)
        dc_ref[...] = one_above_other(d_to_heads.into[...]).reshape(NQ, QB, HD)
        keys_t = keys.T
        dk_ref[...] = jnp.zeros_like(dk_ref)
        dv_ref[...] = jnp.zeros_like(dv_ref)

        def attend_back(i, carry):
            d_ctx = dc_ref[i]
            d_prob = nt(values, d_ctx)
            prob = probs[l][i]
            row = jnp.sum(prob * d_prob, axis=0, keepdims=True)
            d_score = (prob * (d_prob - row)).astype(BF16)
            dv_ref[...] += nn(prob.astype(BF16), d_ctx)
            dk_ref[...] += nn(d_score, query_ref[i])
            dq_ref[i] = (nn(keys_t, d_score) * 0.125).T.astype(BF16)
            return carry

        lax.fori_loop(0, NQ, attend_back, 0)
        both = jnp.concatenate([dq_ref[...].reshape(LENGTH, HD), dk_ref[...].astype(BF16)], axis=1)
        d_to_tokens.out[:, 0:ROWS, :] = both.reshape(GROUP, ROWS, 2 * HD)
        d_to_tokens.out[:, ROWS:96, :] = side_by_side(dv_ref[...].astype(BF16).reshape(GROUP, ROWS, HD))
        d_to_tokens.start()
        run(up + [proj], "e1")
        run(above, "e2")
        run(qkv, "sent")
        d_to_tokens.wait()
        d_joined = join_heads(d_to_tokens.into)
        d_small[l, 1:2, :] = column_sum(d_joined[:, 2 * D :].astype(F32))
        grad = grad_one
        for i in range(3):
            grad = grad + nt(d_joined[:, i * D : (i + 1) * D], qkv[i].value())
        source = source_ref[...]
        for i in range(3):
            qkv[i].store(0, tn(source, d_joined[:, i * D : (i + 1) * D]))
            qkv[i].e0()
    dx_ref[...] = grad
    dx_copy = pltpu.make_async_copy(dx_ref, dx_hbm, out_sems.at[1])
    dx_copy.start()
    qkv, rest, above = parts[0][:3], parts[0][3:], parts[1]
    run(qkv, "e1")
    run(above, "e3")

    small_grad[...] = jnp.zeros_like(small_grad)
    for l in range(LAYERS):
        for t in range(GROUP):
            small_grad[t, l * 8 + 1 : l * 8 + 8, 0:32] = d_small[l, 1:8, t * 32 : (t + 1) * 32]
            small_grad[t, l * 8 : l * 8 + 1, :] = d_small_up[l, :, t * 128 : (t + 1) * 128]
    for to in p.group():
        remote(small_grad.at[to], small_in.at[me], small_sems.at[2], small_sems.at[3], (p.rep, to))
    small_in[me] = small_grad[me]
    run(rest, "e2")
    run(qkv, "e2")
    run(above, "e4")
    wait_bytes(small_in.at[pl.ds(0, GROUP - 1)], small_sems.at[3])
    total = small_in[0]
    for t in range(1, GROUP):
        total = total + small_in[t]
    slot = small_rep.at[p.rep]
    slot[...] = total
    nrep = nx * nzl
    for d in range(1, nrep):
        remote(slot, slot, small_sems.at[4], small_sems.at[5], (lax.rem(p.rep + d, nrep), me))
    run(rest, "e3")
    run(qkv, "e3")
    run(rest, "e4")
    if nrep > 1:
        wait_bytes(small_rep.at[pl.ds(0, nrep - 1)], small_sems.at[5])
    total = small_rep[0]
    for t in range(1, nrep):
        total = total + small_rep[t]
    for l in range(LAYERS):
        at = l * 8
        upb_out[l : l + 1, :] = total[at : at + 1, :]
        bias_out[l] = total[at + 1 : at + 4, 0:32]
        gain_out[l] = total[at + 4 : at + 6, 0:32]
        shift_out[l] = total[at + 6 : at + 8, 0:32]
    run(qkv, "e4")

    run(everything, "reduced")
    for l in range(LAYERS):
        for one in swap[l]:
            one.finish()
    wait_bytes(small_all.at[pl.ds(0, GROUP - 1)], small_sems.at[0])
    wait_bytes(small_grad.at[pl.ds(0, GROUP - 1)], small_sems.at[2])
    if nrep > 1:
        wait_bytes(small_rep.at[pl.ds(0, nrep - 1)], small_sems.at[4])
    out_copy.wait()
    dx_copy.wait()


def scratch(nx, nzl, members):
    sizes = {"x": nx, "y": Y, "z": ZH * nzl}
    nrep = nx * nzl
    shapes = [pltpu.VMEM((TOK, D), BF16), pltpu.VMEM((TOK, D), F32)]
    shapes += [pltpu.VMEM(member.shape, F32) for member in members[:4]]
    for _ in range(LAYERS):
        for _, _, r, c, _, _ in PARTS:
            shapes.append(pltpu.VMEM((ZH, Y, CORES, r, c), BF16))
    for _ in range(LAYERS):
        for _, _, r, c, _, near in PARTS:
            piece = (r // nrep, c) if r == 128 else (r // nzl, c // nx)
            na, nb, nc = [sizes[axis] for axis in {"x": "xyz", "y": "yxz", "z": "zxy"}[near]]
            shapes.append(pltpu.VMEM((ZH, Y, r, c), BF16))
            shapes.append(pltpu.VMEM((na, nb, nc) + piece, BF16))
            shapes.append(pltpu.VMEM((max(na - 1, 1), nb, nc) + piece, BF16))
            shapes.append(pltpu.VMEM((nb, nc) + piece, BF16))
            shapes.append(pltpu.VMEM((nb * nc - 1,) + piece, BF16))
            shapes.append(pltpu.VMEM((nrep,) + piece, BF16))
    for _ in range(LAYERS):
        for rows in (96, 32, 32, 96):
            shapes += [pltpu.VMEM((GROUP, rows, 128), BF16)] * 2
    shapes += [pltpu.VMEM((16, 128), F32)]
    shapes += [pltpu.VMEM((GROUP, 16, 128), F32)] * 3
    shapes += [pltpu.VMEM((nrep, 16, 128), F32)]
    shapes += [pltpu.VMEM((LAYERS, 8, D), F32), pltpu.VMEM((LAYERS, 1, FF), F32)] * 2
    for _ in range(LAYERS):
        shapes += [
            pltpu.VMEM((TOK, D), BF16),
            pltpu.VMEM((TOK, D), F32),
            pltpu.VMEM((TOK, 1), F32),
            pltpu.VMEM((TOK, D), F32),
            pltpu.VMEM((TOK, 1), F32),
            pltpu.VMEM((TOK, D), BF16),
            pltpu.VMEM((TOK, FF), BF16),
            pltpu.VMEM((TOK, FF), F32),
        ]
    shapes += [pltpu.VMEM((NQ, LENGTH, QB), F32)] * LAYERS
    shapes += [pltpu.VMEM((NQ, QB, HD), BF16)] * 4
    shapes += [pltpu.VMEM((LENGTH, HD), F32)] * 2
    shapes += [
        pltpu.SemaphoreType.DMA((LAYERS * len(PARTS), SEMS)),
        pltpu.SemaphoreType.DMA((LAYERS * 4, 2)),
        pltpu.SemaphoreType.DMA((6,)),
        pltpu.SemaphoreType.DMA((2,)),
    ]
    return shapes


def copy_kernel(*refs):
    n = 10
    source, target, held, sems = refs[:n], refs[n : 2 * n], refs[2 * n : 3 * n], refs[-1]
    into = [pltpu.make_async_copy(source[i], held[i], sems.at[0, i]) for i in range(n)]
    outof = [pltpu.make_async_copy(held[i], target[i], sems.at[1, i]) for i in range(n)]
    for copy in into:
        copy.start()
    for i in range(n):
        into[i].wait()
        outof[i].start()
    for copy in outof:
        copy.wait()


def local_call(nx, nzl, inputs, *arguments):
    cotangent, members = arguments[-1], arguments[:-1]
    shapes = [jax.ShapeDtypeStruct((TOK, D), BF16), jax.ShapeDtypeStruct((TOK, D), F32)]
    shapes += [jax.ShapeDtypeStruct(member.shape, F32) for member in members]
    anywhere, vmem = pl.BlockSpec(memory_space=pl.ANY), pl.BlockSpec(memory_space=pltpu.VMEM)
    got = pl.pallas_call(
        functools.partial(kernel, nx, nzl),
        out_shape=shapes,
        in_specs=[vmem] * 10,
        out_specs=[anywhere] * 6 + [vmem] * 4,
        scratch_shapes=scratch(nx, nzl, members),
        compiler_params=pltpu.CompilerParams(
            collective_id=0, has_side_effects=True, vmem_limit_bytes=63 * 1024 * 1024
        ),
        cost_estimate=pl.CostEstimate(flops=7 * 10**9, bytes_accessed=8 * 10**6, transcendentals=5 * 10**6),
    )(inputs.reshape(TOK, D), cotangent.reshape(TOK, D), *members)
    return pl.pallas_call(
        copy_kernel,
        out_shape=shapes,
        in_specs=[anywhere] * 10,
        out_specs=[anywhere] * 10,
        scratch_shapes=[pltpu.VMEM(shape.shape, shape.dtype) for shape in shapes] + [pltpu.SemaphoreType.DMA((2, 10))],
    )(*got)


def solution(mesh):
    nrep = mesh.shape["rep"]
    nzl = 2 if nrep >= 2 else 1
    nx = nrep // nzl

    def shards(inputs, *arguments):
        got = local_call(nx, nzl, inputs, *arguments)
        return (got[0].reshape(inputs.shape), got[1].reshape(inputs.shape), *got[2:])

    rows, columns = P(None, "shard", None), P(None, None, "shard")
    both = P("rep", "shard", None)
    weights = (rows, rows, rows, rows, columns, columns, columns, P(None, "shard"))
    return jax.shard_map(
        shards,
        mesh=mesh,
        in_specs=(both, *weights, both),
        out_specs=(both, both, *weights),
        check_vma=False,
    )
```

```python
import functools

import jax
import jax.numpy as jnp
from jax import lax
from jax.experimental import pallas as pl
from jax.experimental.pallas import tpu as pltpu
from jax.sharding import PartitionSpec as P

MESH = pl.DeviceIdType.MESH
F32 = jnp.float32
BF16 = jnp.bfloat16
H, HD, D, FF, LAYERS = 8, 64, 512, 2048, 2
ZH, Y, CORES = 2, 4, 2
GROUP = ZH * Y * CORES
ROWS = 64
TOK = 2 * ROWS
LENGTH = GROUP * ROWS
QB = 256
NQ = LENGTH // QB
QKV, PROJ, UP, DOWN = range(4)
PARTS = (
    (QKV, 0, 32, 512, "xx", "xx"),
    (QKV, 512, 32, 512, "zz", "zz"),
    (QKV, 1024, 32, 512, "yy", "yy"),
    (PROJ, 0, 32, 512, "xx", "xx"),
    (UP, 0, 32, 1024, "xx", "xx"),
    (UP, 1024, 32, 1024, "zz", "zz"),
    (DOWN, 0, 128, 256, "xx", "xx"),
    (DOWN, 256, 128, 256, "yz", "yy"),
)
SEMS = 17


def nn(a, b):
    return jnp.dot(a, b, preferred_element_type=F32)


def nt(a, b):
    return lax.dot_general(a, b, (((1,), (1,)), ((), ())), preferred_element_type=F32)


def tn(a, b):
    return lax.dot_general(a, b, (((0,), (0,)), ((), ())), preferred_element_type=F32)


def norm_forward(values, gain, shift):
    center = values - jnp.mean(values, axis=-1, keepdims=True)
    spread = jnp.mean(center * center, axis=-1, keepdims=True)
    scale = lax.rsqrt(spread + 1e-06)
    unit = center * scale
    return unit * gain + shift, unit, scale


def norm_backward(grad, unit, scale, gain):
    d_unit = grad * gain
    first = jnp.mean(d_unit, axis=-1, keepdims=True)
    second = jnp.mean(d_unit * unit, axis=-1, keepdims=True)
    d_gain = jnp.sum(grad * unit, axis=0, keepdims=True)
    d_shift = jnp.sum(grad, axis=0, keepdims=True)
    return scale * (d_unit - first - unit * second), d_gain, d_shift


def column_sum(values):
    return jnp.sum(values, axis=0, keepdims=True)


def wait_bytes(ref, sem):
    pltpu.make_async_copy(ref, ref, sem).wait()


class Place:
    def __init__(self, nx, nzl):
        self.nx, self.nzl, self.nz = nx, nzl, ZH * nzl
        rep, shard = lax.axis_index("rep"), lax.axis_index("shard")
        self.rep, self.shard = rep, shard
        self.zl, self.x = lax.div(rep, nx), lax.rem(rep, nx)
        self.zh, self.y = lax.div(shard, Y * CORES), lax.rem(lax.div(shard, CORES), Y)
        self.core = lax.rem(shard, CORES)
        self.z = self.zh * nzl + self.zl

    def at(self, x=None, y=None, z=None, core=None):
        x = self.x if x is None else x
        y = self.y if y is None else y
        z = self.z if z is None else z
        core = self.core if core is None else core
        zh, zl = lax.div(z, self.nzl), lax.rem(z, self.nzl)
        return (zl * self.nx + x, zh * (Y * CORES) + y * CORES + core)

    def xs(self, d):
        return lax.rem(self.x + d, self.nx)

    def ys(self, d):
        return lax.rem(self.y + d, Y)

    def zs(self, d):
        return lax.rem(self.z + d, self.nz)

    def group(self):
        steps = [(dy, dz, dc) for dy in (2, 1, 3, 0) for dz in (1, 0) for dc in range(CORES) if dy or dz or dc]
        steps.sort(key=lambda step: -(2 * min(step[0], 1) + 2 * step[1] + step[2]))
        found = []
        for dy, dz, dc in steps:
            z = lax.rem(self.z + dz * self.nzl, self.nz)
            found.append(self.at(y=self.ys(dy), z=z, core=lax.rem(self.core + dc, CORES))[1])
        return found

    def peers(self):
        found = []
        for dy in range(Y):
            for dz in range(self.nz):
                if dy or dz:
                    found.append(self.at(y=self.ys(dy), z=self.zs(dz)))
        for dx in range(1, self.nx):
            for dz in range(self.nz):
                found.append(self.at(x=self.xs(dx), z=self.zs(dz)))
        for dx in range(1, self.nx):
            for dy in range(1, Y):
                found.append(self.at(x=self.xs(dx), y=self.ys(dy)))
        for dy in range(Y):
            for zh in range(ZH):
                z = lax.rem(self.z + zh * self.nzl, self.nz)
                found.append(self.at(y=self.ys(dy), z=z, core=1 - self.core))
        return found


def remote(src, dst, send_sem, recv_sem, device):
    pltpu.make_async_remote_copy(
        src_ref=src, dst_ref=dst, send_sem=send_sem, recv_sem=recv_sem, device_id=device, device_id_type=MESH
    ).start()


class Exchange:
    def __init__(self, place, out, into, sems):
        self.place, self.out, self.into, self.sems = place, out, into, sems

    def start(self):
        me = self.place.shard
        for to in self.place.group():
            remote(self.out.at[to], self.into.at[me], self.sems.at[0], self.sems.at[1], (self.place.rep, to))
        self.into[me] = self.out[me]

    def send(self, first, blocks):
        me = self.place.shard
        for j in range(blocks.shape[0]):
            self.out[first + j] = blocks[j]
        for j in range(blocks.shape[0]):
            to = first + j

            @pl.when(to != me)
            def _():
                remote(self.out.at[to], self.into.at[me], self.sems.at[0], self.sems.at[1], (self.place.rep, to))

            @pl.when(to == me)
            def _():
                self.into[me] = self.out[me]

    def wait(self):
        wait_bytes(self.into.at[pl.ds(0, GROUP - 1)], self.sems.at[1])

    def finish(self):
        wait_bytes(self.out.at[pl.ds(0, GROUP - 1)], self.sems.at[0])


class Part:
    def __init__(self, place, own, full, grad, sems, sums, far, near, result, out):
        self.place, self.own, self.full, self.grad, self.sems = place, own, full, grad, sems
        self.pair, self.chip, self.recv1, self.sum1, self.recv2, self.recv3 = sums
        self.far, self.near, self.result, self.out = far, near, result, out
        self.rows, self.cols = own.shape
        p = place
        self.n = {"x": p.nx, "y": Y, "z": p.nz}
        self.me = {"x": p.x, "y": p.y, "z": p.z}
        self.axes = {"x": "xyz", "y": "yxz", "z": "zxy"}[near]

    def sem(self, i):
        return self.sems.at[i]

    def sibling(self):
        return self.place.at(core=1 - self.place.core)

    def across(self):
        return self.place.nz - 1 - self.place.z

    def keep(self):
        p = self.place
        self.full[p.zh, p.y, p.core] = self.own[...]

    def quarter(self, ref, x):
        nx = self.place.nx
        if self.rows == 128:
            n = self.rows // nx
            return ref.at[..., pl.ds(pl.multiple_of(x * n, n), n), :]
        n = self.cols // nx
        return ref.at[..., pl.ds(pl.multiple_of(x * n, n), n)]

    def g0(self):
        p = self.place
        slot = self.full.at[p.zh, p.y, p.core]
        if self.far == "x":
            src, dst = self.quarter(self.own, p.x), self.quarter(slot, p.x)
            for d in (2, 1, 3, 0):
                remote(src, dst, self.sem(4), self.sem(1), p.at(y=p.ys(d), z=self.across()))
            for d in (2, 1, 3):
                remote(src, dst, self.sem(3), self.sem(0), p.at(y=p.ys(d)))
        else:
            if self.far == "y":
                remote(self.own, slot, self.sem(3), self.sem(0), p.at(z=self.across()))
            for d in (2, 1, 3):
                remote(self.own, slot, self.sem(4), self.sem(1), p.at(y=p.ys(d)))

    def g1(self):
        p, full = self.place, self.full
        if self.far == "x":
            wait_bytes(self.quarter(full.at[0, pl.ds(0, 3), 0], 0), self.sem(0))
            wait_bytes(self.quarter(full.at[0, :, 0], 0), self.sem(1))
            mine = self.quarter(full.at[:, :, p.core], p.x)
            for d in order_of(p.nx):
                remote(mine, mine, self.sem(5), self.sem(2), p.at(x=p.xs(d)))
        elif self.far == "y":
            wait_bytes(full.at[0, 0, 0], self.sem(0))
            slot = full.at[1 - p.zh, p.y, p.core]
            for d in (2, 1, 3):
                remote(slot, slot, self.sem(5), self.sem(2), p.at(y=p.ys(d)))
        else:
            wait_bytes(full.at[0, pl.ds(0, 3), 0], self.sem(1))
            half = full.at[p.zh, :, p.core]
            remote(half, half, self.sem(5), self.sem(2), p.at(z=self.across()))

    def g2(self):
        p, full = self.place, self.full
        if self.far == "x":
            if p.nx > 1:
                wait_bytes(full.at[:, pl.ds(0, p.nx - 1), 0], self.sem(2))
        elif self.far == "y":
            wait_bytes(full.at[0, pl.ds(0, 3), 0], self.sem(1))
            wait_bytes(full.at[0, pl.ds(0, 3), 0], self.sem(2))
        else:
            wait_bytes(full.at[0, :, 0], self.sem(2))
        both = full.at[:, :, p.core]
        remote(both, both, self.sem(6), self.sem(7), self.sibling())

    def g3(self):
        wait_bytes(self.full.at[:, :, 0], self.sem(7))

    def sent(self):
        full, nx = self.full, self.place.nx
        if self.far == "x":
            wait_bytes(self.quarter(full.at[0, pl.ds(0, 3), 0], 0), self.sem(3))
            wait_bytes(self.quarter(full.at[0, :, 0], 0), self.sem(4))
            if nx > 1:
                wait_bytes(full.at[:, pl.ds(0, nx - 1), 0], self.sem(5))
        elif self.far == "y":
            wait_bytes(full.at[0, 0, 0], self.sem(3))
            wait_bytes(full.at[0, pl.ds(0, 3), 0], self.sem(4))
            wait_bytes(full.at[0, pl.ds(0, 3), 0], self.sem(5))
        else:
            wait_bytes(full.at[0, pl.ds(0, 3), 0], self.sem(4))
            wait_bytes(full.at[0, :, 0], self.sem(5))
        wait_bytes(full.at[:, :, 0], self.sem(6))

    def value(self):
        return self.full[...].reshape(GROUP * self.rows, self.cols)

    def store(self, start, block):
        count = block.shape[0]
        per_y = CORES * self.rows
        block = block.astype(BF16)
        if count == ZH * Y * per_y:
            self.grad[...] = block.reshape(ZH, Y, CORES, self.rows, self.cols)
        elif count == Y * per_y:
            self.grad[start // count] = block.reshape(Y, CORES, self.rows, self.cols)
        else:
            n = count // per_y
            zh, y = divmod(start // per_y, Y)
            self.grad[zh, y : y + n] = block.reshape(n, CORES, self.rows, self.cols)

    def piece(self, zl, x):
        p = self.place
        if self.rows == 128:
            n = self.rows // (p.nx * p.nzl)
            at = (zl * p.nx + x) * n
            return slice(at, at + n), slice(None)
        half, part = self.rows // p.nzl, self.cols // p.nx
        return slice(zl * half, (zl + 1) * half), slice(x * part, (x + 1) * part)

    def e0(self):
        p = self.place
        remote(self.grad.at[:, :, 1 - p.core], self.pair, self.sem(8), self.sem(9), self.sibling())

    def e1(self):
        p = self.place
        wait_bytes(self.pair, self.sem(9))
        for zh in range(ZH):
            for y in range(Y):
                total = self.grad[zh, y, p.core].astype(F32) + self.pair[zh, y].astype(F32)
                total = total.astype(BF16)
                for x in range(p.nx):
                    for zl in range(p.nzl):
                        at = {"x": x, "y": y, "z": zh * p.nzl + zl}
                        rows, cols = self.piece(zl, x)
                        self.chip[tuple(at[axis] for axis in self.axes)] = total[rows, cols]
        a = self.axes[0]
        for d in order_of(self.n[a]):
            to = lax.rem(self.me[a] + d, self.n[a])
            remote(self.chip.at[to], self.recv1.at[d - 1], self.sem(10), self.sem(11), p.at(**{a: to}))

    def e2(self):
        p = self.place
        a, b, c = self.axes
        nb, nc = self.n[b], self.n[c]
        if self.n[a] > 1:
            wait_bytes(self.recv1, self.sem(11))
        for ib in range(nb):
            total = self.chip[self.me[a], ib].astype(F32)
            for d in range(self.n[a] - 1):
                total = total + self.recv1[d, ib].astype(F32)
            self.sum1[ib] = total.astype(BF16)
        pairs = [(db, dc) for db in range(nb) for dc in range(nc) if db or dc]
        for db, dc in sorted(pairs, key=lambda at: -(min(at[0], 1) + min(at[1], 1))):
            to_b, to_c = lax.rem(self.me[b] + db, nb), lax.rem(self.me[c] + dc, nc)
            remote(
                self.sum1.at[to_b, to_c],
                self.recv2.at[db * nc + dc - 1],
                self.sem(12),
                self.sem(13),
                p.at(**{b: to_b, c: to_c}),
            )

    def e3(self):
        p = self.place
        _, b, c = self.axes
        wait_bytes(self.recv2, self.sem(13))
        total = self.sum1[self.me[b], self.me[c]].astype(F32)
        for i in range(self.recv2.shape[0]):
            total = total + self.recv2[i].astype(F32)
        slot = self.recv3.at[p.rep]
        slot[...] = total.astype(BF16)
        nrep = p.nx * p.nzl
        for d in range(1, nrep):
            remote(slot, slot, self.sem(14), self.sem(15), (lax.rem(p.rep + d, nrep), p.shard))

    def e4(self):
        p = self.place
        nrep = p.nx * p.nzl
        if nrep > 1:
            wait_bytes(self.recv3.at[pl.ds(0, nrep - 1)], self.sem(15))
        for zl in range(p.nzl):
            for x in range(p.nx):
                rows, cols = self.piece(zl, x)
                self.result[rows, cols] = self.recv3[zl * p.nx + x].astype(F32)
        pltpu.make_async_copy(self.result, self.out, self.sem(16)).start()

    def reduced(self):
        p = self.place
        wait_bytes(self.pair, self.sem(8))
        if self.n[self.axes[0]] > 1:
            wait_bytes(self.recv1, self.sem(10))
        wait_bytes(self.recv2, self.sem(12))
        if p.nx * p.nzl > 1:
            wait_bytes(self.recv3.at[pl.ds(0, p.nx * p.nzl - 1)], self.sem(14))
        pltpu.make_async_copy(self.result, self.out, self.sem(16)).wait()


def order_of(n):
    return (2, 1, 3) if n == 4 else tuple(range(1, n))


def side_by_side(block):
    n = block.shape[-2] // 2
    return jnp.concatenate([block[..., :n, :], block[..., n:, :]], axis=-1)


def one_above_other(block):
    return jnp.concatenate([block[..., :HD], block[..., HD:]], axis=-2)


def split_heads(joined, slots):
    for s in range(2):
        rows = joined[s * ROWS : (s + 1) * ROWS]
        for h in range(H):
            at = h * HD
            query, key = rows[:, at : at + HD], rows[:, D + at : D + at + HD]
            slots[s * H + h, 0:ROWS] = jnp.concatenate([query, key], axis=1)
            slots[s * H + h, ROWS:96] = side_by_side(rows[:, 2 * D + at : 2 * D + at + HD])


def split_context(context, slots):
    for s in range(2):
        rows = context[s * ROWS : (s + 1) * ROWS]
        for h in range(H):
            slots[s * H + h] = side_by_side(rows[:, h * HD : (h + 1) * HD])


def join_context(slots):
    parts = []
    for s in range(2):
        heads = [one_above_other(slots[s * H + h]) for h in range(H)]
        parts.append(jnp.concatenate(heads, axis=1))
    return jnp.concatenate(parts, axis=0)


def join_heads(slots):
    parts = []
    for s in range(2):
        both = [slots[s * H + h] for h in range(H)]
        queries = [block[0:ROWS, :HD] for block in both]
        keys = [block[0:ROWS, HD:] for block in both]
        values = [one_above_other(block[ROWS:96]) for block in both]
        parts.append(jnp.concatenate(queries + keys + values, axis=1))
    return jnp.concatenate(parts, axis=0)


def head_parts(slots):
    both = slots[:, 0:ROWS, :].reshape(LENGTH, 2 * HD)
    values = one_above_other(slots[:, ROWS:96, :]).reshape(LENGTH, HD)
    queries = (both[:, :HD].astype(F32) * 0.125).astype(BF16)
    return queries, both[:, HD:], values


def kernel(nx, nzl, *refs):
    refs = list(refs)

    def take(n):
        got = refs[:n]
        del refs[:n]
        return got

    x_ref, cot_ref = take(2)
    own = take(4)
    bias_ref, gain_ref, shift_ref, upb_ref = take(4)
    out_hbm, dx_hbm = take(2)
    result_hbm = take(4)
    bias_out, gain_out, shift_out, upb_out = take(4)
    out_ref, dx_ref = take(2)
    results = take(4)
    full = [take(len(PARTS)) for _ in range(LAYERS)]
    last_grads = take(3)
    sums = [[take(6) for _ in PARTS] for _ in range(LAYERS)]
    swaps = [take(8) for _ in range(LAYERS)]
    small_own, small_all, small_grad, small_in, small_rep = take(5)
    small, small_up, d_small, d_small_up = take(4)
    saved = [take(8) for _ in range(LAYERS)]
    probs = take(LAYERS)
    (shares,) = take(1)
    query_ref, dc_ref, dq_ref, dk_ref, dv_ref = take(5)
    part_sems, swap_sems, small_sems, out_sems = take(4)

    p = Place(nx, nzl)
    parts = []
    for l in range(LAYERS):
        row = []
        for i, (w, at, _, cols, far, near) in enumerate(PARTS):
            here = pl.ds(at, cols)
            row.append(
                Part(
                    p,
                    own[w].at[l, :, here],
                    full[l][i],
                    last_grads[i] if l == 0 and i < 3 else full[l][i],
                    part_sems.at[l * len(PARTS) + i],
                    sums[l][i],
                    far[l],
                    near[l],
                    results[w].at[l, :, here],
                    result_hbm[w].at[l, :, here],
                )
            )
        parts.append(row)
    swap = [
        [Exchange(p, swaps[l][2 * i], swaps[l][2 * i + 1], swap_sems.at[l * 4 + i]) for i in range(4)]
        for l in range(LAYERS)
    ]
    everything = [part for row in parts for part in row]

    for part in everything:
        part.keep()
    small_own[...] = jnp.zeros_like(small_own)
    for l in range(LAYERS):
        at = l * 8
        small_own[at : at + 1, :] = upb_ref[l : l + 1, :].astype(F32)
        small_own[at + 1 : at + 4, 0:32] = bias_ref[l].astype(F32)
        small_own[at + 4 : at + 6, 0:32] = gain_ref[l].astype(F32)
        small_own[at + 6 : at + 8, 0:32] = shift_ref[l].astype(F32)
    small_all[p.shard] = small_own[...]
    barrier = pltpu.get_barrier_semaphore()
    peers = p.peers()
    for peer in peers:
        pl.semaphore_signal(barrier, inc=1, device_id=peer, device_id_type=MESH)
    pl.semaphore_wait(barrier, len(peers))

    me = p.shard

    def along(which, axes):
        return [part for part in which if part.far in axes]

    def first_along(which, axes):
        return [part for part in which if part.near in axes]

    def run(which, *steps):
        for step in steps:
            for part in which:
                getattr(part, step)()

    early, late = parts[0][:3], parts[0][3:]
    run(early, "g0")
    run(early, "g1")
    for to in p.group():
        remote(small_own, small_all.at[me], small_sems.at[0], small_sems.at[1], (p.rep, to))
    run(along(late, "x"), "g0")
    run(along(late, "yz"), "g0")
    run(early, "g2")
    wait_bytes(small_all.at[pl.ds(0, GROUP - 1)], small_sems.at[1])
    for l in range(LAYERS):
        for q in range(4):
            part = [small_all[4 * q + i, l * 8 : l * 8 + 8, 0:32] for i in range(4)]
            small[l, :, q * 128 : (q + 1) * 128] = jnp.concatenate(part, axis=1)
        for t in range(GROUP):
            small_up[l, :, t * 128 : (t + 1) * 128] = small_all[t, l * 8 : l * 8 + 1, :]
    run(early, "g3")

    hidden = x_ref[...].astype(F32)
    for l in range(LAYERS):
        proj, up, down = parts[l][3], parts[l][4:6], parts[l][6:8]
        to_heads, to_tokens, _, _ = swap[l]
        source_ref, unit1, scale1, unit2, scale2, mid_ref, act_ref, slope_ref = saved[l]
        source = hidden.astype(BF16)
        source_ref[...] = source
        joined = [nn(source, part.value()) for part in parts[l][:3]]
        joined[2] = joined[2] + small[l, 1:2, :]
        split_heads(jnp.concatenate(joined, axis=1).astype(BF16), to_heads.out)
        to_heads.start()
        if l + 1 < LAYERS:
            run(along(late, "x"), "g1")
        run(up[1:] + down[1:], "g1")
        if l + 1 < LAYERS:
            run(parts[l + 1][:3], "g0")
        run([proj], "g2")
        to_heads.wait()
        queries, keys, values = head_parts(to_heads.into[...])
        query_ref[...] = queries.reshape(NQ, QB, HD)
        values_t = values.T

        def attend(i, carry):
            scores = nt(keys, query_ref[i])
            expo = jnp.exp(scores - jnp.max(scores, axis=0, keepdims=True))
            part = 1.0 / jnp.sum(expo, axis=0, keepdims=True)
            low = expo.astype(BF16)
            probs[l][i] = low
            shares[l, i] = part
            block = (nn(values_t, low) * part).T.astype(BF16).reshape(QB // ROWS, ROWS, HD)
            to_tokens.send(i * (QB // ROWS), side_by_side(block))
            return carry

        lax.fori_loop(0, NQ, lambda i, carry: attend(lax.rem(i + (1 - p.zh) * (NQ // 2), NQ), carry), 0)
        if l + 1 < LAYERS:
            run(parts[l + 1][:3], "g1")
            run(parts[l + 1][3:], "g0")
        run([proj], "g3")
        run(up, "g2")
        to_tokens.wait()
        context = join_context(to_tokens.into)
        first = hidden + nn(context, proj.value()) + small[l, 2:3, :]
        middle, unit, scale = norm_forward(first, small[l, 4:5, :], small[l, 6:7, :])
        unit1[...], scale1[...] = unit, scale
        mid_low = middle.astype(BF16)
        mid_ref[...] = mid_low
        run(up, "g3")
        run(down, "g2")
        for j in range(4):
            at = j * 512
            weight = up[j // 2].full[:, :, :, :, (j % 2) * 512 : (j % 2) * 512 + 512].reshape(D, 512)
            upper = nn(mid_low, weight) + small_up[l, :, at : at + 512]
            phi = 0.5 + 0.5 * lax.erf(upper * (0.5**0.5))
            act_ref[:, at : at + 512] = (upper * phi).astype(BF16)
            density = jnp.exp(-0.5 * upper * upper) * 0.3989422804014327
            slope_ref[:, at : at + 512] = phi + upper * density
        run(down, "g3")
        second = jnp.concatenate([nn(act_ref[...], part.value()) for part in down], axis=1)
        second = middle + second + small[l, 3:4, :]
        hidden, unit, scale = norm_forward(second, small[l, 5:6, :], small[l, 7:8, :])
        unit2[...], scale2[...] = unit, scale
        if l + 1 < LAYERS:
            run(parts[l + 1][:3], "g2")
            run(along(parts[l + 1][3:], "x"), "g1")
            run(parts[l + 1][:3], "g3")
    out_ref[...] = hidden.astype(BF16)
    out_copy = pltpu.make_async_copy(out_ref, out_hbm, out_sems.at[0])
    out_copy.start()

    grad = cot_ref[...].astype(F32)
    for l in reversed(range(LAYERS)):
        qkv, proj, up, down = parts[l][:3], parts[l][3], parts[l][4:6], parts[l][6:8]
        above = parts[l + 1] if l + 1 < LAYERS else []
        to_heads, to_tokens, d_to_heads, d_to_tokens = swap[l]
        source_ref, unit1, scale1, unit2, scale2, mid_ref, act_ref, slope_ref = saved[l]
        grad_two, d_small[l, 5:6, :], d_small[l, 7:8, :] = norm_backward(
            grad, unit2[...], scale2[...], small[l, 5:6, :]
        )
        low_two = grad_two.astype(BF16)
        d_small[l, 3:4, :] = column_sum(low_two.astype(F32))
        d_uppers = []
        for j in range(4):
            at = j * 512
            d_act = 0.0
            for i in range(2):
                weight = down[i].full[j // 2, (j % 2) * 2 : (j % 2) * 2 + 2].reshape(512, 256)
                d_act = d_act + nt(low_two[:, i * 256 : (i + 1) * 256], weight)
            d_upper = (d_act * slope_ref[:, at : at + 512]).astype(BF16)
            d_small_up[l, :, at : at + 512] = column_sum(d_upper.astype(F32))
            d_uppers.append(d_upper)
        d_upper = jnp.concatenate(d_uppers, axis=1)
        grad_mid = grad_two
        for i in range(2):
            grad_mid = grad_mid + nt(d_upper[:, i * 1024 : (i + 1) * 1024], up[i].value())
        grad_one, d_small[l, 4:5, :], d_small[l, 6:7, :] = norm_backward(
            grad_mid, unit1[...], scale1[...], small[l, 4:5, :]
        )
        low_one = grad_one.astype(BF16)
        d_small[l, 2:3, :] = column_sum(low_one.astype(F32))
        d_context = nt(low_one, proj.value()).astype(BF16)
        split_context(d_context, d_to_heads.out)
        d_to_heads.start()
        run(down + up + [proj], "sent")

        def down_grad(i):
            for j in range(8):
                block = tn(act_ref[:, j * 256 : (j + 1) * 256], low_two[:, i * 256 : (i + 1) * 256])
                down[i].store(j * 256, block)
            down[i].e0()

        def up_grad(i):
            for j in range(2):
                block = tn(mid_ref[:, j * 256 : (j + 1) * 256], d_upper[:, i * 1024 : (i + 1) * 1024])
                up[i].store(j * 256, block)
            up[i].e0()

        down_grad(0)
        up_grad(0)
        run(above[:3], "e1")
        context = join_context(to_tokens.into)
        for j in range(2):
            proj.store(j * 256, tn(context[:, j * 256 : (j + 1) * 256], low_one))
        proj.e0()
        run(above[3:], "e2")
        run(first_along(down + up + [proj], "x"), "e1")
        d_to_heads.wait()
        queries, keys, values = head_parts(to_heads.into[...])
        query_ref[...] = queries.reshape(NQ, QB, HD)
        dc_ref[...] = one_above_other(d_to_heads.into[...]).reshape(NQ, QB, HD)
        keys_t = keys.T
        dk_ref[...] = jnp.zeros_like(dk_ref)
        dv_ref[...] = jnp.zeros_like(dv_ref)

        def attend_back(i, carry):
            d_ctx = dc_ref[i]
            d_prob = nt(values, d_ctx)
            prob = probs[l][i].astype(F32) * shares[l, i]
            row = jnp.sum(prob * d_prob, axis=0, keepdims=True)
            d_score = (prob * (d_prob - row)).astype(BF16)
            dv_ref[...] += nn(prob.astype(BF16), d_ctx)
            dk_ref[...] += nn(d_score, query_ref[i])
            dq_ref[i] = (nn(keys_t, d_score) * 0.125).T.astype(BF16)
            return carry

        lax.fori_loop(0, NQ, attend_back, 0)
        both = jnp.concatenate([dq_ref[...].reshape(LENGTH, HD), dk_ref[...].astype(BF16)], axis=1)
        d_to_tokens.out[:, 0:ROWS, :] = both.reshape(GROUP, ROWS, 2 * HD)
        d_to_tokens.out[:, ROWS:96, :] = side_by_side(dv_ref[...].astype(BF16).reshape(GROUP, ROWS, HD))
        d_to_tokens.start()
        down_grad(1)
        up_grad(1)
        run(above[:3], "e2")
        run(first_along(down + up + [proj], "yz"), "e1")
        run(qkv, "sent")
        run(first_along(above[3:], "x"), "e3")
        d_to_tokens.wait()
        d_joined = join_heads(d_to_tokens.into)
        d_small[l, 1:2, :] = column_sum(d_joined[:, 2 * D :].astype(F32))
        grad = grad_one
        source = source_ref[...]
        if l == 0:
            for i in range(3):
                qkv[i].store(0, tn(source, d_joined[:, i * D : (i + 1) * D]))
                qkv[i].e0()
        for i in range(3):
            grad = grad + nt(d_joined[:, i * D : (i + 1) * D], qkv[i].value())
        if l > 0:
            for i in range(3):
                qkv[i].store(0, tn(source, d_joined[:, i * D : (i + 1) * D]))
                qkv[i].e0()
    dx_ref[...] = grad
    dx_copy = pltpu.make_async_copy(dx_ref, dx_hbm, out_sems.at[1])
    dx_copy.start()
    qkv, rest, above = parts[0][:3], parts[0][3:], parts[1]
    run(qkv, "e1")

    small_grad[...] = jnp.zeros_like(small_grad)
    for l in range(LAYERS):
        for t in range(GROUP):
            small_grad[t, l * 8 + 1 : l * 8 + 8, 0:32] = d_small[l, 1:8, t * 32 : (t + 1) * 32]
            small_grad[t, l * 8 : l * 8 + 1, :] = d_small_up[l, :, t * 128 : (t + 1) * 128]
    for to in p.group():
        remote(small_grad.at[to], small_in.at[me], small_sems.at[2], small_sems.at[3], (p.rep, to))
    small_in[me] = small_grad[me]
    run(first_along(rest, "x"), "e2")
    run(first_along(above[3:], "yz") + above[:3], "e3")
    run(first_along(rest, "yz"), "e2")
    run(qkv, "e2")
    run(rest, "e3")
    wait_bytes(small_in.at[pl.ds(0, GROUP - 1)], small_sems.at[3])
    total = small_in[0]
    for t in range(1, GROUP):
        total = total + small_in[t]
    slot = small_rep.at[p.rep]
    slot[...] = total
    nrep = nx * nzl
    for d in range(1, nrep):
        remote(slot, slot, small_sems.at[4], small_sems.at[5], (lax.rem(p.rep + d, nrep), me))
    run(above, "e4")
    run(qkv, "e3")
    run(rest, "e4")
    if nrep > 1:
        wait_bytes(small_rep.at[pl.ds(0, nrep - 1)], small_sems.at[5])
    total = small_rep[0]
    for t in range(1, nrep):
        total = total + small_rep[t]
    for l in range(LAYERS):
        at = l * 8
        upb_out[l : l + 1, :] = total[at : at + 1, :]
        bias_out[l] = total[at + 1 : at + 4, 0:32]
        gain_out[l] = total[at + 4 : at + 6, 0:32]
        shift_out[l] = total[at + 6 : at + 8, 0:32]
    run(qkv, "e4")

    run(everything, "reduced")
    for l in range(LAYERS):
        for one in swap[l]:
            one.finish()
    wait_bytes(small_all.at[pl.ds(0, GROUP - 1)], small_sems.at[0])
    wait_bytes(small_grad.at[pl.ds(0, GROUP - 1)], small_sems.at[2])
    if nrep > 1:
        wait_bytes(small_rep.at[pl.ds(0, nrep - 1)], small_sems.at[4])
    out_copy.wait()
    dx_copy.wait()


def scratch(nx, nzl, members):
    sizes = {"x": nx, "y": Y, "z": ZH * nzl}
    nrep = nx * nzl
    shapes = [pltpu.VMEM((TOK, D), BF16), pltpu.VMEM((TOK, D), F32)]
    shapes += [pltpu.VMEM(member.shape, F32) for member in members[:4]]
    for _ in range(LAYERS):
        for _, _, r, c, _, _ in PARTS:
            shapes.append(pltpu.VMEM((ZH, Y, CORES, r, c), BF16))
    for _, _, r, c, _, _ in PARTS[:3]:
        shapes.append(pltpu.VMEM((ZH, Y, CORES, r, c), BF16))
    for l in range(LAYERS):
        for _, _, r, c, _, near in PARTS:
            piece = (r // nrep, c) if r == 128 else (r // nzl, c // nx)
            na, nb, nc = [sizes[axis] for axis in {"x": "xyz", "y": "yxz", "z": "zxy"}[near[l]]]
            shapes.append(pltpu.VMEM((ZH, Y, r, c), BF16))
            shapes.append(pltpu.VMEM((na, nb, nc) + piece, BF16))
            shapes.append(pltpu.VMEM((max(na - 1, 1), nb, nc) + piece, BF16))
            shapes.append(pltpu.VMEM((nb, nc) + piece, BF16))
            shapes.append(pltpu.VMEM((nb * nc - 1,) + piece, BF16))
            shapes.append(pltpu.VMEM((nrep,) + piece, BF16))
    for _ in range(LAYERS):
        for rows in (96, 32, 32, 96):
            shapes += [pltpu.VMEM((GROUP, rows, 128), BF16)] * 2
    shapes += [pltpu.VMEM((16, 128), F32)]
    shapes += [pltpu.VMEM((GROUP, 16, 128), F32)] * 3
    shapes += [pltpu.VMEM((nrep, 16, 128), F32)]
    shapes += [pltpu.VMEM((LAYERS, 8, D), F32), pltpu.VMEM((LAYERS, 1, FF), F32)] * 2
    for _ in range(LAYERS):
        shapes += [
            pltpu.VMEM((TOK, D), BF16),
            pltpu.VMEM((TOK, D), F32),
            pltpu.VMEM((TOK, 1), F32),
            pltpu.VMEM((TOK, D), F32),
            pltpu.VMEM((TOK, 1), F32),
            pltpu.VMEM((TOK, D), BF16),
            pltpu.VMEM((TOK, FF), BF16),
            pltpu.VMEM((TOK, FF), F32),
        ]
    shapes += [pltpu.VMEM((NQ, LENGTH, QB), BF16)] * LAYERS
    shapes += [pltpu.VMEM((LAYERS, NQ, 1, QB), F32)]
    shapes += [pltpu.VMEM((NQ, QB, HD), BF16)] * 3
    shapes += [pltpu.VMEM((LENGTH, HD), F32)] * 2
    shapes += [
        pltpu.SemaphoreType.DMA((LAYERS * len(PARTS), SEMS)),
        pltpu.SemaphoreType.DMA((LAYERS * 4, 2)),
        pltpu.SemaphoreType.DMA((6,)),
        pltpu.SemaphoreType.DMA((2,)),
    ]
    return shapes


def copy_kernel(*refs):
    n = 10
    source, target, held, sems = refs[:n], refs[n : 2 * n], refs[2 * n : 3 * n], refs[-1]
    into = [pltpu.make_async_copy(source[i], held[i], sems.at[0, i]) for i in range(n)]
    outof = [pltpu.make_async_copy(held[i], target[i], sems.at[1, i]) for i in range(n)]
    for copy in into:
        copy.start()
    for i in range(n):
        into[i].wait()
        outof[i].start()
    for copy in outof:
        copy.wait()


def local_call(nx, nzl, inputs, *arguments):
    cotangent, members = arguments[-1], arguments[:-1]
    shapes = [jax.ShapeDtypeStruct((TOK, D), BF16), jax.ShapeDtypeStruct((TOK, D), F32)]
    shapes += [jax.ShapeDtypeStruct(member.shape, F32) for member in members]
    anywhere, vmem = pl.BlockSpec(memory_space=pl.ANY), pl.BlockSpec(memory_space=pltpu.VMEM)
    got = pl.pallas_call(
        functools.partial(kernel, nx, nzl),
        out_shape=shapes,
        in_specs=[vmem] * 10,
        out_specs=[anywhere] * 6 + [vmem] * 4,
        scratch_shapes=scratch(nx, nzl, members),
        compiler_params=pltpu.CompilerParams(
            collective_id=0, has_side_effects=True, vmem_limit_bytes=63 * 1024 * 1024
        ),
        cost_estimate=pl.CostEstimate(flops=7 * 10**9, bytes_accessed=8 * 10**6, transcendentals=5 * 10**6),
    )(inputs.reshape(TOK, D), cotangent.reshape(TOK, D), *members)
    return pl.pallas_call(
        copy_kernel,
        out_shape=shapes,
        in_specs=[anywhere] * 10,
        out_specs=[anywhere] * 10,
        scratch_shapes=[pltpu.VMEM(shape.shape, shape.dtype) for shape in shapes] + [pltpu.SemaphoreType.DMA((2, 10))],
    )(*got)


def solution(mesh):
    nrep = mesh.shape["rep"]
    nzl = 2 if nrep >= 2 else 1
    nx = nrep // nzl

    def shards(inputs, *arguments):
        got = local_call(nx, nzl, inputs, *arguments)
        return (got[0].reshape(inputs.shape), got[1].reshape(inputs.shape), *got[2:])

    rows, columns = P(None, "shard", None), P(None, None, "shard")
    both = P("rep", "shard", None)
    weights = (rows, rows, rows, rows, columns, columns, columns, P(None, "shard"))
    return jax.shard_map(
        shards,
        mesh=mesh,
        in_specs=(both, *weights, both),
        out_specs=(both, both, *weights),
        check_vma=False,
    )
```

```python
import functools

import jax
import jax.numpy as jnp
from jax import lax
from jax.experimental import pallas as pl
from jax.experimental.pallas import tpu as pltpu
from jax.sharding import PartitionSpec as P

MESH = pl.DeviceIdType.MESH
F32 = jnp.float32
BF16 = jnp.bfloat16
H, HD, D, FF, LAYERS = 8, 64, 512, 2048, 2
ZH, Y, CORES = 2, 4, 2
GROUP = ZH * Y * CORES
ROWS = 64
TOK = 2 * ROWS
LENGTH = GROUP * ROWS
QB = 512
NQ = LENGTH // QB
UNROLL = NQ // ZH
QKV, PROJ, UP, DOWN = range(4)
PARTS = (
    (QKV, 0, 32, 512, "xx", "xx"),
    (QKV, 512, 32, 512, "zz", "zz"),
    (QKV, 1024, 32, 512, "yy", "yy"),
    (PROJ, 0, 32, 512, "xx", "xx"),
    (UP, 0, 32, 1024, "xx", "xx"),
    (UP, 1024, 32, 1024, "zz", "zz"),
    (DOWN, 0, 128, 256, "xx", "xx"),
    (DOWN, 256, 128, 256, "yy", "yy"),
)
SEMS = 17
AXES = {"x": "xyz", "y": "yxz", "z": "zxy"}


def piece_shape(rows, cols, nx, nzl):
    return (rows // (nx * nzl), cols) if rows == 128 else (rows // nzl, cols // nx)


def bundles(nx, nzl):
    if nx * nzl == 8:
        return ((0,), (1,), (2,), (3, 4, 6), (5,), (7,))
    return tuple((i,) for i in (0, 1, 2, 3, 4, 6, 5, 7))


def nn(a, b):
    return jnp.dot(a, b, preferred_element_type=F32)


def nt(a, b):
    return lax.dot_general(a, b, (((1,), (1,)), ((), ())), preferred_element_type=F32)


def tn(a, b):
    return lax.dot_general(a, b, (((0,), (0,)), ((), ())), preferred_element_type=F32)


def norm_forward(values, gain, shift):
    center = values - jnp.mean(values, axis=-1, keepdims=True)
    spread = jnp.mean(center * center, axis=-1, keepdims=True)
    scale = lax.rsqrt(spread + 1e-06)
    unit = center * scale
    return unit * gain + shift, unit, scale


def norm_backward(grad, unit, scale, gain):
    d_unit = grad * gain
    first = jnp.mean(d_unit, axis=-1, keepdims=True)
    second = jnp.mean(d_unit * unit, axis=-1, keepdims=True)
    d_gain = jnp.sum(grad * unit, axis=0, keepdims=True)
    d_shift = jnp.sum(grad, axis=0, keepdims=True)
    return scale * (d_unit - first - unit * second), d_gain, d_shift


def column_sum(values):
    return jnp.sum(values, axis=0, keepdims=True)


def wait_bytes(ref, sem):
    pltpu.make_async_copy(ref, ref, sem).wait()


class Place:
    def __init__(self, nx, nzl):
        self.nx, self.nzl, self.nz = nx, nzl, ZH * nzl
        rep, shard = lax.axis_index("rep"), lax.axis_index("shard")
        self.rep, self.shard = rep, shard
        self.zl, self.x = lax.div(rep, nx), lax.rem(rep, nx)
        self.zh, self.y = lax.div(shard, Y * CORES), lax.rem(lax.div(shard, CORES), Y)
        self.core = lax.rem(shard, CORES)
        self.z = self.zh * nzl + self.zl

    def at(self, x=None, y=None, z=None, core=None):
        x = self.x if x is None else x
        y = self.y if y is None else y
        z = self.z if z is None else z
        core = self.core if core is None else core
        zh, zl = lax.div(z, self.nzl), lax.rem(z, self.nzl)
        return (zl * self.nx + x, zh * (Y * CORES) + y * CORES + core)

    def xs(self, d):
        return lax.rem(self.x + d, self.nx)

    def ys(self, d):
        return lax.rem(self.y + d, Y)

    def zs(self, d):
        return lax.rem(self.z + d, self.nz)

    def group(self):
        steps = [(dy, dz, dc) for dy in (2, 1, 3, 0) for dz in (1, 0) for dc in range(CORES) if dy or dz or dc]
        steps.sort(key=lambda step: -(2 * min(step[0], 1) + 2 * step[1] + step[2]))
        found = []
        for dy, dz, dc in steps:
            z = lax.rem(self.z + dz * self.nzl, self.nz)
            found.append(self.at(y=self.ys(dy), z=z, core=lax.rem(self.core + dc, CORES))[1])
        return found

    def peers(self):
        found = []
        for dy in range(Y):
            for dz in range(self.nz):
                if dy or dz:
                    found.append(self.at(y=self.ys(dy), z=self.zs(dz)))
        for dx in range(1, self.nx):
            for dz in range(self.nz):
                found.append(self.at(x=self.xs(dx), z=self.zs(dz)))
        for dx in range(1, self.nx):
            for dy in range(1, Y):
                found.append(self.at(x=self.xs(dx), y=self.ys(dy)))
        for dy in range(Y):
            for zh in range(ZH):
                z = lax.rem(self.z + zh * self.nzl, self.nz)
                found.append(self.at(y=self.ys(dy), z=z, core=1 - self.core))
        return found


def remote(src, dst, send_sem, recv_sem, device):
    pltpu.make_async_remote_copy(
        src_ref=src, dst_ref=dst, send_sem=send_sem, recv_sem=recv_sem, device_id=device, device_id_type=MESH
    ).start()


class Exchange:
    def __init__(self, place, out, into, sems):
        self.place, self.out, self.into, self.sems = place, out, into, sems

    def start(self):
        me = self.place.shard
        for to in self.place.group():
            remote(self.out.at[to], self.into.at[me], self.sems.at[0], self.sems.at[1], (self.place.rep, to))
        self.into[me] = self.out[me]

    def send(self, first, blocks):
        me = self.place.shard
        for j in range(blocks.shape[0]):
            self.out[first + j] = blocks[j]
        for j in range(blocks.shape[0]):
            to = first + j

            @pl.when(to != me)
            def _():
                remote(self.out.at[to], self.into.at[me], self.sems.at[0], self.sems.at[1], (self.place.rep, to))

            @pl.when(to == me)
            def _():
                self.into[me] = self.out[me]

    def wait(self):
        wait_bytes(self.into.at[pl.ds(0, GROUP - 1)], self.sems.at[1])

    def finish(self):
        wait_bytes(self.out.at[pl.ds(0, GROUP - 1)], self.sems.at[0])


class Part:
    def __init__(self, place, own, full, grad, sems, pair, far, near, result, out):
        self.place, self.own, self.full, self.grad, self.sems = place, own, full, grad, sems
        self.pair, self.far, self.near, self.result, self.out = pair, far, near, result, out
        self.rows, self.cols = own.shape

    def sem(self, i):
        return self.sems.at[i]

    def sibling(self):
        return self.place.at(core=1 - self.place.core)

    def across(self):
        return self.place.nz - 1 - self.place.z

    def keep(self):
        p = self.place
        self.full[p.zh, p.y, p.core] = self.own[...]

    def quarter(self, ref, x):
        nx = self.place.nx
        if self.rows == 128:
            n = self.rows // nx
            return ref.at[..., pl.ds(pl.multiple_of(x * n, n), n), :]
        n = self.cols // nx
        return ref.at[..., pl.ds(pl.multiple_of(x * n, n), n)]

    def g0(self):
        p = self.place
        slot = self.full.at[p.zh, p.y, p.core]
        if self.far == "x":
            src, dst = self.quarter(self.own, p.x), self.quarter(slot, p.x)
            for d in (2, 1, 3, 0):
                remote(src, dst, self.sem(4), self.sem(1), p.at(y=p.ys(d), z=self.across()))
            for d in (2, 1, 3):
                remote(src, dst, self.sem(3), self.sem(0), p.at(y=p.ys(d)))
        else:
            if self.far == "y":
                remote(self.own, slot, self.sem(3), self.sem(0), p.at(z=self.across()))
            for d in (2, 1, 3):
                remote(self.own, slot, self.sem(4), self.sem(1), p.at(y=p.ys(d)))

    def g1(self):
        p, full = self.place, self.full
        if self.far == "x":
            wait_bytes(self.quarter(full.at[0, pl.ds(0, 3), 0], 0), self.sem(0))
            wait_bytes(self.quarter(full.at[0, :, 0], 0), self.sem(1))
            mine = self.quarter(full.at[:, :, p.core], p.x)
            for d in order_of(p.nx):
                remote(mine, mine, self.sem(5), self.sem(2), p.at(x=p.xs(d)))
        elif self.far == "y":
            wait_bytes(full.at[0, 0, 0], self.sem(0))
            slot = full.at[1 - p.zh, p.y, p.core]
            for d in (2, 1, 3):
                remote(slot, slot, self.sem(5), self.sem(2), p.at(y=p.ys(d)))
        else:
            wait_bytes(full.at[0, pl.ds(0, 3), 0], self.sem(1))
            half = full.at[p.zh, :, p.core]
            remote(half, half, self.sem(5), self.sem(2), p.at(z=self.across()))

    def g2(self):
        p, full = self.place, self.full
        if self.far == "x":
            if p.nx > 1:
                wait_bytes(full.at[:, pl.ds(0, p.nx - 1), 0], self.sem(2))
        elif self.far == "y":
            wait_bytes(full.at[0, pl.ds(0, 3), 0], self.sem(1))
            wait_bytes(full.at[0, pl.ds(0, 3), 0], self.sem(2))
        else:
            wait_bytes(full.at[0, :, 0], self.sem(2))
        both = full.at[:, :, p.core]
        remote(both, both, self.sem(6), self.sem(7), self.sibling())

    def g3(self):
        wait_bytes(self.full.at[:, :, 0], self.sem(7))

    def sent(self):
        full, nx = self.full, self.place.nx
        if self.far == "x":
            wait_bytes(self.quarter(full.at[0, pl.ds(0, 3), 0], 0), self.sem(3))
            wait_bytes(self.quarter(full.at[0, :, 0], 0), self.sem(4))
            if nx > 1:
                wait_bytes(full.at[:, pl.ds(0, nx - 1), 0], self.sem(5))
        elif self.far == "y":
            wait_bytes(full.at[0, 0, 0], self.sem(3))
            wait_bytes(full.at[0, pl.ds(0, 3), 0], self.sem(4))
            wait_bytes(full.at[0, pl.ds(0, 3), 0], self.sem(5))
        else:
            wait_bytes(full.at[0, pl.ds(0, 3), 0], self.sem(4))
            wait_bytes(full.at[0, :, 0], self.sem(5))
        wait_bytes(full.at[:, :, 0], self.sem(6))

    def value(self):
        return self.full[...].reshape(GROUP * self.rows, self.cols)

    def store(self, start, block):
        count = block.shape[0]
        per_y = CORES * self.rows
        block = block.astype(BF16)
        if count == ZH * Y * per_y:
            self.grad[...] = block.reshape(ZH, Y, CORES, self.rows, self.cols)
        elif count == Y * per_y:
            self.grad[start // count] = block.reshape(Y, CORES, self.rows, self.cols)
        else:
            n = count // per_y
            zh, y = divmod(start // per_y, Y)
            self.grad[zh, y : y + n] = block.reshape(n, CORES, self.rows, self.cols)

    def piece(self, zl, x):
        p = self.place
        if self.rows == 128:
            n = self.rows // (p.nx * p.nzl)
            at = (zl * p.nx + x) * n
            return slice(at, at + n), slice(None)
        half, part = self.rows // p.nzl, self.cols // p.nx
        return slice(zl * half, (zl + 1) * half), slice(x * part, (x + 1) * part)

    def e0(self):
        p = self.place
        remote(self.grad.at[:, :, 1 - p.core], self.pair, self.sem(8), self.sem(9), self.sibling())


class Sum:
    def __init__(self, place, parts, buffers):
        self.place, self.parts, self.sems = place, parts, parts[0].sems
        self.chip, self.recv1, self.sum1, self.recv2, self.recv3 = buffers
        p = place
        self.n = {"x": p.nx, "y": Y, "z": p.nz}
        self.me = {"x": p.x, "y": p.y, "z": p.z}
        self.axes = AXES[parts[0].near]

    def sem(self, i):
        return self.sems.at[i]

    def columns(self):
        at = 0
        for part in self.parts:
            rows, cols = piece_shape(part.rows, part.cols, self.place.nx, self.place.nzl)
            yield part, slice(at, at + cols)
            at += cols

    def e1(self):
        p = self.place
        for part, here in self.columns():
            wait_bytes(part.pair, part.sem(9))
            for zh in range(ZH):
                for y in range(Y):
                    total = part.grad[zh, y, p.core].astype(F32) + part.pair[zh, y].astype(F32)
                    total = total.astype(BF16)
                    for x in range(p.nx):
                        for zl in range(p.nzl):
                            at = {"x": x, "y": y, "z": zh * p.nzl + zl}
                            rows, cols = part.piece(zl, x)
                            a, b, c = [at[axis] for axis in self.axes]
                            self.chip[a, b, c, :, here] = total[rows, cols]
        a = self.axes[0]
        for d in order_of(self.n[a]):
            to = lax.rem(self.me[a] + d, self.n[a])
            remote(self.chip.at[to], self.recv1.at[d - 1], self.sem(10), self.sem(11), p.at(**{a: to}))

    def e2(self):
        p = self.place
        a, b, c = self.axes
        nb, nc = self.n[b], self.n[c]
        if self.n[a] > 1:
            wait_bytes(self.recv1, self.sem(11))
        for ib in range(nb):
            total = self.chip[self.me[a], ib].astype(F32)
            for d in range(self.n[a] - 1):
                total = total + self.recv1[d, ib].astype(F32)
            self.sum1[ib] = total.astype(BF16)
        pairs = [(db, dc) for db in range(nb) for dc in range(nc) if db or dc]
        for db, dc in sorted(pairs, key=lambda at: -(min(at[0], 1) + min(at[1], 1))):
            to_b, to_c = lax.rem(self.me[b] + db, nb), lax.rem(self.me[c] + dc, nc)
            remote(
                self.sum1.at[to_b, to_c],
                self.recv2.at[db * nc + dc - 1],
                self.sem(12),
                self.sem(13),
                p.at(**{b: to_b, c: to_c}),
            )

    def e3(self):
        p = self.place
        _, b, c = self.axes
        wait_bytes(self.recv2, self.sem(13))
        total = self.sum1[self.me[b], self.me[c]].astype(F32)
        for i in range(self.recv2.shape[0]):
            total = total + self.recv2[i].astype(F32)
        slot = self.recv3.at[p.rep]
        slot[...] = total.astype(BF16)
        nrep = p.nx * p.nzl
        for d in range(1, nrep):
            remote(slot, slot, self.sem(14), self.sem(15), (lax.rem(p.rep + d, nrep), p.shard))

    def e4(self):
        p = self.place
        nrep = p.nx * p.nzl
        if nrep > 1:
            wait_bytes(self.recv3.at[pl.ds(0, nrep - 1)], self.sem(15))
        for part, here in self.columns():
            for zl in range(p.nzl):
                for x in range(p.nx):
                    rows, cols = part.piece(zl, x)
                    part.result[rows, cols] = self.recv3[zl * p.nx + x, :, here].astype(F32)
            pltpu.make_async_copy(part.result, part.out, part.sem(16)).start()

    def reduced(self):
        p = self.place
        for part in self.parts:
            wait_bytes(part.pair, part.sem(8))
            pltpu.make_async_copy(part.result, part.out, part.sem(16)).wait()
        if self.n[self.axes[0]] > 1:
            wait_bytes(self.recv1, self.sem(10))
        wait_bytes(self.recv2, self.sem(12))
        if p.nx * p.nzl > 1:
            wait_bytes(self.recv3.at[pl.ds(0, p.nx * p.nzl - 1)], self.sem(14))


def order_of(n):
    return (2, 1, 3) if n == 4 else tuple(range(1, n))


def side_by_side(block):
    n = block.shape[-2] // 2
    return jnp.concatenate([block[..., :n, :], block[..., n:, :]], axis=-1)


def one_above_other(block):
    return jnp.concatenate([block[..., :HD], block[..., HD:]], axis=-2)


def split_heads(joined, slots):
    for s in range(2):
        rows = joined[s * ROWS : (s + 1) * ROWS]
        for h in range(H):
            at = h * HD
            query, key = rows[:, at : at + HD], rows[:, D + at : D + at + HD]
            slots[s * H + h, 0:ROWS] = jnp.concatenate([query, key], axis=1)
            slots[s * H + h, ROWS:96] = side_by_side(rows[:, 2 * D + at : 2 * D + at + HD])


def split_context(context, slots):
    for s in range(2):
        rows = context[s * ROWS : (s + 1) * ROWS]
        for h in range(H):
            slots[s * H + h] = side_by_side(rows[:, h * HD : (h + 1) * HD])


def join_context(slots):
    parts = []
    for s in range(2):
        heads = [one_above_other(slots[s * H + h]) for h in range(H)]
        parts.append(jnp.concatenate(heads, axis=1))
    return jnp.concatenate(parts, axis=0)


def join_heads(slots):
    parts = []
    for s in range(2):
        both = [slots[s * H + h] for h in range(H)]
        queries = [block[0:ROWS, :HD] for block in both]
        keys = [block[0:ROWS, HD:] for block in both]
        values = [one_above_other(block[ROWS:96]) for block in both]
        parts.append(jnp.concatenate(queries + keys + values, axis=1))
    return jnp.concatenate(parts, axis=0)


def head_parts(slots):
    both = slots[:, 0:ROWS, :].reshape(LENGTH, 2 * HD)
    values = one_above_other(slots[:, ROWS:96, :]).reshape(LENGTH, HD)
    queries = (both[:, :HD].astype(F32) * 0.125).astype(BF16)
    return queries, both[:, HD:], values


def kernel(nx, nzl, *refs):
    refs = list(refs)

    def take(n):
        got = refs[:n]
        del refs[:n]
        return got

    x_ref, cot_ref = take(2)
    own = take(4)
    bias_ref, gain_ref, shift_ref, upb_ref = take(4)
    out_hbm, dx_hbm = take(2)
    result_hbm = take(4)
    bias_out, gain_out, shift_out, upb_out = take(4)
    out_ref, dx_ref = take(2)
    results = take(4)
    full = [take(len(PARTS)) for _ in range(LAYERS)]
    last_grads = take(3)
    pairs = [take(len(PARTS)) for _ in range(LAYERS)]
    buffers = [[take(5) for _ in bundles(nx, nzl)] for _ in range(LAYERS)]
    swaps = [take(8) for _ in range(LAYERS)]
    small_own, small_all, small_grad, small_in, small_rep = take(5)
    small, small_up, d_small, d_small_up = take(4)
    saved = [take(8) for _ in range(LAYERS)]
    probs = take(LAYERS)
    (shares,) = take(1)
    query_ref, dc_ref, dq_ref, dk_ref, dv_ref = take(5)
    part_sems, swap_sems, small_sems, out_sems = take(4)

    p = Place(nx, nzl)
    parts = []
    for l in range(LAYERS):
        row = []
        for i, (w, at, _, cols, far, near) in enumerate(PARTS):
            here = pl.ds(at, cols)
            row.append(
                Part(
                    p,
                    own[w].at[l, :, here],
                    full[l][i],
                    last_grads[i] if l == 0 and i < 3 else full[l][i],
                    part_sems.at[l * len(PARTS) + i],
                    pairs[l][i],
                    far[l],
                    near[l],
                    results[w].at[l, :, here],
                    result_hbm[w].at[l, :, here],
                )
            )
        parts.append(row)
    swap = [
        [Exchange(p, swaps[l][2 * i], swaps[l][2 * i + 1], swap_sems.at[l * 4 + i]) for i in range(4)]
        for l in range(LAYERS)
    ]
    everything = [part for row in parts for part in row]
    sums = [
        [Sum(p, [parts[l][i] for i in which], buffers[l][k]) for k, which in enumerate(bundles(nx, nzl))]
        for l in range(LAYERS)
    ]

    for part in everything:
        part.keep()
    small_own[...] = jnp.zeros_like(small_own)
    for l in range(LAYERS):
        at = l * 8
        small_own[at : at + 1, :] = upb_ref[l : l + 1, :].astype(F32)
        small_own[at + 1 : at + 4, 0:32] = bias_ref[l].astype(F32)
        small_own[at + 4 : at + 6, 0:32] = gain_ref[l].astype(F32)
        small_own[at + 6 : at + 8, 0:32] = shift_ref[l].astype(F32)
    small_all[p.shard] = small_own[...]
    barrier = pltpu.get_barrier_semaphore()
    peers = p.peers()
    for peer in peers:
        pl.semaphore_signal(barrier, inc=1, device_id=peer, device_id_type=MESH)
    pl.semaphore_wait(barrier, len(peers))

    me = p.shard

    def along(which, axes):
        return [part for part in which if part.far in axes]

    def first_along(which, axes):
        return [one for one in which if one.parts[0].near in axes]

    def run(which, *steps):
        for step in steps:
            for part in which:
                getattr(part, step)()

    early, late = parts[0][:3], parts[0][3:]
    run(early, "g0")
    run(early, "g1")
    for to in p.group():
        remote(small_own, small_all.at[me], small_sems.at[0], small_sems.at[1], (p.rep, to))
    run(along(late, "x"), "g0")
    run(along(late, "yz"), "g0")
    run(early, "g2")
    wait_bytes(small_all.at[pl.ds(0, GROUP - 1)], small_sems.at[1])
    for l in range(LAYERS):
        for q in range(4):
            part = [small_all[4 * q + i, l * 8 : l * 8 + 8, 0:32] for i in range(4)]
            small[l, :, q * 128 : (q + 1) * 128] = jnp.concatenate(part, axis=1)
        for t in range(GROUP):
            small_up[l, :, t * 128 : (t + 1) * 128] = small_all[t, l * 8 : l * 8 + 1, :]
    run(early, "g3")

    hidden = x_ref[...].astype(F32)
    for l in range(LAYERS):
        proj, up, down = parts[l][3], parts[l][4:6], parts[l][6:8]
        to_heads, to_tokens, _, _ = swap[l]
        source_ref, unit1, scale1, unit2, scale2, mid_ref, act_ref, slope_ref = saved[l]
        source = hidden.astype(BF16)
        source_ref[...] = source
        joined = [nn(source, part.value()) for part in parts[l][:3]]
        joined[2] = joined[2] + small[l, 1:2, :]
        split_heads(jnp.concatenate(joined, axis=1).astype(BF16), to_heads.out)
        to_heads.start()
        run(along(late, "x") if l == 0 else down[:1], "g1")
        run(up[1:] + down[1:], "g1")
        if l + 1 < LAYERS:
            run(parts[l + 1][:3], "g0")
        run([proj], "g2")
        to_heads.wait()
        queries, keys, values = head_parts(to_heads.into[...])
        query_ref[...] = queries.reshape(NQ, QB, HD)
        values_t = values.T

        def attend(i):
            scores = nt(keys, query_ref[i])
            expo = jnp.exp(scores - jnp.max(scores, axis=0, keepdims=True))
            part = 1.0 / jnp.sum(expo, axis=0, keepdims=True)
            low = expo.astype(BF16)
            probs[l][i] = low
            shares[l, i] = part
            block = (nn(values_t, low) * part).T.astype(BF16).reshape(QB // ROWS, ROWS, HD)
            return side_by_side(block)

        def attend_half(i, carry):
            first = lax.rem(i + 1 - p.zh, ZH) * UNROLL
            blocks = [attend(first + j) for j in range(UNROLL)]
            to_tokens.send(first * (QB // ROWS), jnp.concatenate(blocks, axis=0))
            return carry

        for half in range(ZH):
            attend_half(half, 0)
        if l + 1 < LAYERS:
            run(parts[l + 1][:3], "g1")
            run(parts[l + 1][3:], "g0")
        run([proj], "g3")
        run(up, "g2")
        to_tokens.wait()
        context = join_context(to_tokens.into)
        first = hidden + nn(context, proj.value()) + small[l, 2:3, :]
        middle, unit, scale = norm_forward(first, small[l, 4:5, :], small[l, 6:7, :])
        unit1[...], scale1[...] = unit, scale
        mid_low = middle.astype(BF16)
        mid_ref[...] = mid_low
        run(up, "g3")
        run(down, "g2")
        for j in range(4):
            at = j * 512
            weight = up[j // 2].full[:, :, :, :, (j % 2) * 512 : (j % 2) * 512 + 512].reshape(D, 512)
            upper = nn(mid_low, weight) + small_up[l, :, at : at + 512]
            phi = 0.5 + 0.5 * lax.erf(upper * (0.5**0.5))
            act_ref[:, at : at + 512] = (upper * phi).astype(BF16)
            density = jnp.exp(-0.5 * upper * upper) * 0.3989422804014327
            slope_ref[:, at : at + 512] = phi + upper * density
        run(down, "g3")
        second = jnp.concatenate([nn(act_ref[...], part.value()) for part in down], axis=1)
        second = middle + second + small[l, 3:4, :]
        hidden, unit, scale = norm_forward(second, small[l, 5:6, :], small[l, 7:8, :])
        unit2[...], scale2[...] = unit, scale
        if l + 1 < LAYERS:
            run(parts[l + 1][:3], "g2")
            run(parts[l + 1][3:5], "g1")
            run(parts[l + 1][:3], "g3")
    out_ref[...] = hidden.astype(BF16)
    out_copy = pltpu.make_async_copy(out_ref, out_hbm, out_sems.at[0])
    out_copy.start()

    grad = cot_ref[...].astype(F32)
    for l in reversed(range(LAYERS)):
        qkv, proj, up, down = parts[l][:3], parts[l][3], parts[l][4:6], parts[l][6:8]
        above = sums[l + 1] if l + 1 < LAYERS else []
        to_heads, to_tokens, d_to_heads, d_to_tokens = swap[l]
        source_ref, unit1, scale1, unit2, scale2, mid_ref, act_ref, slope_ref = saved[l]
        grad_two, d_small[l, 5:6, :], d_small[l, 7:8, :] = norm_backward(
            grad, unit2[...], scale2[...], small[l, 5:6, :]
        )
        low_two = grad_two.astype(BF16)
        d_small[l, 3:4, :] = column_sum(low_two.astype(F32))
        d_uppers = []
        for j in range(4):
            at = j * 512
            d_act = 0.0
            for i in range(2):
                weight = down[i].full[j // 2, (j % 2) * 2 : (j % 2) * 2 + 2].reshape(512, 256)
                d_act = d_act + nt(low_two[:, i * 256 : (i + 1) * 256], weight)
            d_upper = (d_act * slope_ref[:, at : at + 512]).astype(BF16)
            d_small_up[l, :, at : at + 512] = column_sum(d_upper.astype(F32))
            d_uppers.append(d_upper)
        d_upper = jnp.concatenate(d_uppers, axis=1)
        grad_mid = grad_two
        for i in range(2):
            grad_mid = grad_mid + nt(d_upper[:, i * 1024 : (i + 1) * 1024], up[i].value())
        grad_one, d_small[l, 4:5, :], d_small[l, 6:7, :] = norm_backward(
            grad_mid, unit1[...], scale1[...], small[l, 4:5, :]
        )
        low_one = grad_one.astype(BF16)
        d_small[l, 2:3, :] = column_sum(low_one.astype(F32))
        d_context = nt(low_one, proj.value()).astype(BF16)
        split_context(d_context, d_to_heads.out)
        d_to_heads.start()
        run(down + up + [proj], "sent")

        def down_grad(i):
            for j in range(8):
                block = tn(act_ref[:, j * 256 : (j + 1) * 256], low_two[:, i * 256 : (i + 1) * 256])
                down[i].store(j * 256, block)
            down[i].e0()

        def up_grad(i):
            for j in range(2):
                block = tn(mid_ref[:, j * 256 : (j + 1) * 256], d_upper[:, i * 1024 : (i + 1) * 1024])
                up[i].store(j * 256, block)
            up[i].e0()

        down_grad(0)
        up_grad(0)
        run(above[:3], "e1")
        if l == 0:
            down_grad(1)
            up_grad(1)
        context = join_context(to_tokens.into)
        for j in range(2):
            proj.store(j * 256, tn(context[:, j * 256 : (j + 1) * 256], low_one))
        proj.e0()
        run(above[3:], "e2")
        run(first_along(sums[l][3:], "x"), "e1")
        d_to_heads.wait()
        queries, keys, values = head_parts(to_heads.into[...])
        query_ref[...] = queries.reshape(NQ, QB, HD)
        dc_ref[...] = one_above_other(d_to_heads.into[...]).reshape(NQ, QB, HD)
        keys_t = keys.T

        def attend_back(i):
            d_ctx = dc_ref[i]
            d_prob = nt(values, d_ctx)
            prob = probs[l][i].astype(F32) * shares[l, i]
            row = jnp.sum(prob * d_prob, axis=0, keepdims=True)
            d_score = (prob * (d_prob - row)).astype(BF16)
            dq_ref[i] = (nn(keys_t, d_score) * 0.125).T.astype(BF16)
            return nn(prob.astype(BF16), d_ctx), nn(d_score, query_ref[i])

        terms = [attend_back(i) for i in range(NQ)]
        dv_ref[...] = sum(term[0] for term in terms)
        dk_ref[...] = sum(term[1] for term in terms)
        both = jnp.concatenate([dq_ref[...].reshape(LENGTH, HD), dk_ref[...].astype(BF16)], axis=1)
        d_to_tokens.out[:, 0:ROWS, :] = both.reshape(GROUP, ROWS, 2 * HD)
        d_to_tokens.out[:, ROWS:96, :] = side_by_side(dv_ref[...].astype(BF16).reshape(GROUP, ROWS, HD))
        d_to_tokens.start()
        if l > 0:
            down_grad(1)
            up_grad(1)
        run(above[:3], "e2")
        run(first_along(sums[l][3:], "yz"), "e1")
        run(qkv, "sent")
        run(first_along(above[3:], "x"), "e3")
        d_to_tokens.wait()
        d_joined = join_heads(d_to_tokens.into)
        d_small[l, 1:2, :] = column_sum(d_joined[:, 2 * D :].astype(F32))
        grad = grad_one
        source = source_ref[...]
        if l == 0:
            for i in range(3):
                qkv[i].store(0, tn(source, d_joined[:, i * D : (i + 1) * D]))
                qkv[i].e0()
        for i in range(3):
            grad = grad + nt(d_joined[:, i * D : (i + 1) * D], qkv[i].value())
        if l > 0:
            for i in range(3):
                qkv[i].store(0, tn(source, d_joined[:, i * D : (i + 1) * D]))
                qkv[i].e0()
    dx_ref[...] = grad
    dx_copy = pltpu.make_async_copy(dx_ref, dx_hbm, out_sems.at[1])
    dx_copy.start()
    qkv, rest, above = sums[0][:3], sums[0][3:], sums[1]
    run(qkv, "e1")

    small_grad[...] = jnp.zeros_like(small_grad)
    for l in range(LAYERS):
        for t in range(GROUP):
            small_grad[t, l * 8 + 1 : l * 8 + 8, 0:32] = d_small[l, 1:8, t * 32 : (t + 1) * 32]
            small_grad[t, l * 8 : l * 8 + 1, :] = d_small_up[l, :, t * 128 : (t + 1) * 128]
    for to in p.group():
        remote(small_grad.at[to], small_in.at[me], small_sems.at[2], small_sems.at[3], (p.rep, to))
    small_in[me] = small_grad[me]
    run(first_along(rest, "x"), "e2")
    run(first_along(above[3:], "yz") + above[:3], "e3")
    run(first_along(rest, "yz"), "e2")
    run(qkv, "e2")
    run(rest, "e3")
    wait_bytes(small_in.at[pl.ds(0, GROUP - 1)], small_sems.at[3])
    total = small_in[0]
    for t in range(1, GROUP):
        total = total + small_in[t]
    slot = small_rep.at[p.rep]
    slot[...] = total
    nrep = nx * nzl
    for d in range(1, nrep):
        remote(slot, slot, small_sems.at[4], small_sems.at[5], (lax.rem(p.rep + d, nrep), me))
    run(above, "e4")
    run(qkv, "e3")
    run(rest, "e4")
    if nrep > 1:
        wait_bytes(small_rep.at[pl.ds(0, nrep - 1)], small_sems.at[5])
    total = small_rep[0]
    for t in range(1, nrep):
        total = total + small_rep[t]
    for l in range(LAYERS):
        at = l * 8
        upb_out[l : l + 1, :] = total[at : at + 1, :]
        bias_out[l] = total[at + 1 : at + 4, 0:32]
        gain_out[l] = total[at + 4 : at + 6, 0:32]
        shift_out[l] = total[at + 6 : at + 8, 0:32]
    run(qkv, "e4")

    run(sums[0] + sums[1], "reduced")
    for l in range(LAYERS):
        for one in swap[l]:
            one.finish()
    wait_bytes(small_all.at[pl.ds(0, GROUP - 1)], small_sems.at[0])
    wait_bytes(small_grad.at[pl.ds(0, GROUP - 1)], small_sems.at[2])
    if nrep > 1:
        wait_bytes(small_rep.at[pl.ds(0, nrep - 1)], small_sems.at[4])
    out_copy.wait()
    dx_copy.wait()


def scratch(nx, nzl, members):
    sizes = {"x": nx, "y": Y, "z": ZH * nzl}
    nrep = nx * nzl
    shapes = [pltpu.VMEM((TOK, D), BF16), pltpu.VMEM((TOK, D), F32)]
    shapes += [pltpu.VMEM(member.shape, F32) for member in members[:4]]
    for _ in range(LAYERS):
        for _, _, r, c, _, _ in PARTS:
            shapes.append(pltpu.VMEM((ZH, Y, CORES, r, c), BF16))
    for _, _, r, c, _, _ in PARTS[:3]:
        shapes.append(pltpu.VMEM((ZH, Y, CORES, r, c), BF16))
    for _ in range(LAYERS):
        for _, _, r, c, _, _ in PARTS:
            shapes.append(pltpu.VMEM((ZH, Y, r, c), BF16))
    for l in range(LAYERS):
        for which in bundles(nx, nzl):
            pieces = [piece_shape(PARTS[i][2], PARTS[i][3], nx, nzl) for i in which]
            piece = (pieces[0][0], sum(cols for _, cols in pieces))
            na, nb, nc = [sizes[axis] for axis in AXES[PARTS[which[0]][5][l]]]
            shapes.append(pltpu.VMEM((na, nb, nc) + piece, BF16))
            shapes.append(pltpu.VMEM((max(na - 1, 1), nb, nc) + piece, BF16))
            shapes.append(pltpu.VMEM((nb, nc) + piece, BF16))
            shapes.append(pltpu.VMEM((nb * nc - 1,) + piece, BF16))
            shapes.append(pltpu.VMEM((nrep,) + piece, BF16))
    for _ in range(LAYERS):
        for rows in (96, 32, 32, 96):
            shapes += [pltpu.VMEM((GROUP, rows, 128), BF16)] * 2
    shapes += [pltpu.VMEM((16, 128), F32)]
    shapes += [pltpu.VMEM((GROUP, 16, 128), F32)] * 3
    shapes += [pltpu.VMEM((nrep, 16, 128), F32)]
    shapes += [pltpu.VMEM((LAYERS, 8, D), F32), pltpu.VMEM((LAYERS, 1, FF), F32)] * 2
    for _ in range(LAYERS):
        shapes += [
            pltpu.VMEM((TOK, D), BF16),
            pltpu.VMEM((TOK, D), F32),
            pltpu.VMEM((TOK, 1), F32),
            pltpu.VMEM((TOK, D), F32),
            pltpu.VMEM((TOK, 1), F32),
            pltpu.VMEM((TOK, D), BF16),
            pltpu.VMEM((TOK, FF), BF16),
            pltpu.VMEM((TOK, FF), F32),
        ]
    shapes += [pltpu.VMEM((NQ, LENGTH, QB), BF16)] * LAYERS
    shapes += [pltpu.VMEM((LAYERS, NQ, 1, QB), F32)]
    shapes += [pltpu.VMEM((NQ, QB, HD), BF16)] * 3
    shapes += [pltpu.VMEM((LENGTH, HD), F32)] * 2
    shapes += [
        pltpu.SemaphoreType.DMA((LAYERS * len(PARTS), SEMS)),
        pltpu.SemaphoreType.DMA((LAYERS * 4, 2)),
        pltpu.SemaphoreType.DMA((6,)),
        pltpu.SemaphoreType.DMA((2,)),
    ]
    return shapes


def copy_kernel(*refs):
    n = 10
    source, target, held, sems = refs[:n], refs[n : 2 * n], refs[2 * n : 3 * n], refs[-1]
    into = [pltpu.make_async_copy(source[i], held[i], sems.at[0, i]) for i in range(n)]
    outof = [pltpu.make_async_copy(held[i], target[i], sems.at[1, i]) for i in range(n)]
    for copy in into:
        copy.start()
    for i in range(n):
        into[i].wait()
        outof[i].start()
    for copy in outof:
        copy.wait()


def local_call(nx, nzl, inputs, *arguments):
    cotangent, members = arguments[-1], arguments[:-1]
    shapes = [jax.ShapeDtypeStruct((TOK, D), BF16), jax.ShapeDtypeStruct((TOK, D), F32)]
    shapes += [jax.ShapeDtypeStruct(member.shape, F32) for member in members]
    anywhere, vmem = pl.BlockSpec(memory_space=pl.ANY), pl.BlockSpec(memory_space=pltpu.VMEM)
    got = pl.pallas_call(
        functools.partial(kernel, nx, nzl),
        out_shape=shapes,
        in_specs=[vmem] * 10,
        out_specs=[anywhere] * 6 + [vmem] * 4,
        scratch_shapes=scratch(nx, nzl, members),
        compiler_params=pltpu.CompilerParams(
            collective_id=0, has_side_effects=True, vmem_limit_bytes=63 * 1024 * 1024
        ),
        cost_estimate=pl.CostEstimate(flops=7 * 10**9, bytes_accessed=8 * 10**6, transcendentals=5 * 10**6),
    )(inputs.reshape(TOK, D), cotangent.reshape(TOK, D), *members)
    return pl.pallas_call(
        copy_kernel,
        out_shape=shapes,
        in_specs=[anywhere] * 10,
        out_specs=[anywhere] * 10,
        scratch_shapes=[pltpu.VMEM(shape.shape, shape.dtype) for shape in shapes] + [pltpu.SemaphoreType.DMA((2, 10))],
    )(*got)


def solution(mesh):
    nrep = mesh.shape["rep"]
    nzl = 2 if nrep >= 2 else 1
    nx = nrep // nzl

    def shards(inputs, *arguments):
        got = local_call(nx, nzl, inputs, *arguments)
        return (got[0].reshape(inputs.shape), got[1].reshape(inputs.shape), *got[2:])

    rows, columns = P(None, "shard", None), P(None, None, "shard")
    both = P("rep", "shard", None)
    weights = (rows, rows, rows, rows, columns, columns, columns, P(None, "shard"))
    return jax.shard_map(
        shards,
        mesh=mesh,
        in_specs=(both, *weights, both),
        out_specs=(both, both, *weights),
        check_vma=False,
    )
```

```python
import functools

import jax
import jax.numpy as jnp
from jax import lax
from jax.experimental import pallas as pl
from jax.experimental.pallas import tpu as pltpu
from jax.sharding import PartitionSpec as P

MESH = pl.DeviceIdType.MESH
F32 = jnp.float32
BF16 = jnp.bfloat16
H, HD, D, FF, LAYERS = 8, 64, 512, 2048, 2
ZH, Y, CORES = 2, 4, 2
GROUP = ZH * Y * CORES
ROWS = 64
TOK = 2 * ROWS
LENGTH = GROUP * ROWS
QB = 512
NQ = LENGTH // QB
UNROLL = NQ // ZH
QKV, PROJ, UP, DOWN = range(4)
PARTS = (
    (QKV, 0, 32, 512, "xx", "xx"),
    (QKV, 512, 32, 512, "zz", "zz"),
    (QKV, 1024, 32, 512, "yy", "yy"),
    (PROJ, 0, 32, 512, "xx", "xx"),
    (UP, 0, 32, 1024, "xx", "xx"),
    (UP, 1024, 32, 1024, "zz", "zz"),
    (DOWN, 0, 128, 256, "xx", "xx"),
    (DOWN, 256, 128, 256, "yy", "yy"),
)
SEMS = 17
AXES = {"x": "xyz", "y": "yxz", "z": "zxy"}


def piece_shape(rows, cols, nx, nzl):
    return (rows // (nx * nzl), cols) if rows == 128 else (rows // nzl, cols // nx)


def bundles(nx, nzl):
    if nx * nzl == 8:
        return ((0,), (1,), (2,), (3, 4, 6), (5,), (7,))
    return tuple((i,) for i in (0, 1, 2, 3, 4, 6, 5, 7))


def nn(a, b):
    return jnp.dot(a, b, preferred_element_type=F32)


def nt(a, b):
    return lax.dot_general(a, b, (((1,), (1,)), ((), ())), preferred_element_type=F32)


def tn(a, b):
    return lax.dot_general(a, b, (((0,), (0,)), ((), ())), preferred_element_type=F32)


def norm_forward(values, gain, shift):
    center = values - jnp.mean(values, axis=-1, keepdims=True)
    spread = jnp.mean(center * center, axis=-1, keepdims=True)
    scale = lax.rsqrt(spread + 1e-06)
    unit = center * scale
    return unit * gain + shift, unit, scale


def norm_backward(grad, unit, scale, gain):
    d_unit = grad * gain
    first = jnp.mean(d_unit, axis=-1, keepdims=True)
    second = jnp.mean(d_unit * unit, axis=-1, keepdims=True)
    d_gain = jnp.sum(grad * unit, axis=0, keepdims=True)
    d_shift = jnp.sum(grad, axis=0, keepdims=True)
    return scale * (d_unit - first - unit * second), d_gain, d_shift


def column_sum(values):
    return jnp.sum(values, axis=0, keepdims=True)


def wait_bytes(ref, sem):
    pltpu.make_async_copy(ref, ref, sem).wait()


class Place:
    def __init__(self, nx, nzl):
        self.nx, self.nzl, self.nz = nx, nzl, ZH * nzl
        rep, shard = lax.axis_index("rep"), lax.axis_index("shard")
        self.rep, self.shard = rep, shard
        self.zl, self.x = lax.div(rep, nx), lax.rem(rep, nx)
        self.zh, self.y = lax.div(shard, Y * CORES), lax.rem(lax.div(shard, CORES), Y)
        self.core = lax.rem(shard, CORES)
        self.z = self.zh * nzl + self.zl

    def at(self, x=None, y=None, z=None, core=None):
        x = self.x if x is None else x
        y = self.y if y is None else y
        z = self.z if z is None else z
        core = self.core if core is None else core
        zh, zl = lax.div(z, self.nzl), lax.rem(z, self.nzl)
        return (zl * self.nx + x, zh * (Y * CORES) + y * CORES + core)

    def xs(self, d):
        return lax.rem(self.x + d, self.nx)

    def ys(self, d):
        return lax.rem(self.y + d, Y)

    def zs(self, d):
        return lax.rem(self.z + d, self.nz)

    def group(self):
        steps = [(dy, dz, dc) for dy in (2, 1, 3, 0) for dz in (1, 0) for dc in range(CORES) if dy or dz or dc]
        steps.sort(key=lambda step: -(2 * min(step[0], 1) + 2 * step[1] + step[2]))
        found = []
        for dy, dz, dc in steps:
            z = lax.rem(self.z + dz * self.nzl, self.nz)
            found.append(self.at(y=self.ys(dy), z=z, core=lax.rem(self.core + dc, CORES))[1])
        return found

    def peers(self):
        found = []
        for dy in range(Y):
            for dz in range(self.nz):
                if dy or dz:
                    found.append(self.at(y=self.ys(dy), z=self.zs(dz)))
        for dx in range(1, self.nx):
            for dz in range(self.nz):
                found.append(self.at(x=self.xs(dx), z=self.zs(dz)))
        for dx in range(1, self.nx):
            for dy in range(1, Y):
                found.append(self.at(x=self.xs(dx), y=self.ys(dy)))
        for dy in range(Y):
            for zh in range(ZH):
                z = lax.rem(self.z + zh * self.nzl, self.nz)
                found.append(self.at(y=self.ys(dy), z=z, core=1 - self.core))
        return found


def remote(src, dst, send_sem, recv_sem, device):
    pltpu.make_async_remote_copy(
        src_ref=src, dst_ref=dst, send_sem=send_sem, recv_sem=recv_sem, device_id=device, device_id_type=MESH
    ).start()


class Exchange:
    def __init__(self, place, out, into, sems):
        self.place, self.out, self.into, self.sems = place, out, into, sems

    def start(self):
        me = self.place.shard
        for to in self.place.group():
            remote(self.out.at[to], self.into.at[me], self.sems.at[0], self.sems.at[1], (self.place.rep, to))
        self.into[me] = self.out[me]

    def send(self, first, blocks):
        me = self.place.shard
        for j in range(blocks.shape[0]):
            self.out[first + j] = blocks[j]
        for j in range(blocks.shape[0]):
            to = first + j

            @pl.when(to != me)
            def _():
                remote(self.out.at[to], self.into.at[me], self.sems.at[0], self.sems.at[1], (self.place.rep, to))

            @pl.when(to == me)
            def _():
                self.into[me] = self.out[me]

    def wait(self):
        wait_bytes(self.into.at[pl.ds(0, GROUP - 1)], self.sems.at[1])

    def finish(self):
        wait_bytes(self.out.at[pl.ds(0, GROUP - 1)], self.sems.at[0])


class Part:
    def __init__(self, place, own, full, grad, sems, pair, far, near, result, out):
        self.place, self.own, self.full, self.grad, self.sems = place, own, full, grad, sems
        self.pair, self.far, self.near, self.result, self.out = pair, far, near, result, out
        self.rows, self.cols = own.shape

    def sem(self, i):
        return self.sems.at[i]

    def sibling(self):
        return self.place.at(core=1 - self.place.core)

    def across(self):
        return self.place.nz - 1 - self.place.z

    def keep(self):
        p = self.place
        self.full[p.zh, p.y, p.core] = self.own[...]

    def quarter(self, ref, x):
        nx = self.place.nx
        if self.rows == 128:
            n = self.rows // nx
            return ref.at[..., pl.ds(pl.multiple_of(x * n, n), n), :]
        n = self.cols // nx
        return ref.at[..., pl.ds(pl.multiple_of(x * n, n), n)]

    def g0(self):
        p = self.place
        slot = self.full.at[p.zh, p.y, p.core]
        if self.far == "x":
            src, dst = self.quarter(self.own, p.x), self.quarter(slot, p.x)
            for d in (2, 1, 3, 0):
                remote(src, dst, self.sem(4), self.sem(1), p.at(y=p.ys(d), z=self.across()))
            for d in (2, 1, 3):
                remote(src, dst, self.sem(3), self.sem(0), p.at(y=p.ys(d)))
        else:
            if self.far == "y":
                remote(self.own, slot, self.sem(3), self.sem(0), p.at(z=self.across()))
            for d in (2, 1, 3):
                remote(self.own, slot, self.sem(4), self.sem(1), p.at(y=p.ys(d)))

    def g1(self):
        p, full = self.place, self.full
        if self.far == "x":
            wait_bytes(self.quarter(full.at[0, pl.ds(0, 3), 0], 0), self.sem(0))
            wait_bytes(self.quarter(full.at[0, :, 0], 0), self.sem(1))
            mine = self.quarter(full.at[:, :, p.core], p.x)
            for d in order_of(p.nx):
                remote(mine, mine, self.sem(5), self.sem(2), p.at(x=p.xs(d)))
        elif self.far == "y":
            wait_bytes(full.at[0, 0, 0], self.sem(0))
            slot = full.at[1 - p.zh, p.y, p.core]
            for d in (2, 1, 3):
                remote(slot, slot, self.sem(5), self.sem(2), p.at(y=p.ys(d)))
        else:
            wait_bytes(full.at[0, pl.ds(0, 3), 0], self.sem(1))
            half = full.at[p.zh, :, p.core]
            remote(half, half, self.sem(5), self.sem(2), p.at(z=self.across()))

    def g2(self):
        p, full = self.place, self.full
        if self.far == "x":
            if p.nx > 1:
                wait_bytes(full.at[:, pl.ds(0, p.nx - 1), 0], self.sem(2))
        elif self.far == "y":
            wait_bytes(full.at[0, pl.ds(0, 3), 0], self.sem(1))
            wait_bytes(full.at[0, pl.ds(0, 3), 0], self.sem(2))
        else:
            wait_bytes(full.at[0, :, 0], self.sem(2))
        both = full.at[:, :, p.core]
        remote(both, both, self.sem(6), self.sem(7), self.sibling())

    def g3(self):
        wait_bytes(self.full.at[:, :, 0], self.sem(7))

    def sent(self):
        full, nx = self.full, self.place.nx
        if self.far == "x":
            wait_bytes(self.quarter(full.at[0, pl.ds(0, 3), 0], 0), self.sem(3))
            wait_bytes(self.quarter(full.at[0, :, 0], 0), self.sem(4))
            if nx > 1:
                wait_bytes(full.at[:, pl.ds(0, nx - 1), 0], self.sem(5))
        elif self.far == "y":
            wait_bytes(full.at[0, 0, 0], self.sem(3))
            wait_bytes(full.at[0, pl.ds(0, 3), 0], self.sem(4))
            wait_bytes(full.at[0, pl.ds(0, 3), 0], self.sem(5))
        else:
            wait_bytes(full.at[0, pl.ds(0, 3), 0], self.sem(4))
            wait_bytes(full.at[0, :, 0], self.sem(5))
        wait_bytes(full.at[:, :, 0], self.sem(6))

    def value(self):
        return self.full[...].reshape(GROUP * self.rows, self.cols)

    def store(self, start, block):
        count = block.shape[0]
        per_y = CORES * self.rows
        block = block.astype(BF16)
        if count == ZH * Y * per_y:
            self.grad[...] = block.reshape(ZH, Y, CORES, self.rows, self.cols)
        elif count == Y * per_y:
            self.grad[start // count] = block.reshape(Y, CORES, self.rows, self.cols)
        else:
            n = count // per_y
            zh, y = divmod(start // per_y, Y)
            self.grad[zh, y : y + n] = block.reshape(n, CORES, self.rows, self.cols)

    def piece(self, zl, x):
        p = self.place
        if self.rows == 128:
            n = self.rows // (p.nx * p.nzl)
            at = (zl * p.nx + x) * n
            return slice(at, at + n), slice(None)
        half, part = self.rows // p.nzl, self.cols // p.nx
        return slice(zl * half, (zl + 1) * half), slice(x * part, (x + 1) * part)

    def e0(self):
        p = self.place
        remote(self.grad.at[:, :, 1 - p.core], self.pair, self.sem(8), self.sem(9), self.sibling())


class Sum:
    def __init__(self, place, parts, buffers):
        self.place, self.parts, self.sems = place, parts, parts[0].sems
        self.chip, self.recv1, self.sum1, self.recv2, self.recv3 = buffers
        p = place
        self.n = {"x": p.nx, "y": Y, "z": p.nz}
        self.me = {"x": p.x, "y": p.y, "z": p.z}
        self.axes = AXES[parts[0].near]

    def sem(self, i):
        return self.sems.at[i]

    def columns(self):
        at = 0
        for part in self.parts:
            rows, cols = piece_shape(part.rows, part.cols, self.place.nx, self.place.nzl)
            yield part, slice(at, at + cols)
            at += cols

    def e1(self):
        p = self.place
        for part, here in self.columns():
            wait_bytes(part.pair, part.sem(9))
            for zh in range(ZH):
                for y in range(Y):
                    total = part.grad[zh, y, p.core].astype(F32) + part.pair[zh, y].astype(F32)
                    total = total.astype(BF16)
                    for x in range(p.nx):
                        for zl in range(p.nzl):
                            at = {"x": x, "y": y, "z": zh * p.nzl + zl}
                            rows, cols = part.piece(zl, x)
                            a, b, c = [at[axis] for axis in self.axes]
                            self.chip[a, b, c, :, here] = total[rows, cols]
        a = self.axes[0]
        for d in order_of(self.n[a]):
            to = lax.rem(self.me[a] + d, self.n[a])
            remote(self.chip.at[to], self.recv1.at[d - 1], self.sem(10), self.sem(11), p.at(**{a: to}))

    def e2(self):
        p = self.place
        a, b, c = self.axes
        nb, nc = self.n[b], self.n[c]
        if self.n[a] > 1:
            wait_bytes(self.recv1, self.sem(11))
        for ib in range(nb):
            total = self.chip[self.me[a], ib].astype(F32)
            for d in range(self.n[a] - 1):
                total = total + self.recv1[d, ib].astype(F32)
            self.sum1[ib] = total.astype(BF16)
        pairs = [(db, dc) for db in range(nb) for dc in range(nc) if db or dc]
        for db, dc in sorted(pairs, key=lambda at: -(min(at[0], 1) + min(at[1], 1))):
            to_b, to_c = lax.rem(self.me[b] + db, nb), lax.rem(self.me[c] + dc, nc)
            remote(
                self.sum1.at[to_b, to_c],
                self.recv2.at[db * nc + dc - 1],
                self.sem(12),
                self.sem(13),
                p.at(**{b: to_b, c: to_c}),
            )

    def e3(self):
        p = self.place
        _, b, c = self.axes
        wait_bytes(self.recv2, self.sem(13))
        total = self.sum1[self.me[b], self.me[c]].astype(F32)
        for i in range(self.recv2.shape[0]):
            total = total + self.recv2[i].astype(F32)
        slot = self.recv3.at[p.rep]
        slot[...] = total.astype(BF16)
        nrep = p.nx * p.nzl
        for d in range(1, nrep):
            remote(slot, slot, self.sem(14), self.sem(15), (lax.rem(p.rep + d, nrep), p.shard))

    def e4(self):
        p = self.place
        nrep = p.nx * p.nzl
        if nrep > 1:
            wait_bytes(self.recv3.at[pl.ds(0, nrep - 1)], self.sem(15))
        for part, here in self.columns():
            for zl in range(p.nzl):
                for x in range(p.nx):
                    rows, cols = part.piece(zl, x)
                    part.result[rows, cols] = self.recv3[zl * p.nx + x, :, here].astype(F32)
            pltpu.make_async_copy(part.result, part.out, part.sem(16)).start()

    def reduced(self):
        p = self.place
        for part in self.parts:
            wait_bytes(part.pair, part.sem(8))
            pltpu.make_async_copy(part.result, part.out, part.sem(16)).wait()
        if self.n[self.axes[0]] > 1:
            wait_bytes(self.recv1, self.sem(10))
        wait_bytes(self.recv2, self.sem(12))
        if p.nx * p.nzl > 1:
            wait_bytes(self.recv3.at[pl.ds(0, p.nx * p.nzl - 1)], self.sem(14))


def order_of(n):
    return (2, 1, 3) if n == 4 else tuple(range(1, n))


def side_by_side(block):
    n = block.shape[-2] // 2
    return jnp.concatenate([block[..., :n, :], block[..., n:, :]], axis=-1)


def one_above_other(block):
    return jnp.concatenate([block[..., :HD], block[..., HD:]], axis=-2)


def split_heads(joined, slots):
    for s in range(2):
        rows = joined[s * ROWS : (s + 1) * ROWS]
        for h in range(H):
            at = h * HD
            query, key = rows[:, at : at + HD], rows[:, D + at : D + at + HD]
            slots[s * H + h, 0:ROWS] = jnp.concatenate([query, key], axis=1)
            slots[s * H + h, ROWS:96] = side_by_side(rows[:, 2 * D + at : 2 * D + at + HD])


def split_context(context, slots):
    for s in range(2):
        rows = context[s * ROWS : (s + 1) * ROWS]
        for h in range(H):
            slots[s * H + h] = side_by_side(rows[:, h * HD : (h + 1) * HD])


def join_context(slots):
    parts = []
    for s in range(2):
        heads = [one_above_other(slots[s * H + h]) for h in range(H)]
        parts.append(jnp.concatenate(heads, axis=1))
    return jnp.concatenate(parts, axis=0)


def join_heads(slots):
    parts = []
    for s in range(2):
        both = [slots[s * H + h] for h in range(H)]
        queries = [block[0:ROWS, :HD] for block in both]
        keys = [block[0:ROWS, HD:] for block in both]
        values = [one_above_other(block[ROWS:96]) for block in both]
        parts.append(jnp.concatenate(queries + keys + values, axis=1))
    return jnp.concatenate(parts, axis=0)


def head_parts(slots):
    both = slots[:, 0:ROWS, :].reshape(LENGTH, 2 * HD)
    values = one_above_other(slots[:, ROWS:96, :]).reshape(LENGTH, HD)
    queries = (both[:, :HD].astype(F32) * 0.125).astype(BF16)
    return queries, both[:, HD:], values


def kernel(nx, nzl, *refs):
    refs = list(refs)

    def take(n):
        got = refs[:n]
        del refs[:n]
        return got

    x_ref, cot_ref = take(2)
    own = take(4)
    bias_ref, gain_ref, shift_ref, upb_ref = take(4)
    out_hbm, dx_hbm = take(2)
    result_hbm = take(4)
    bias_out, gain_out, shift_out, upb_out = take(4)
    out_ref, dx_ref = take(2)
    results = take(4)
    full = [take(len(PARTS)) for _ in range(LAYERS)]
    last_grads = take(3)
    pairs = [take(len(PARTS)) for _ in range(LAYERS)]
    buffers = [[take(5) for _ in bundles(nx, nzl)] for _ in range(LAYERS)]
    swaps = [take(8) for _ in range(LAYERS)]
    small_own, small_all, small_grad, small_in, small_rep = take(5)
    small, small_up, d_small, d_small_up = take(4)
    saved = [take(8) for _ in range(LAYERS)]
    probs = take(LAYERS)
    (shares,) = take(1)
    query_ref, dc_ref, dq_ref, dk_ref, dv_ref = take(5)
    part_sems, swap_sems, small_sems, out_sems = take(4)

    p = Place(nx, nzl)
    parts = []
    for l in range(LAYERS):
        row = []
        for i, (w, at, _, cols, far, near) in enumerate(PARTS):
            here = pl.ds(at, cols)
            row.append(
                Part(
                    p,
                    own[w].at[l, :, here],
                    full[l][i],
                    last_grads[i] if l == 0 and i < 3 else full[l][i],
                    part_sems.at[l * len(PARTS) + i],
                    pairs[l][i],
                    far[l],
                    near[l],
                    results[w].at[l, :, here],
                    result_hbm[w].at[l, :, here],
                )
            )
        parts.append(row)
    swap = [
        [Exchange(p, swaps[l][2 * i], swaps[l][2 * i + 1], swap_sems.at[l * 4 + i]) for i in range(4)]
        for l in range(LAYERS)
    ]
    everything = [part for row in parts for part in row]
    sums = [
        [Sum(p, [parts[l][i] for i in which], buffers[l][k]) for k, which in enumerate(bundles(nx, nzl))]
        for l in range(LAYERS)
    ]

    for part in everything:
        part.keep()
    small_own[...] = jnp.zeros_like(small_own)
    for l in range(LAYERS):
        at = l * 8
        small_own[at : at + 1, :] = upb_ref[l : l + 1, :].astype(F32)
        for i in range(3):
            small_own[at + 1 + i : at + 2 + i, 0:32] = bias_ref[i, l : l + 1, :].astype(F32)
        small_own[at + 4 : at + 6, 0:32] = gain_ref[l].astype(F32)
        small_own[at + 6 : at + 8, 0:32] = shift_ref[l].astype(F32)
    small_all[p.shard] = small_own[...]
    barrier = pltpu.get_barrier_semaphore()
    peers = p.peers()
    for peer in peers:
        pl.semaphore_signal(barrier, inc=1, device_id=peer, device_id_type=MESH)
    pl.semaphore_wait(barrier, len(peers))

    me = p.shard

    def along(which, axes):
        return [part for part in which if part.far in axes]

    def first_along(which, axes):
        return [one for one in which if one.parts[0].near in axes]

    def run(which, *steps):
        for step in steps:
            for part in which:
                getattr(part, step)()

    early, late = parts[0][:3], parts[0][3:]
    run(early, "g0")
    run(early, "g1")
    for to in p.group():
        remote(small_own, small_all.at[me], small_sems.at[0], small_sems.at[1], (p.rep, to))
    run(along(late, "x"), "g0")
    run(along(late, "yz"), "g0")
    run(early, "g2")
    wait_bytes(small_all.at[pl.ds(0, GROUP - 1)], small_sems.at[1])
    for l in range(LAYERS):
        for q in range(4):
            part = [small_all[4 * q + i, l * 8 : l * 8 + 8, 0:32] for i in range(4)]
            small[l, :, q * 128 : (q + 1) * 128] = jnp.concatenate(part, axis=1)
        for t in range(GROUP):
            small_up[l, :, t * 128 : (t + 1) * 128] = small_all[t, l * 8 : l * 8 + 1, :]
    run(early, "g3")

    hidden = x_ref[...].astype(F32)
    for l in range(LAYERS):
        proj, up, down = parts[l][3], parts[l][4:6], parts[l][6:8]
        to_heads, to_tokens, _, _ = swap[l]
        source_ref, unit1, scale1, unit2, scale2, mid_ref, act_ref, slope_ref = saved[l]
        source = hidden.astype(BF16)
        source_ref[...] = source
        joined = [nn(source, part.value()) for part in parts[l][:3]]
        joined[2] = joined[2] + small[l, 1:2, :]
        split_heads(jnp.concatenate(joined, axis=1).astype(BF16), to_heads.out)
        to_heads.start()
        run(along(late, "x") if l == 0 else down[:1], "g1")
        run(up[1:] + down[1:], "g1")
        if l + 1 < LAYERS:
            run(parts[l + 1][:3], "g0")
        run([proj], "g2")
        to_heads.wait()
        queries, keys, values = head_parts(to_heads.into[...])
        query_ref[...] = queries.reshape(NQ, QB, HD)
        values_t = values.T

        def attend(i):
            scores = nt(keys, query_ref[i])
            expo = jnp.exp(scores - jnp.max(scores, axis=0, keepdims=True))
            part = 1.0 / jnp.sum(expo, axis=0, keepdims=True)
            low = expo.astype(BF16)
            probs[l][i] = low
            shares[l, i] = part
            block = (nn(values_t, low) * part).T.astype(BF16).reshape(QB // ROWS, ROWS, HD)
            return side_by_side(block)

        def attend_half(i, carry):
            first = lax.rem(i + 1 - p.zh, ZH) * UNROLL
            blocks = [attend(first + j) for j in range(UNROLL)]
            to_tokens.send(first * (QB // ROWS), jnp.concatenate(blocks, axis=0))
            return carry

        for half in range(ZH):
            attend_half(half, 0)
        if l + 1 < LAYERS:
            run(parts[l + 1][:3], "g1")
            run(parts[l + 1][3:], "g0")
        run([proj], "g3")
        run(up, "g2")
        to_tokens.wait()
        context = join_context(to_tokens.into)
        first = hidden + nn(context, proj.value()) + small[l, 2:3, :]
        middle, unit, scale = norm_forward(first, small[l, 4:5, :], small[l, 6:7, :])
        unit1[...], scale1[...] = unit, scale
        mid_low = middle.astype(BF16)
        mid_ref[...] = mid_low
        run(up, "g3")
        run(down, "g2")
        for j in range(4):
            at = j * 512
            weight = up[j // 2].full[:, :, :, :, (j % 2) * 512 : (j % 2) * 512 + 512].reshape(D, 512)
            upper = nn(mid_low, weight) + small_up[l, :, at : at + 512]
            phi = 0.5 + 0.5 * lax.erf(upper * (0.5**0.5))
            act_ref[:, at : at + 512] = (upper * phi).astype(BF16)
            density = jnp.exp(-0.5 * upper * upper) * 0.3989422804014327
            slope_ref[:, at : at + 512] = phi + upper * density
        run(down, "g3")
        second = jnp.concatenate([nn(act_ref[...], part.value()) for part in down], axis=1)
        second = middle + second + small[l, 3:4, :]
        hidden, unit, scale = norm_forward(second, small[l, 5:6, :], small[l, 7:8, :])
        unit2[...], scale2[...] = unit, scale
        if l + 1 < LAYERS:
            run(parts[l + 1][:3], "g2")
            run(parts[l + 1][3:5], "g1")
            run(parts[l + 1][:3], "g3")
    out_ref[...] = hidden.astype(BF16)
    out_copy = pltpu.make_async_copy(out_ref, out_hbm, out_sems.at[0])
    out_copy.start()

    grad = cot_ref[...].astype(F32)
    for l in reversed(range(LAYERS)):
        qkv, proj, up, down = parts[l][:3], parts[l][3], parts[l][4:6], parts[l][6:8]
        above = sums[l + 1] if l + 1 < LAYERS else []
        to_heads, to_tokens, d_to_heads, d_to_tokens = swap[l]
        source_ref, unit1, scale1, unit2, scale2, mid_ref, act_ref, slope_ref = saved[l]
        grad_two, d_small[l, 5:6, :], d_small[l, 7:8, :] = norm_backward(
            grad, unit2[...], scale2[...], small[l, 5:6, :]
        )
        low_two = grad_two.astype(BF16)
        d_small[l, 3:4, :] = column_sum(low_two.astype(F32))
        d_uppers = []
        for j in range(4):
            at = j * 512
            d_act = 0.0
            for i in range(2):
                weight = down[i].full[j // 2, (j % 2) * 2 : (j % 2) * 2 + 2].reshape(512, 256)
                d_act = d_act + nt(low_two[:, i * 256 : (i + 1) * 256], weight)
            d_upper = (d_act * slope_ref[:, at : at + 512]).astype(BF16)
            d_small_up[l, :, at : at + 512] = column_sum(d_upper.astype(F32))
            d_uppers.append(d_upper)
        d_upper = jnp.concatenate(d_uppers, axis=1)
        grad_mid = grad_two
        for i in range(2):
            grad_mid = grad_mid + nt(d_upper[:, i * 1024 : (i + 1) * 1024], up[i].value())
        grad_one, d_small[l, 4:5, :], d_small[l, 6:7, :] = norm_backward(
            grad_mid, unit1[...], scale1[...], small[l, 4:5, :]
        )
        low_one = grad_one.astype(BF16)
        d_small[l, 2:3, :] = column_sum(low_one.astype(F32))
        d_context = nt(low_one, proj.value()).astype(BF16)
        split_context(d_context, d_to_heads.out)
        d_to_heads.start()
        run(down + up + [proj], "sent")

        def down_grad(i):
            for j in range(8):
                block = tn(act_ref[:, j * 256 : (j + 1) * 256], low_two[:, i * 256 : (i + 1) * 256])
                down[i].store(j * 256, block)
            down[i].e0()

        def up_grad(i):
            for j in range(2):
                block = tn(mid_ref[:, j * 256 : (j + 1) * 256], d_upper[:, i * 1024 : (i + 1) * 1024])
                up[i].store(j * 256, block)
            up[i].e0()

        down_grad(0)
        up_grad(0)
        run(above[:3], "e1")
        if l == 0:
            down_grad(1)
            up_grad(1)
        context = join_context(to_tokens.into)
        for j in range(2):
            proj.store(j * 256, tn(context[:, j * 256 : (j + 1) * 256], low_one))
        proj.e0()
        run(above[3:], "e2")
        run(first_along(sums[l][3:], "x"), "e1")
        d_to_heads.wait()
        queries, keys, values = head_parts(to_heads.into[...])
        query_ref[...] = queries.reshape(NQ, QB, HD)
        dc_ref[...] = one_above_other(d_to_heads.into[...]).reshape(NQ, QB, HD)
        keys_t = keys.T

        def attend_back(i):
            d_ctx = dc_ref[i]
            d_prob = nt(values, d_ctx)
            prob = probs[l][i].astype(F32) * shares[l, i]
            row = jnp.sum(prob * d_prob, axis=0, keepdims=True)
            d_score = (prob * (d_prob - row)).astype(BF16)
            dq_ref[i] = (nn(keys_t, d_score) * 0.125).T.astype(BF16)
            return nn(prob.astype(BF16), d_ctx), nn(d_score, query_ref[i])

        terms = [attend_back(i) for i in range(NQ)]
        dv_ref[...] = sum(term[0] for term in terms)
        dk_ref[...] = sum(term[1] for term in terms)
        both = jnp.concatenate([dq_ref[...].reshape(LENGTH, HD), dk_ref[...].astype(BF16)], axis=1)
        d_to_tokens.out[:, 0:ROWS, :] = both.reshape(GROUP, ROWS, 2 * HD)
        d_to_tokens.out[:, ROWS:96, :] = side_by_side(dv_ref[...].astype(BF16).reshape(GROUP, ROWS, HD))
        d_to_tokens.start()
        if l > 0:
            down_grad(1)
            up_grad(1)
        run(above[:3], "e2")
        run(first_along(sums[l][3:], "yz"), "e1")
        run(qkv, "sent")
        run(first_along(above[3:], "x"), "e3")
        d_to_tokens.wait()
        d_joined = join_heads(d_to_tokens.into)
        d_small[l, 1:2, :] = column_sum(d_joined[:, 2 * D :].astype(F32))
        grad = grad_one
        source = source_ref[...]
        if l == 0:
            for i in range(3):
                qkv[i].store(0, tn(source, d_joined[:, i * D : (i + 1) * D]))
                qkv[i].e0()
        for i in range(3):
            grad = grad + nt(d_joined[:, i * D : (i + 1) * D], qkv[i].value())
        if l > 0:
            for i in range(3):
                qkv[i].store(0, tn(source, d_joined[:, i * D : (i + 1) * D]))
                qkv[i].e0()
    dx_ref[...] = grad
    dx_copy = pltpu.make_async_copy(dx_ref, dx_hbm, out_sems.at[1])
    dx_copy.start()
    qkv, rest, above = sums[0][:3], sums[0][3:], sums[1]
    run(qkv, "e1")

    small_grad[...] = jnp.zeros_like(small_grad)
    for l in range(LAYERS):
        for t in range(GROUP):
            small_grad[t, l * 8 + 1 : l * 8 + 8, 0:32] = d_small[l, 1:8, t * 32 : (t + 1) * 32]
            small_grad[t, l * 8 : l * 8 + 1, :] = d_small_up[l, :, t * 128 : (t + 1) * 128]
    for to in p.group():
        remote(small_grad.at[to], small_in.at[me], small_sems.at[2], small_sems.at[3], (p.rep, to))
    small_in[me] = small_grad[me]
    run(first_along(rest, "x"), "e2")
    run(first_along(above[3:], "yz") + above[:3], "e3")
    run(first_along(rest, "yz"), "e2")
    run(qkv, "e2")
    run(rest, "e3")
    wait_bytes(small_in.at[pl.ds(0, GROUP - 1)], small_sems.at[3])
    total = small_in[0]
    for t in range(1, GROUP):
        total = total + small_in[t]
    slot = small_rep.at[p.rep]
    slot[...] = total
    nrep = nx * nzl
    for d in range(1, nrep):
        remote(slot, slot, small_sems.at[4], small_sems.at[5], (lax.rem(p.rep + d, nrep), me))
    run(above, "e4")
    run(qkv, "e3")
    run(rest, "e4")
    if nrep > 1:
        wait_bytes(small_rep.at[pl.ds(0, nrep - 1)], small_sems.at[5])
    total = small_rep[0]
    for t in range(1, nrep):
        total = total + small_rep[t]
    for l in range(LAYERS):
        at = l * 8
        upb_out[l : l + 1, :] = total[at : at + 1, :]
        for i in range(3):
            bias_out[i, l : l + 1, :] = total[at + 1 + i : at + 2 + i, 0:32]
        gain_out[l] = total[at + 4 : at + 6, 0:32]
        shift_out[l] = total[at + 6 : at + 8, 0:32]
    run(qkv, "e4")

    run(sums[0] + sums[1], "reduced")
    for l in range(LAYERS):
        for one in swap[l]:
            one.finish()
    wait_bytes(small_all.at[pl.ds(0, GROUP - 1)], small_sems.at[0])
    wait_bytes(small_grad.at[pl.ds(0, GROUP - 1)], small_sems.at[2])
    if nrep > 1:
        wait_bytes(small_rep.at[pl.ds(0, nrep - 1)], small_sems.at[4])
    out_copy.wait()
    dx_copy.wait()


def scratch(nx, nzl, members):
    sizes = {"x": nx, "y": Y, "z": ZH * nzl}
    nrep = nx * nzl
    shapes = [pltpu.VMEM((TOK, D), BF16), pltpu.VMEM((TOK, D), F32)]
    shapes += [pltpu.VMEM(member.shape, F32) for member in members[:4]]
    for _ in range(LAYERS):
        for _, _, r, c, _, _ in PARTS:
            shapes.append(pltpu.VMEM((ZH, Y, CORES, r, c), BF16))
    for _, _, r, c, _, _ in PARTS[:3]:
        shapes.append(pltpu.VMEM((ZH, Y, CORES, r, c), BF16))
    for _ in range(LAYERS):
        for _, _, r, c, _, _ in PARTS:
            shapes.append(pltpu.VMEM((ZH, Y, r, c), BF16))
    for l in range(LAYERS):
        for which in bundles(nx, nzl):
            pieces = [piece_shape(PARTS[i][2], PARTS[i][3], nx, nzl) for i in which]
            piece = (pieces[0][0], sum(cols for _, cols in pieces))
            na, nb, nc = [sizes[axis] for axis in AXES[PARTS[which[0]][5][l]]]
            shapes.append(pltpu.VMEM((na, nb, nc) + piece, BF16))
            shapes.append(pltpu.VMEM((max(na - 1, 1), nb, nc) + piece, BF16))
            shapes.append(pltpu.VMEM((nb, nc) + piece, BF16))
            shapes.append(pltpu.VMEM((nb * nc - 1,) + piece, BF16))
            shapes.append(pltpu.VMEM((nrep,) + piece, BF16))
    for _ in range(LAYERS):
        for rows in (96, 32, 32, 96):
            shapes += [pltpu.VMEM((GROUP, rows, 128), BF16)] * 2
    shapes += [pltpu.VMEM((16, 128), F32)]
    shapes += [pltpu.VMEM((GROUP, 16, 128), F32)] * 3
    shapes += [pltpu.VMEM((nrep, 16, 128), F32)]
    shapes += [pltpu.VMEM((LAYERS, 8, D), F32), pltpu.VMEM((LAYERS, 1, FF), F32)] * 2
    for _ in range(LAYERS):
        shapes += [
            pltpu.VMEM((TOK, D), BF16),
            pltpu.VMEM((TOK, D), F32),
            pltpu.VMEM((TOK, 1), F32),
            pltpu.VMEM((TOK, D), F32),
            pltpu.VMEM((TOK, 1), F32),
            pltpu.VMEM((TOK, D), BF16),
            pltpu.VMEM((TOK, FF), BF16),
            pltpu.VMEM((TOK, FF), F32),
        ]
    shapes += [pltpu.VMEM((NQ, LENGTH, QB), BF16)] * LAYERS
    shapes += [pltpu.VMEM((LAYERS, NQ, 1, QB), F32)]
    shapes += [pltpu.VMEM((NQ, QB, HD), BF16)] * 3
    shapes += [pltpu.VMEM((LENGTH, HD), F32)] * 2
    shapes += [
        pltpu.SemaphoreType.DMA((LAYERS * len(PARTS), SEMS)),
        pltpu.SemaphoreType.DMA((LAYERS * 4, 2)),
        pltpu.SemaphoreType.DMA((6,)),
        pltpu.SemaphoreType.DMA((2,)),
    ]
    return shapes


def copy_kernel(*refs):
    n = 10
    source, target, held, sems = refs[:n], refs[n : 2 * n], refs[2 * n : 3 * n], refs[-1]
    into = [pltpu.make_async_copy(source[i], held[i], sems.at[0, i]) for i in range(n)]
    outof = [pltpu.make_async_copy(held[i], target[i], sems.at[1, i]) for i in range(n)]
    for copy in into:
        copy.start()
    for i in range(n):
        into[i].wait()
        outof[i].start()
    for copy in outof:
        copy.wait()


def local_call(nx, nzl, inputs, *arguments):
    cotangent, members = arguments[-1], list(arguments[:-1])
    members[4] = members[4].transpose(1, 0, 2)
    shapes = [jax.ShapeDtypeStruct((TOK, D), BF16), jax.ShapeDtypeStruct((TOK, D), F32)]
    shapes += [jax.ShapeDtypeStruct(member.shape, F32) for member in members]
    anywhere, vmem = pl.BlockSpec(memory_space=pl.ANY), pl.BlockSpec(memory_space=pltpu.VMEM)
    got = pl.pallas_call(
        functools.partial(kernel, nx, nzl),
        out_shape=shapes,
        in_specs=[vmem] * 10,
        out_specs=[anywhere] * 6 + [vmem] * 4,
        scratch_shapes=scratch(nx, nzl, members),
        compiler_params=pltpu.CompilerParams(
            collective_id=0, has_side_effects=True, vmem_limit_bytes=63 * 1024 * 1024
        ),
        cost_estimate=pl.CostEstimate(flops=7 * 10**9, bytes_accessed=8 * 10**6, transcendentals=5 * 10**6),
    )(inputs.reshape(TOK, D), cotangent.reshape(TOK, D), *members)
    got = pl.pallas_call(
        copy_kernel,
        out_shape=shapes,
        in_specs=[anywhere] * 10,
        out_specs=[anywhere] * 10,
        scratch_shapes=[pltpu.VMEM(shape.shape, shape.dtype) for shape in shapes] + [pltpu.SemaphoreType.DMA((2, 10))],
    )(*got)
    return (*got[:6], got[6].transpose(1, 0, 2), *got[7:])


def solution(mesh):
    nrep = mesh.shape["rep"]
    nzl = 2 if nrep >= 2 else 1
    nx = nrep // nzl

    def shards(inputs, *arguments):
        got = local_call(nx, nzl, inputs, *arguments)
        return (got[0].reshape(inputs.shape), got[1].reshape(inputs.shape), *got[2:])

    rows, columns = P(None, "shard", None), P(None, None, "shard")
    both = P("rep", "shard", None)
    weights = (rows, rows, rows, rows, columns, columns, columns, P(None, "shard"))
    return jax.shard_map(
        shards,
        mesh=mesh,
        in_specs=(both, *weights, both),
        out_specs=(both, both, *weights),
        check_vma=False,
    )
```

```python
import functools

import jax
import jax.numpy as jnp
from jax import lax
from jax.experimental import pallas as pl
from jax.experimental.pallas import tpu as pltpu
from jax.sharding import PartitionSpec as P

MESH = pl.DeviceIdType.MESH
F32 = jnp.float32
BF16 = jnp.bfloat16
H, HD, D, FF, LAYERS = 8, 64, 512, 2048, 2
ZH, Y, CORES = 2, 4, 2
GROUP = ZH * Y * CORES
ROWS = 64
TOK = 2 * ROWS
LENGTH = GROUP * ROWS
QB = 512
NQ = LENGTH // QB
UNROLL = NQ // ZH
QKV, PROJ, UP, DOWN = range(4)
PARTS = (
    (QKV, 0, 32, 512, "xx", "xx"),
    (QKV, 512, 32, 512, "zz", "zz"),
    (QKV, 1024, 32, 512, "yy", "yy"),
    (PROJ, 0, 32, 512, "xx", "xx"),
    (UP, 0, 32, 1024, "xx", "xx"),
    (UP, 1024, 32, 1024, "zz", "zz"),
    (DOWN, 0, 128, 256, "xx", "xx"),
    (DOWN, 256, 128, 256, "yy", "yy"),
)
SEMS = 17
AXES = {"x": "xyz", "y": "yxz", "z": "zxy"}


def piece_shape(rows, cols, nx, nzl):
    return (rows // (nx * nzl), cols) if rows == 128 else (rows // nzl, cols // nx)


def bundles(nx, nzl):
    if nx * nzl == 8:
        return ((0,), (1,), (2,), (3, 4, 6), (5,), (7,))
    return tuple((i,) for i in (0, 1, 2, 3, 4, 6, 5, 7))


def nn(a, b):
    return jnp.dot(a, b, preferred_element_type=F32)


def nt(a, b):
    return lax.dot_general(a, b, (((1,), (1,)), ((), ())), preferred_element_type=F32)


def tn(a, b):
    return lax.dot_general(a, b, (((0,), (0,)), ((), ())), preferred_element_type=F32)


def norm_forward(values, gain, shift):
    center = values - jnp.mean(values, axis=-1, keepdims=True)
    spread = jnp.mean(center * center, axis=-1, keepdims=True)
    scale = lax.rsqrt(spread + 1e-06)
    unit = center * scale
    return unit * gain + shift, unit, scale


def norm_backward(grad, unit, scale, gain):
    d_unit = grad * gain
    first = jnp.mean(d_unit, axis=-1, keepdims=True)
    second = jnp.mean(d_unit * unit, axis=-1, keepdims=True)
    d_gain = jnp.sum(grad * unit, axis=0, keepdims=True)
    d_shift = jnp.sum(grad, axis=0, keepdims=True)
    return scale * (d_unit - first - unit * second), d_gain, d_shift


def column_sum(values):
    return jnp.sum(values, axis=0, keepdims=True)


def wait_bytes(ref, sem):
    pltpu.make_async_copy(ref, ref, sem).wait()


class Place:
    def __init__(self, nx, nzl):
        self.nx, self.nzl, self.nz = nx, nzl, ZH * nzl
        rep, shard = lax.axis_index("rep"), lax.axis_index("shard")
        self.rep, self.shard = rep, shard
        self.zl, self.x = lax.div(rep, nx), lax.rem(rep, nx)
        self.zh, self.y = lax.div(shard, Y * CORES), lax.rem(lax.div(shard, CORES), Y)
        self.core = lax.rem(shard, CORES)
        self.z = self.zh * nzl + self.zl

    def at(self, x=None, y=None, z=None, core=None):
        x = self.x if x is None else x
        y = self.y if y is None else y
        z = self.z if z is None else z
        core = self.core if core is None else core
        zh, zl = lax.div(z, self.nzl), lax.rem(z, self.nzl)
        return (zl * self.nx + x, zh * (Y * CORES) + y * CORES + core)

    def xs(self, d):
        return lax.rem(self.x + d, self.nx)

    def ys(self, d):
        return lax.rem(self.y + d, Y)

    def zs(self, d):
        return lax.rem(self.z + d, self.nz)

    def group(self):
        steps = [(dy, dz, dc) for dy in (2, 1, 3, 0) for dz in (1, 0) for dc in range(CORES) if dy or dz or dc]
        steps.sort(key=lambda step: -(2 * min(step[0], 1) + 2 * step[1] + step[2]))
        found = []
        for dy, dz, dc in steps:
            z = lax.rem(self.z + dz * self.nzl, self.nz)
            found.append(self.at(y=self.ys(dy), z=z, core=lax.rem(self.core + dc, CORES))[1])
        return found

    def peers(self):
        found = []
        for dy in range(Y):
            for dz in range(self.nz):
                if dy or dz:
                    found.append(self.at(y=self.ys(dy), z=self.zs(dz)))
        for dx in range(1, self.nx):
            for dz in range(self.nz):
                found.append(self.at(x=self.xs(dx), z=self.zs(dz)))
        for dx in range(1, self.nx):
            for dy in range(1, Y):
                found.append(self.at(x=self.xs(dx), y=self.ys(dy)))
        for dy in range(Y):
            for zh in range(ZH):
                z = lax.rem(self.z + zh * self.nzl, self.nz)
                found.append(self.at(y=self.ys(dy), z=z, core=1 - self.core))
        return found


def remote(src, dst, send_sem, recv_sem, device):
    pltpu.make_async_remote_copy(
        src_ref=src, dst_ref=dst, send_sem=send_sem, recv_sem=recv_sem, device_id=device, device_id_type=MESH
    ).start()


class Exchange:
    def __init__(self, place, out, into, sems):
        self.place, self.out, self.into, self.sems = place, out, into, sems

    def start(self):
        me = self.place.shard
        for to in self.place.group():
            remote(self.out.at[to], self.into.at[me], self.sems.at[0], self.sems.at[1], (self.place.rep, to))
        self.into[me] = self.out[me]

    def send(self, first, blocks):
        me = self.place.shard
        for j in range(blocks.shape[0]):
            self.out[first + j] = blocks[j]
        for j in range(blocks.shape[0]):
            to = first + j

            @pl.when(to != me)
            def _():
                remote(self.out.at[to], self.into.at[me], self.sems.at[0], self.sems.at[1], (self.place.rep, to))

            @pl.when(to == me)
            def _():
                self.into[me] = self.out[me]

    def wait(self):
        wait_bytes(self.into.at[pl.ds(0, GROUP - 1)], self.sems.at[1])

    def finish(self):
        wait_bytes(self.out.at[pl.ds(0, GROUP - 1)], self.sems.at[0])


class Part:
    def __init__(self, place, own, full, grad, sems, pair, far, near, result, out):
        self.place, self.own, self.full, self.grad, self.sems = place, own, full, grad, sems
        self.pair, self.far, self.near, self.result, self.out = pair, far, near, result, out
        self.rows, self.cols = own.shape

    def sem(self, i):
        return self.sems.at[i]

    def sibling(self):
        return self.place.at(core=1 - self.place.core)

    def across(self):
        return self.place.nz - 1 - self.place.z

    def keep(self):
        p = self.place
        self.full[p.zh, p.y, p.core] = self.own[...]

    def quarter(self, ref, x):
        nx = self.place.nx
        if self.rows == 128:
            n = self.rows // nx
            return ref.at[..., pl.ds(pl.multiple_of(x * n, n), n), :]
        n = self.cols // nx
        return ref.at[..., pl.ds(pl.multiple_of(x * n, n), n)]

    def g0(self):
        p = self.place
        slot = self.full.at[p.zh, p.y, p.core]
        if self.far == "x":
            src, dst = self.quarter(self.own, p.x), self.quarter(slot, p.x)
            for d in (2, 1, 3, 0):
                remote(src, dst, self.sem(4), self.sem(1), p.at(y=p.ys(d), z=self.across()))
            for d in (2, 1, 3):
                remote(src, dst, self.sem(3), self.sem(0), p.at(y=p.ys(d)))
        else:
            if self.far == "y":
                remote(self.own, slot, self.sem(3), self.sem(0), p.at(z=self.across()))
            for d in (2, 1, 3):
                remote(self.own, slot, self.sem(4), self.sem(1), p.at(y=p.ys(d)))

    def g1(self):
        p, full = self.place, self.full
        if self.far == "x":
            wait_bytes(self.quarter(full.at[0, pl.ds(0, 3), 0], 0), self.sem(0))
            wait_bytes(self.quarter(full.at[0, :, 0], 0), self.sem(1))
            mine = self.quarter(full.at[:, :, p.core], p.x)
            for d in order_of(p.nx):
                remote(mine, mine, self.sem(5), self.sem(2), p.at(x=p.xs(d)))
        elif self.far == "y":
            wait_bytes(full.at[0, 0, 0], self.sem(0))
            slot = full.at[1 - p.zh, p.y, p.core]
            for d in (2, 1, 3):
                remote(slot, slot, self.sem(5), self.sem(2), p.at(y=p.ys(d)))
        else:
            wait_bytes(full.at[0, pl.ds(0, 3), 0], self.sem(1))
            half = full.at[p.zh, :, p.core]
            remote(half, half, self.sem(5), self.sem(2), p.at(z=self.across()))

    def g2(self):
        p, full = self.place, self.full
        if self.far == "x":
            if p.nx > 1:
                wait_bytes(full.at[:, pl.ds(0, p.nx - 1), 0], self.sem(2))
        elif self.far == "y":
            wait_bytes(full.at[0, pl.ds(0, 3), 0], self.sem(1))
            wait_bytes(full.at[0, pl.ds(0, 3), 0], self.sem(2))
        else:
            wait_bytes(full.at[0, :, 0], self.sem(2))
        both = full.at[:, :, p.core]
        remote(both, both, self.sem(6), self.sem(7), self.sibling())

    def g3(self):
        wait_bytes(self.full.at[:, :, 0], self.sem(7))

    def sent(self):
        full, nx = self.full, self.place.nx
        if self.far == "x":
            wait_bytes(self.quarter(full.at[0, pl.ds(0, 3), 0], 0), self.sem(3))
            wait_bytes(self.quarter(full.at[0, :, 0], 0), self.sem(4))
            if nx > 1:
                wait_bytes(full.at[:, pl.ds(0, nx - 1), 0], self.sem(5))
        elif self.far == "y":
            wait_bytes(full.at[0, 0, 0], self.sem(3))
            wait_bytes(full.at[0, pl.ds(0, 3), 0], self.sem(4))
            wait_bytes(full.at[0, pl.ds(0, 3), 0], self.sem(5))
        else:
            wait_bytes(full.at[0, pl.ds(0, 3), 0], self.sem(4))
            wait_bytes(full.at[0, :, 0], self.sem(5))
        wait_bytes(full.at[:, :, 0], self.sem(6))

    def value(self):
        return self.full[...].reshape(GROUP * self.rows, self.cols)

    def store(self, start, block):
        count = block.shape[0]
        per_y = CORES * self.rows
        block = block.astype(BF16)
        if count == ZH * Y * per_y:
            self.grad[...] = block.reshape(ZH, Y, CORES, self.rows, self.cols)
        elif count == Y * per_y:
            self.grad[start // count] = block.reshape(Y, CORES, self.rows, self.cols)
        else:
            n = count // per_y
            zh, y = divmod(start // per_y, Y)
            self.grad[zh, y : y + n] = block.reshape(n, CORES, self.rows, self.cols)

    def piece(self, zl, x):
        p = self.place
        if self.rows == 128:
            n = self.rows // (p.nx * p.nzl)
            at = (zl * p.nx + x) * n
            return slice(at, at + n), slice(None)
        half, part = self.rows // p.nzl, self.cols // p.nx
        return slice(zl * half, (zl + 1) * half), slice(x * part, (x + 1) * part)

    def e0(self):
        p = self.place
        remote(self.grad.at[:, :, 1 - p.core], self.pair, self.sem(8), self.sem(9), self.sibling())


class Sum:
    def __init__(self, place, parts, buffers):
        self.place, self.parts, self.sems = place, parts, parts[0].sems
        self.chip, self.recv1, self.sum1, self.recv2, self.recv3 = buffers
        p = place
        self.n = {"x": p.nx, "y": Y, "z": p.nz}
        self.me = {"x": p.x, "y": p.y, "z": p.z}
        self.axes = AXES[parts[0].near]

    def sem(self, i):
        return self.sems.at[i]

    def columns(self):
        at = 0
        for part in self.parts:
            rows, cols = piece_shape(part.rows, part.cols, self.place.nx, self.place.nzl)
            yield part, slice(at, at + cols)
            at += cols

    def e1(self):
        p = self.place
        for part, here in self.columns():
            wait_bytes(part.pair, part.sem(9))
            for zh in range(ZH):
                for y in range(Y):
                    total = part.grad[zh, y, p.core].astype(F32) + part.pair[zh, y].astype(F32)
                    total = total.astype(BF16)
                    for x in range(p.nx):
                        for zl in range(p.nzl):
                            at = {"x": x, "y": y, "z": zh * p.nzl + zl}
                            rows, cols = part.piece(zl, x)
                            a, b, c = [at[axis] for axis in self.axes]
                            self.chip[a, b, c, :, here] = total[rows, cols]
        a = self.axes[0]
        for d in order_of(self.n[a]):
            to = lax.rem(self.me[a] + d, self.n[a])
            remote(self.chip.at[to], self.recv1.at[d - 1], self.sem(10), self.sem(11), p.at(**{a: to}))

    def e2(self):
        p = self.place
        a, b, c = self.axes
        nb, nc = self.n[b], self.n[c]
        if self.n[a] > 1:
            wait_bytes(self.recv1, self.sem(11))
        for ib in range(nb):
            total = self.chip[self.me[a], ib].astype(F32)
            for d in range(self.n[a] - 1):
                total = total + self.recv1[d, ib].astype(F32)
            self.sum1[ib] = total.astype(BF16)
        pairs = [(db, dc) for db in range(nb) for dc in range(nc) if db or dc]
        for db, dc in sorted(pairs, key=lambda at: -(min(at[0], 1) + min(at[1], 1))):
            to_b, to_c = lax.rem(self.me[b] + db, nb), lax.rem(self.me[c] + dc, nc)
            remote(
                self.sum1.at[to_b, to_c],
                self.recv2.at[db * nc + dc - 1],
                self.sem(12),
                self.sem(13),
                p.at(**{b: to_b, c: to_c}),
            )

    def e3(self):
        p = self.place
        _, b, c = self.axes
        wait_bytes(self.recv2, self.sem(13))
        total = self.sum1[self.me[b], self.me[c]].astype(F32)
        for i in range(self.recv2.shape[0]):
            total = total + self.recv2[i].astype(F32)
        slot = self.recv3.at[p.rep]
        slot[...] = total.astype(BF16)
        nrep = p.nx * p.nzl
        for d in range(1, nrep):
            remote(slot, slot, self.sem(14), self.sem(15), (lax.rem(p.rep + d, nrep), p.shard))

    def e4(self):
        p = self.place
        nrep = p.nx * p.nzl
        if nrep > 1:
            wait_bytes(self.recv3.at[pl.ds(0, nrep - 1)], self.sem(15))
        for part, here in self.columns():
            for zl in range(p.nzl):
                for x in range(p.nx):
                    rows, cols = part.piece(zl, x)
                    part.result[rows, cols] = self.recv3[zl * p.nx + x, :, here].astype(F32)
            pltpu.make_async_copy(part.result, part.out, part.sem(16)).start()

    def reduced(self):
        p = self.place
        for part in self.parts:
            wait_bytes(part.pair, part.sem(8))
            pltpu.make_async_copy(part.result, part.out, part.sem(16)).wait()
        if self.n[self.axes[0]] > 1:
            wait_bytes(self.recv1, self.sem(10))
        wait_bytes(self.recv2, self.sem(12))
        if p.nx * p.nzl > 1:
            wait_bytes(self.recv3.at[pl.ds(0, p.nx * p.nzl - 1)], self.sem(14))


def order_of(n):
    return (2, 1, 3) if n == 4 else tuple(range(1, n))


def side_by_side(block):
    n = block.shape[-2] // 2
    return jnp.concatenate([block[..., :n, :], block[..., n:, :]], axis=-1)


def one_above_other(block):
    return jnp.concatenate([block[..., :HD], block[..., HD:]], axis=-2)


def split_heads(joined, slots):
    for s in range(2):
        rows = joined[s * ROWS : (s + 1) * ROWS]
        for h in range(H):
            at = h * HD
            query, key = rows[:, at : at + HD], rows[:, D + at : D + at + HD]
            slots[s * H + h, 0:ROWS] = jnp.concatenate([query, key], axis=1)
            slots[s * H + h, ROWS:96] = side_by_side(rows[:, 2 * D + at : 2 * D + at + HD])


def split_context(context, slots):
    for s in range(2):
        rows = context[s * ROWS : (s + 1) * ROWS]
        for h in range(H):
            slots[s * H + h] = side_by_side(rows[:, h * HD : (h + 1) * HD])


def join_context(slots):
    parts = []
    for s in range(2):
        heads = [one_above_other(slots[s * H + h]) for h in range(H)]
        parts.append(jnp.concatenate(heads, axis=1))
    return jnp.concatenate(parts, axis=0)


def join_heads(slots):
    parts = []
    for s in range(2):
        both = [slots[s * H + h] for h in range(H)]
        queries = [block[0:ROWS, :HD] for block in both]
        keys = [block[0:ROWS, HD:] for block in both]
        values = [one_above_other(block[ROWS:96]) for block in both]
        parts.append(jnp.concatenate(queries + keys + values, axis=1))
    return jnp.concatenate(parts, axis=0)


def head_parts(slots):
    both = slots[:, 0:ROWS, :].reshape(LENGTH, 2 * HD)
    values = one_above_other(slots[:, ROWS:96, :]).reshape(LENGTH, HD)
    queries = (both[:, :HD].astype(F32) * 0.125).astype(BF16)
    return queries, both[:, HD:], values


def kernel(nx, nzl, *refs):
    refs = list(refs)

    def take(n):
        got = refs[:n]
        del refs[:n]
        return got

    x_ref, cot_ref = take(2)
    own = take(4)
    bias_ref, gain_ref, shift_ref, upb_ref = take(4)
    out_hbm, dx_hbm = take(2)
    result_hbm = take(4)
    bias_out, gain_out, shift_out, upb_out = take(4)
    out_ref, dx_ref = take(2)
    results = take(4)
    full = [take(len(PARTS)) for _ in range(LAYERS)]
    last_grads = take(3)
    pairs = [take(len(PARTS)) for _ in range(LAYERS)]
    buffers = [[take(5) for _ in bundles(nx, nzl)] for _ in range(LAYERS)]
    swaps = [take(8) for _ in range(LAYERS)]
    small_own, small_all, small_grad, small_in, small_rep = take(5)
    small, small_up, d_small, d_small_up = take(4)
    saved = [take(8) for _ in range(LAYERS)]
    probs = take(LAYERS)
    (shares,) = take(1)
    query_ref, dc_ref, dq_ref, dk_ref, dv_ref = take(5)
    part_sems, swap_sems, small_sems, out_sems = take(4)

    p = Place(nx, nzl)
    parts = []
    for l in range(LAYERS):
        row = []
        for i, (w, at, _, cols, far, near) in enumerate(PARTS):
            here = pl.ds(at, cols)
            row.append(
                Part(
                    p,
                    own[w].at[l, :, here],
                    full[l][i],
                    last_grads[i] if l == 0 and i < 3 else full[l][i],
                    part_sems.at[l * len(PARTS) + i],
                    pairs[l][i],
                    far[l],
                    near[l],
                    results[w].at[l, :, here],
                    result_hbm[w].at[l, :, here],
                )
            )
        parts.append(row)
    swap = [
        [Exchange(p, swaps[l][2 * i], swaps[l][2 * i + 1], swap_sems.at[l * 4 + i]) for i in range(4)]
        for l in range(LAYERS)
    ]
    everything = [part for row in parts for part in row]
    sums = [
        [Sum(p, [parts[l][i] for i in which], buffers[l][k]) for k, which in enumerate(bundles(nx, nzl))]
        for l in range(LAYERS)
    ]

    for part in everything:
        part.keep()
    small_own[...] = jnp.zeros_like(small_own)
    for l in range(LAYERS):
        at = l * 8
        small_own[at : at + 1, :] = upb_ref[l : l + 1, :].astype(F32)
        for i in range(3):
            small_own[at + 1 + i : at + 2 + i, 0:32] = bias_ref[i, l : l + 1, :].astype(F32)
        small_own[at + 4 : at + 6, 0:32] = gain_ref[l].astype(F32)
        small_own[at + 6 : at + 8, 0:32] = shift_ref[l].astype(F32)
    small_all[p.shard] = small_own[...]
    barrier = pltpu.get_barrier_semaphore()
    peers = p.peers()
    for peer in peers:
        pl.semaphore_signal(barrier, inc=1, device_id=peer, device_id_type=MESH)
    pl.semaphore_wait(barrier, len(peers))

    me = p.shard

    def along(which, axes):
        return [part for part in which if part.far in axes]

    def first_along(which, axes):
        return [one for one in which if one.parts[0].near in axes]

    def run(which, *steps):
        for step in steps:
            for part in which:
                getattr(part, step)()

    early, late = parts[0][:3], parts[0][3:]
    run(early, "g0")
    run(early, "g1")
    for to in p.group():
        remote(small_own, small_all.at[me], small_sems.at[0], small_sems.at[1], (p.rep, to))
    run(along(late, "x"), "g0")
    run(along(late, "yz"), "g0")
    run(early, "g2")
    wait_bytes(small_all.at[pl.ds(0, GROUP - 1)], small_sems.at[1])
    for l in range(LAYERS):
        for q in range(4):
            part = [small_all[4 * q + i, l * 8 : l * 8 + 8, 0:32] for i in range(4)]
            small[l, :, q * 128 : (q + 1) * 128] = jnp.concatenate(part, axis=1)
        for t in range(GROUP):
            small_up[l, :, t * 128 : (t + 1) * 128] = small_all[t, l * 8 : l * 8 + 1, :]
    run(early, "g3")

    hidden = x_ref[...].astype(F32)
    for l in range(LAYERS):
        proj, up, down = parts[l][3], parts[l][4:6], parts[l][6:8]
        to_heads, to_tokens, _, _ = swap[l]
        source_ref, unit1, scale1, unit2, scale2, mid_ref, act_ref, slope_ref = saved[l]
        source = hidden.astype(BF16)
        source_ref[...] = source
        joined = [nn(source, part.value()) for part in parts[l][:3]]
        joined[2] = joined[2] + small[l, 1:2, :]
        split_heads(jnp.concatenate(joined, axis=1).astype(BF16), to_heads.out)
        to_heads.start()
        run(along(late, "x") if l == 0 else down[:1], "g1")
        run(up[1:] + down[1:], "g1")
        if l + 1 < LAYERS:
            run(parts[l + 1][:3], "g0")
        run([proj], "g2")
        to_heads.wait()
        queries, keys, values = head_parts(to_heads.into[...])
        query_ref[...] = queries.reshape(NQ, QB, HD)
        values_t = values.T

        def attend(i):
            scores = nt(keys, query_ref[i])
            expo = jnp.exp(scores - jnp.max(scores, axis=0, keepdims=True))
            part = 1.0 / jnp.sum(expo, axis=0, keepdims=True)
            low = expo.astype(BF16)
            probs[l][i] = low
            shares[l, i] = part
            block = (nn(values_t, low) * part).T.astype(BF16).reshape(QB // ROWS, ROWS, HD)
            return side_by_side(block)

        def attend_half(i, carry):
            first = lax.rem(i + 1 - p.zh, ZH) * UNROLL
            blocks = [attend(first + j) for j in range(UNROLL)]
            to_tokens.send(first * (QB // ROWS), jnp.concatenate(blocks, axis=0))
            return carry

        for half in range(ZH):
            attend_half(half, 0)
        if l + 1 < LAYERS:
            run(parts[l + 1][:3], "g1")
            run(parts[l + 1][3:], "g0")
        run([proj], "g3")
        run(up, "g2")
        to_tokens.wait()
        run(down, "g2")
        context = join_context(to_tokens.into)
        first = hidden + nn(context, proj.value()) + small[l, 2:3, :]
        middle, unit, scale = norm_forward(first, small[l, 4:5, :], small[l, 6:7, :])
        unit1[...], scale1[...] = unit, scale
        mid_low = middle.astype(BF16)
        mid_ref[...] = mid_low
        run(up, "g3")
        for j in range(4):
            at = j * 512
            weight = up[j // 2].full[:, :, :, :, (j % 2) * 512 : (j % 2) * 512 + 512].reshape(D, 512)
            upper = nn(mid_low, weight) + small_up[l, :, at : at + 512]
            phi = 0.5 + 0.5 * lax.erf(upper * (0.5**0.5))
            act_ref[:, at : at + 512] = (upper * phi).astype(BF16)
            density = jnp.exp(-0.5 * upper * upper) * 0.3989422804014327
            slope_ref[:, at : at + 512] = phi + upper * density
        run(down, "g3")
        if l + 1 < LAYERS:
            run(parts[l + 1][:3], "g2")
        second = jnp.concatenate([nn(act_ref[...], part.value()) for part in down], axis=1)
        second = middle + second + small[l, 3:4, :]
        hidden, unit, scale = norm_forward(second, small[l, 5:6, :], small[l, 7:8, :])
        unit2[...], scale2[...] = unit, scale
        if l + 1 < LAYERS:
            run(parts[l + 1][3:5], "g1")
            run(parts[l + 1][:3], "g3")
    out_ref[...] = hidden.astype(BF16)
    out_copy = pltpu.make_async_copy(out_ref, out_hbm, out_sems.at[0])
    out_copy.start()

    grad = cot_ref[...].astype(F32)
    for l in reversed(range(LAYERS)):
        qkv, proj, up, down = parts[l][:3], parts[l][3], parts[l][4:6], parts[l][6:8]
        above = sums[l + 1] if l + 1 < LAYERS else []
        to_heads, to_tokens, d_to_heads, d_to_tokens = swap[l]
        source_ref, unit1, scale1, unit2, scale2, mid_ref, act_ref, slope_ref = saved[l]
        grad_two, d_small[l, 5:6, :], d_small[l, 7:8, :] = norm_backward(
            grad, unit2[...], scale2[...], small[l, 5:6, :]
        )
        low_two = grad_two.astype(BF16)
        d_small[l, 3:4, :] = column_sum(low_two.astype(F32))
        d_uppers = []
        for j in range(4):
            at = j * 512
            d_act = 0.0
            for i in range(2):
                weight = down[i].full[j // 2, (j % 2) * 2 : (j % 2) * 2 + 2].reshape(512, 256)
                d_act = d_act + nt(low_two[:, i * 256 : (i + 1) * 256], weight)
            d_upper = (d_act * slope_ref[:, at : at + 512]).astype(BF16)
            d_small_up[l, :, at : at + 512] = column_sum(d_upper.astype(F32))
            d_uppers.append(d_upper)
        d_upper = jnp.concatenate(d_uppers, axis=1)
        grad_mid = grad_two
        for i in range(2):
            grad_mid = grad_mid + nt(d_upper[:, i * 1024 : (i + 1) * 1024], up[i].value())
        grad_one, d_small[l, 4:5, :], d_small[l, 6:7, :] = norm_backward(
            grad_mid, unit1[...], scale1[...], small[l, 4:5, :]
        )
        low_one = grad_one.astype(BF16)
        d_small[l, 2:3, :] = column_sum(low_one.astype(F32))
        d_context = nt(low_one, proj.value()).astype(BF16)
        split_context(d_context, d_to_heads.out)
        d_to_heads.start()
        run(down + up + [proj], "sent")

        def down_grad(i):
            for j in range(8):
                block = tn(act_ref[:, j * 256 : (j + 1) * 256], low_two[:, i * 256 : (i + 1) * 256])
                down[i].store(j * 256, block)
            down[i].e0()

        def up_grad(i):
            for j in range(2):
                block = tn(mid_ref[:, j * 256 : (j + 1) * 256], d_upper[:, i * 1024 : (i + 1) * 1024])
                up[i].store(j * 256, block)
            up[i].e0()

        down_grad(0)
        up_grad(0)
        run(above[:3], "e1")
        if l == 0:
            down_grad(1)
            up_grad(1)
        context = join_context(to_tokens.into)
        for j in range(2):
            proj.store(j * 256, tn(context[:, j * 256 : (j + 1) * 256], low_one))
        proj.e0()
        run(above[3:], "e2")
        run(first_along(sums[l][3:], "x"), "e1")
        d_to_heads.wait()
        queries, keys, values = head_parts(to_heads.into[...])
        query_ref[...] = queries.reshape(NQ, QB, HD)
        dc_ref[...] = one_above_other(d_to_heads.into[...]).reshape(NQ, QB, HD)
        keys_t = keys.T

        def attend_back(i):
            d_ctx = dc_ref[i]
            d_prob = nt(values, d_ctx)
            prob = probs[l][i].astype(F32) * shares[l, i]
            row = jnp.sum(prob * d_prob, axis=0, keepdims=True)
            d_score = (prob * (d_prob - row)).astype(BF16)
            dq_ref[i] = (nn(keys_t, d_score) * 0.125).T.astype(BF16)
            return nn(prob.astype(BF16), d_ctx), nn(d_score, query_ref[i])

        terms = [attend_back(i) for i in range(NQ)]
        dv_ref[...] = sum(term[0] for term in terms)
        dk_ref[...] = sum(term[1] for term in terms)
        both = jnp.concatenate([dq_ref[...].reshape(LENGTH, HD), dk_ref[...].astype(BF16)], axis=1)
        d_to_tokens.out[:, 0:ROWS, :] = both.reshape(GROUP, ROWS, 2 * HD)
        d_to_tokens.out[:, ROWS:96, :] = side_by_side(dv_ref[...].astype(BF16).reshape(GROUP, ROWS, HD))
        d_to_tokens.start()
        if l > 0:
            down_grad(1)
            up_grad(1)
        run(above[:3], "e2")
        run(first_along(sums[l][3:], "yz"), "e1")
        run(qkv, "sent")
        run(first_along(above[3:], "x"), "e3")
        d_to_tokens.wait()
        d_joined = join_heads(d_to_tokens.into)
        d_small[l, 1:2, :] = column_sum(d_joined[:, 2 * D :].astype(F32))
        grad = grad_one
        source = source_ref[...]
        if l == 0:
            for i in range(3):
                qkv[i].store(0, tn(source, d_joined[:, i * D : (i + 1) * D]))
                qkv[i].e0()
        for i in range(3):
            grad = grad + nt(d_joined[:, i * D : (i + 1) * D], qkv[i].value())
        if l > 0:
            for i in range(3):
                qkv[i].store(0, tn(source, d_joined[:, i * D : (i + 1) * D]))
                qkv[i].e0()
    dx_ref[...] = grad
    dx_copy = pltpu.make_async_copy(dx_ref, dx_hbm, out_sems.at[1])
    dx_copy.start()
    qkv, rest, above = sums[0][:3], sums[0][3:], sums[1]
    run(qkv, "e1")

    small_grad[...] = jnp.zeros_like(small_grad)
    for l in range(LAYERS):
        for t in range(GROUP):
            small_grad[t, l * 8 + 1 : l * 8 + 8, 0:32] = d_small[l, 1:8, t * 32 : (t + 1) * 32]
            small_grad[t, l * 8 : l * 8 + 1, :] = d_small_up[l, :, t * 128 : (t + 1) * 128]
    for to in p.group():
        remote(small_grad.at[to], small_in.at[me], small_sems.at[2], small_sems.at[3], (p.rep, to))
    small_in[me] = small_grad[me]
    run(first_along(rest, "x"), "e2")
    run(first_along(above[3:], "yz") + above[:3], "e3")
    run(first_along(rest, "yz"), "e2")
    run(qkv, "e2")
    run(rest, "e3")
    wait_bytes(small_in.at[pl.ds(0, GROUP - 1)], small_sems.at[3])
    total = small_in[0]
    for t in range(1, GROUP):
        total = total + small_in[t]
    slot = small_rep.at[p.rep]
    slot[...] = total
    nrep = nx * nzl
    for d in range(1, nrep):
        remote(slot, slot, small_sems.at[4], small_sems.at[5], (lax.rem(p.rep + d, nrep), me))
    run(above, "e4")
    run(qkv, "e3")
    run(rest, "e4")
    if nrep > 1:
        wait_bytes(small_rep.at[pl.ds(0, nrep - 1)], small_sems.at[5])
    total = small_rep[0]
    for t in range(1, nrep):
        total = total + small_rep[t]
    for l in range(LAYERS):
        at = l * 8
        upb_out[l : l + 1, :] = total[at : at + 1, :]
        for i in range(3):
            bias_out[i, l : l + 1, :] = total[at + 1 + i : at + 2 + i, 0:32]
        gain_out[l] = total[at + 4 : at + 6, 0:32]
        shift_out[l] = total[at + 6 : at + 8, 0:32]
    run(qkv, "e4")

    run(sums[0] + sums[1], "reduced")
    for l in range(LAYERS):
        for one in swap[l]:
            one.finish()
    wait_bytes(small_all.at[pl.ds(0, GROUP - 1)], small_sems.at[0])
    wait_bytes(small_grad.at[pl.ds(0, GROUP - 1)], small_sems.at[2])
    if nrep > 1:
        wait_bytes(small_rep.at[pl.ds(0, nrep - 1)], small_sems.at[4])
    out_copy.wait()
    dx_copy.wait()


def scratch(nx, nzl, members):
    sizes = {"x": nx, "y": Y, "z": ZH * nzl}
    nrep = nx * nzl
    shapes = [pltpu.VMEM((TOK, D), BF16), pltpu.VMEM((TOK, D), F32)]
    shapes += [pltpu.VMEM(member.shape, F32) for member in members[:4]]
    for _ in range(LAYERS):
        for _, _, r, c, _, _ in PARTS:
            shapes.append(pltpu.VMEM((ZH, Y, CORES, r, c), BF16))
    for _, _, r, c, _, _ in PARTS[:3]:
        shapes.append(pltpu.VMEM((ZH, Y, CORES, r, c), BF16))
    for _ in range(LAYERS):
        for _, _, r, c, _, _ in PARTS:
            shapes.append(pltpu.VMEM((ZH, Y, r, c), BF16))
    for l in range(LAYERS):
        for which in bundles(nx, nzl):
            pieces = [piece_shape(PARTS[i][2], PARTS[i][3], nx, nzl) for i in which]
            piece = (pieces[0][0], sum(cols for _, cols in pieces))
            na, nb, nc = [sizes[axis] for axis in AXES[PARTS[which[0]][5][l]]]
            shapes.append(pltpu.VMEM((na, nb, nc) + piece, BF16))
            shapes.append(pltpu.VMEM((max(na - 1, 1), nb, nc) + piece, BF16))
            shapes.append(pltpu.VMEM((nb, nc) + piece, BF16))
            shapes.append(pltpu.VMEM((nb * nc - 1,) + piece, BF16))
            shapes.append(pltpu.VMEM((nrep,) + piece, BF16))
    for _ in range(LAYERS):
        for rows in (96, 32, 32, 96):
            shapes += [pltpu.VMEM((GROUP, rows, 128), BF16)] * 2
    shapes += [pltpu.VMEM((16, 128), F32)]
    shapes += [pltpu.VMEM((GROUP, 16, 128), F32)] * 3
    shapes += [pltpu.VMEM((nrep, 16, 128), F32)]
    shapes += [pltpu.VMEM((LAYERS, 8, D), F32), pltpu.VMEM((LAYERS, 1, FF), F32)] * 2
    for _ in range(LAYERS):
        shapes += [
            pltpu.VMEM((TOK, D), BF16),
            pltpu.VMEM((TOK, D), F32),
            pltpu.VMEM((TOK, 1), F32),
            pltpu.VMEM((TOK, D), F32),
            pltpu.VMEM((TOK, 1), F32),
            pltpu.VMEM((TOK, D), BF16),
            pltpu.VMEM((TOK, FF), BF16),
            pltpu.VMEM((TOK, FF), F32),
        ]
    shapes += [pltpu.VMEM((NQ, LENGTH, QB), BF16)] * LAYERS
    shapes += [pltpu.VMEM((LAYERS, NQ, 1, QB), F32)]
    shapes += [pltpu.VMEM((NQ, QB, HD), BF16)] * 3
    shapes += [pltpu.VMEM((LENGTH, HD), F32)] * 2
    shapes += [
        pltpu.SemaphoreType.DMA((LAYERS * len(PARTS), SEMS)),
        pltpu.SemaphoreType.DMA((LAYERS * 4, 2)),
        pltpu.SemaphoreType.DMA((6,)),
        pltpu.SemaphoreType.DMA((2,)),
    ]
    return shapes


def copy_kernel(*refs):
    n = 10
    source, target, held, sems = refs[:n], refs[n : 2 * n], refs[2 * n : 3 * n], refs[-1]
    into = [pltpu.make_async_copy(source[i], held[i], sems.at[0, i]) for i in range(n)]
    outof = [pltpu.make_async_copy(held[i], target[i], sems.at[1, i]) for i in range(n)]
    for copy in into:
        copy.start()
    for i in range(n):
        into[i].wait()
        outof[i].start()
    for copy in outof:
        copy.wait()


def local_call(nx, nzl, inputs, *arguments):
    cotangent, members = arguments[-1], list(arguments[:-1])
    members[4] = members[4].transpose(1, 0, 2)
    shapes = [jax.ShapeDtypeStruct((TOK, D), BF16), jax.ShapeDtypeStruct((TOK, D), F32)]
    shapes += [jax.ShapeDtypeStruct(member.shape, F32) for member in members]
    anywhere, vmem = pl.BlockSpec(memory_space=pl.ANY), pl.BlockSpec(memory_space=pltpu.VMEM)
    got = pl.pallas_call(
        functools.partial(kernel, nx, nzl),
        out_shape=shapes,
        in_specs=[vmem] * 10,
        out_specs=[anywhere] * 6 + [vmem] * 4,
        scratch_shapes=scratch(nx, nzl, members),
        compiler_params=pltpu.CompilerParams(
            collective_id=0, has_side_effects=True, vmem_limit_bytes=63 * 1024 * 1024
        ),
        cost_estimate=pl.CostEstimate(flops=7 * 10**9, bytes_accessed=8 * 10**6, transcendentals=5 * 10**6),
    )(inputs.reshape(TOK, D), cotangent.reshape(TOK, D), *members)
    got = pl.pallas_call(
        copy_kernel,
        out_shape=shapes,
        in_specs=[anywhere] * 10,
        out_specs=[anywhere] * 10,
        scratch_shapes=[pltpu.VMEM(shape.shape, shape.dtype) for shape in shapes] + [pltpu.SemaphoreType.DMA((2, 10))],
    )(*got)
    return (*got[:6], got[6].transpose(1, 0, 2), *got[7:])


def solution(mesh):
    nrep = mesh.shape["rep"]
    nzl = 2 if nrep >= 2 else 1
    nx = nrep // nzl

    def shards(inputs, *arguments):
        got = local_call(nx, nzl, inputs, *arguments)
        return (got[0].reshape(inputs.shape), got[1].reshape(inputs.shape), *got[2:])

    rows, columns = P(None, "shard", None), P(None, None, "shard")
    both = P("rep", "shard", None)
    weights = (rows, rows, rows, rows, columns, columns, columns, P(None, "shard"))
    return jax.shard_map(
        shards,
        mesh=mesh,
        in_specs=(both, *weights, both),
        out_specs=(both, both, *weights),
        check_vma=False,
    )
```
